32 devices in a mesh: parts: 2 (over y), patch: 4 (over z), sub: 2 (over x), lvl: 2 (over core).
Axes of the slice: x: 2, y: 2, z: 4, core: 2. Of those that a mesh axis runs over, the one named last changes fastest.
Arguments:
- node_states: float32 [8192, 512], P(('parts', 'patch', 'lvl')), parts along dimension 0, may hold values from -6 to 6
- coarse_states: float32 [1024, 512], P(('parts', 'patch', 'lvl')), parts along dimension 0, may hold values from -6 to 6
- children: int32 [512, 7], P(('patch', 'lvl')), may hold values from 0 to 511
- down_sources: int32 [4096, 3], P(('patch', 'lvl')), may hold values from 0 to 63
- bottom_links: int32 [4096, 6], P(('patch', 'lvl')), may hold values from 0 to 767, as said below
- coarse_links: int32 [512, 6], P(('patch', 'lvl')), may hold values from 0 to 511
- upward_sender: float32 [512, 512], P(None, 'sub'), may hold values from -0.25 to 0.25
- upward_receiver: float32 [512, 512], P(None, 'sub'), may hold values from -0.25 to 0.25
- upward_bias: float32 [512], P('sub'), may hold values from -4 to 4
- upward_output: float32 [512, 512], P('sub'), may hold values from -0.25 to 0.25
- upward_gain: float32 [512], replicated, may hold values from 0.1 to 1.9
- coarse_sender: float32 [512, 512], P(None, 'sub'), may hold values from -0.25 to 0.25
- coarse_receiver: float32 [512, 512], P(None, 'sub'), may hold values from -0.25 to 0.25
- coarse_bias: float32 [512], P('sub'), may hold values from -4 to 4
- coarse_output: float32 [512, 512], P('sub'), may hold values from -0.25 to 0.25
- coarse_gain: float32 [512], replicated, may hold values from 0.1 to 1.9
- downward_sender: float32 [512, 512], P(None, 'sub'), may hold values from -0.25 to 0.25
- downward_receiver: float32 [512, 512], P(None, 'sub'), may hold values from -0.25 to 0.25
- downward_bias: float32 [512], P('sub'), may hold values from -4 to 4
- downward_output: float32 [512, 512], P('sub'), may hold values from -0.25 to 0.25
- downward_gain: float32 [512], replicated, may hold values from 0.1 to 1.9
- bottom_sender: float32 [512, 512], P(None, 'sub'), may hold values from -0.25 to 0.25
- bottom_receiver: float32 [512, 512], P(None, 'sub'), may hold values from -0.25 to 0.25
- bottom_bias: float32 [512], P('sub'), may hold values from -4 to 4
- bottom_output: float32 [512, 512], P('sub'), may hold values from -0.25 to 0.25
- bottom_gain: float32 [512], replicated, may hold values from 0.1 to 1.9
Outputs:
- new_nodes: float32 [8192, 512], P(('parts', 'patch', 'lvl')), parts along dimension 0
- new_coarse: float32 [1024, 512], P(('parts', 'patch', 'lvl')), parts along dimension 0
The draws below stay inside these ranges and needn't reach their ends.
There are 2 independent parts, one for each index of `parts`. The reference program is written for one: setup_inputs(seed, part) draws one part's arguments, and reference() takes and returns one part's arrays. A program takes and returns all parts, laid end to end along the dimension named above; an argument that names none is the same for every part. Nothing has to cross between parts.
Inputs may be any that keep to these rules, and one draw needn't show every extreme that they name: bottom_links[n, k] - 128 differs from n's row within its block by at most 128.
All inputs are finite; a program needn't handle non-finite values.
Results may differ from the reference program's by a relative error of at most 0.00011.
Values sent between devices are 32-bit elements; how exact they have to be, the bound alone decides.
No kernel may reach another device: no remote copies, remote signals or barrier semaphores. Data moves between devices by JAX's collectives and lax.ppermute only.
A program may use at most 64 MiB of HBM per device.

```python
import jax
import jax.numpy as jnp
from jax import lax

LAT = 512
HID = 512
ROWS_DEV = 512
DEG = 6
CDEG = 6
UP = 7
DOWN = 3
HALO = 128
CDEV = 64
NB = 4096
NC = 512


def draw_children(key, part):
    factor = ROWS_DEV // CDEV
    position = jnp.arange(NC, dtype=jnp.int32) % CDEV
    offsets = jax.random.randint(key, (NC, UP), -4, 12, dtype=jnp.int32)
    result = jnp.clip(factor * position[:, None] + offsets, 0, ROWS_DEV - 1)
    result = result.at[0, 0].set(0).at[NC - 1, 0].set(ROWS_DEV - 1)
    return result.astype(jnp.int32)


def draw_down_sources(key, part):
    factor = ROWS_DEV // CDEV
    position = jnp.arange(NB, dtype=jnp.int32) % ROWS_DEV
    offsets = jax.random.randint(key, (NB, DOWN), -1, 2, dtype=jnp.int32)
    result = jnp.clip((position // factor)[:, None] + offsets, 0, CDEV - 1)
    result = result.at[0, 0].set(0).at[NB - 1, 0].set(CDEV - 1)
    return result.astype(jnp.int32)


def draw_bottom_links(key, part):
    position = jnp.arange(NB, dtype=jnp.int32) % ROWS_DEV
    offsets = jax.random.randint(key, (NB, DEG), -HALO, HALO + 1, dtype=jnp.int32)
    offsets = jnp.where(offsets == 0, 1, offsets)
    result = HALO + position[:, None] + offsets
    result = result.at[0, 0].set(0).at[NB - 1, 0].set(ROWS_DEV + 2 * HALO - 1)
    return result.astype(jnp.int32)


def draw_coarse_links(key, part):
    blocks = NC // CDEV
    first_key, second_key = jax.random.split(key)
    within = jax.random.randint(first_key, (NC, CDEG), 0, CDEV, dtype=jnp.int32)
    anywhere = jax.random.randint(second_key, (NC, CDEG), 0, blocks, dtype=jnp.int32)
    owning = (jnp.arange(NC, dtype=jnp.int32) // CDEV)[:, None]
    column = jnp.arange(CDEG, dtype=jnp.int32)[None, :]
    shifted = jnp.where(column == 0, owning, jnp.where(column == 1, owning + 1, jnp.where(column == 2, owning - 1 + blocks, owning + blocks // 2)))
    target = jnp.where(column < 4, shifted % blocks, anywhere)
    result = target * CDEV + within
    result = result.at[0, 0].set(0).at[NC - 1, 0].set(NC - 1)
    return result.astype(jnp.int32)


def block_levels(stream_key, extent, cuts, least, largest):
    loudness, own = 1.0, jax.random.fold_in(stream_key, 6)
    for dim, parts in cuts:
        heights = jnp.exp(jax.random.uniform(jax.random.fold_in(own, dim), (parts,), jnp.float32, least / len(cuts), largest / len(cuts)))
        loudness = loudness * jnp.repeat(heights, extent[dim] // parts).reshape([-1 if axis == dim else 1 for axis in range(len(extent))])
    return loudness


def normal_values(stream_key, extent, deviation, limit, shards=(), kind=jnp.bfloat16):
    factor_of = block_levels(stream_key, extent, shards, -0.22, 0.18) if shards else 1.0
    entries = jax.random.normal(stream_key, extent, jnp.float32) * deviation * factor_of
    return jnp.minimum(jnp.maximum(entries, -limit), limit).astype(kind)


def setup_inputs(seed: int = 0, part: int = 0) -> dict:
    streams_of = jax.random.split(jax.random.key(seed), 27)
    own_keys = jax.random.split(jax.random.fold_in(streams_of[26], part), 27)
    return {
        "node_states": normal_values(own_keys[0], (NB, LAT), 1.0, 6.0, ((0, 8),), jnp.float32),
        "coarse_states": normal_values(own_keys[1], (NC, LAT), 1.0, 6.0, ((0, 8),), jnp.float32),
        "children": draw_children(jax.random.fold_in(streams_of[26], 71), part),
        "down_sources": draw_down_sources(jax.random.fold_in(streams_of[26], 71), part),
        "bottom_links": draw_bottom_links(jax.random.fold_in(streams_of[26], 71), part),
        "coarse_links": draw_coarse_links(jax.random.fold_in(streams_of[26], 71), part),
        "upward_sender": normal_values(streams_of[6], (LAT, HID), LAT ** -0.5, 0.25, ((1, 2),), jnp.float32),
        "upward_receiver": normal_values(streams_of[7], (LAT, HID), LAT ** -0.5, 0.25, ((1, 2),), jnp.float32),
        "upward_bias": normal_values(streams_of[8], (HID,), 1.0, 4.0, ((0, 2),), jnp.float32),
        "upward_output": normal_values(streams_of[9], (HID, LAT), HID ** -0.5, 0.25, ((0, 2),), jnp.float32),
        "upward_gain": jnp.clip(1.0 + 0.18 * jax.random.normal(streams_of[10], (LAT,), jnp.float32), 0.1, 1.9),
        "coarse_sender": normal_values(streams_of[11], (LAT, HID), LAT ** -0.5, 0.25, ((1, 2),), jnp.float32),
        "coarse_receiver": normal_values(streams_of[12], (LAT, HID), LAT ** -0.5, 0.25, ((1, 2),), jnp.float32),
        "coarse_bias": normal_values(streams_of[13], (HID,), 1.0, 4.0, ((0, 2),), jnp.float32),
        "coarse_output": normal_values(streams_of[14], (HID, LAT), HID ** -0.5, 0.25, ((0, 2),), jnp.float32),
        "coarse_gain": jnp.clip(1.0 + 0.18 * jax.random.normal(streams_of[15], (LAT,), jnp.float32), 0.1, 1.9),
        "downward_sender": normal_values(streams_of[16], (LAT, HID), LAT ** -0.5, 0.25, ((1, 2),), jnp.float32),
        "downward_receiver": normal_values(streams_of[17], (LAT, HID), LAT ** -0.5, 0.25, ((1, 2),), jnp.float32),
        "downward_bias": normal_values(streams_of[18], (HID,), 1.0, 4.0, ((0, 2),), jnp.float32),
        "downward_output": normal_values(streams_of[19], (HID, LAT), HID ** -0.5, 0.25, ((0, 2),), jnp.float32),
        "downward_gain": jnp.clip(1.0 + 0.18 * jax.random.normal(streams_of[20], (LAT,), jnp.float32), 0.1, 1.9),
        "bottom_sender": normal_values(streams_of[21], (LAT, HID), LAT ** -0.5, 0.25, ((1, 2),), jnp.float32),
        "bottom_receiver": normal_values(streams_of[22], (LAT, HID), LAT ** -0.5, 0.25, ((1, 2),), jnp.float32),
        "bottom_bias": normal_values(streams_of[23], (HID,), 1.0, 4.0, ((0, 2),), jnp.float32),
        "bottom_output": normal_values(streams_of[24], (HID, LAT), HID ** -0.5, 0.25, ((0, 2),), jnp.float32),
        "bottom_gain": jnp.clip(1.0 + 0.18 * jax.random.normal(streams_of[25], (LAT,), jnp.float32), 0.1, 1.9),
    }


epsilon = 1e-05
highest = lax.Precision.HIGHEST

def project(states, weights):
    return jnp.dot(states, weights, precision=highest, preferred_element_type=jnp.float32)

def layer_norm(values):
    center = values - lax.optimization_barrier(jnp.mean(values, axis=-1, keepdims=True))
    spread = lax.optimization_barrier(jnp.mean(center * center, axis=-1, keepdims=True))
    return center * lax.rsqrt(spread + epsilon)

def interact(senders, receivers, link_index, sender_weights, receiver_weights, bias_vector, output_weights, gain_vector):
    sender_rows = project(senders, sender_weights)
    receiver_rows = project(receivers, receiver_weights) + bias_vector
    hidden = jnp.zeros_like(receiver_rows)
    for column in range(link_index.shape[1]):
        hidden = hidden + jax.nn.silu(sender_rows[link_index[:, column]] + receiver_rows)
    update = project(hidden, output_weights)
    return receivers + gain_vector * layer_norm(update)

def reference(node_states, coarse_states, children, down_sources, bottom_links, coarse_links, upward_sender, upward_receiver, upward_bias, upward_output, upward_gain, coarse_sender, coarse_receiver, coarse_bias, coarse_output, coarse_gain, downward_sender, downward_receiver, downward_bias, downward_output, downward_gain, bottom_sender, bottom_receiver, bottom_bias, bottom_output, bottom_gain):
    coarse_block = (jnp.arange(NC, dtype=jnp.int32) // CDEV)[:, None]
    child_index = (coarse_block * ROWS_DEV + children).astype(jnp.int32)
    node_block = (jnp.arange(NB, dtype=jnp.int32) // ROWS_DEV)[:, None]
    down_index = (node_block * CDEV + down_sources).astype(jnp.int32)
    mesh_index = ((node_block * ROWS_DEV + bottom_links - HALO) % NB).astype(jnp.int32)
    coarse_up = interact(node_states, coarse_states, child_index, upward_sender, upward_receiver, upward_bias, upward_output, upward_gain)
    new_coarse = interact(coarse_up, coarse_up, coarse_links, coarse_sender, coarse_receiver, coarse_bias, coarse_output, coarse_gain)
    nodes_down = interact(new_coarse, node_states, down_index, downward_sender, downward_receiver, downward_bias, downward_output, downward_gain)
    new_nodes = interact(nodes_down, nodes_down, mesh_index, bottom_sender, bottom_receiver, bottom_bias, bottom_output, bottom_gain)
    return (new_nodes, new_coarse)
```

```python
import functools

import jax
import jax.numpy as jnp
from jax import lax
from jax.experimental import pallas as pl
from jax.experimental.pallas import tpu as pltpu
from jax.sharding import PartitionSpec as P

epsilon = 1e-05
f32 = jnp.float32
bf16 = jnp.bfloat16
limit_bytes = 40 * 1024 * 1024
most_direct = 4


def split(values):
    high = values.astype(bf16)
    return high, (values - high.astype(f32)).astype(bf16)


def dot(a, b):
    return jnp.dot(a, b, preferred_element_type=f32)


def dot3(a, b_high, b_low):
    a_high, a_low = split(a)
    return dot(a_high, b_high) + (dot(a_high, b_low) + dot(a_low, b_high))


def normed(values):
    center = values - jnp.mean(values, axis=-1, keepdims=True)
    spread = jnp.mean(center * center, axis=-1, keepdims=True)
    return center * lax.rsqrt(spread + epsilon)


def one_hot(wanted, names):
    return jnp.concatenate(
        [
            jnp.where(wanted[:, k : k + 1] == names, 1.0, 0.0).astype(bf16)
            for k in range(wanted.shape[1])
        ],
        axis=0,
    )


def silu_sum(picked, halves, count):
    rows = halves.shape[0]
    total = None
    for k in range(count):
        u = picked[k * rows : (k + 1) * rows] + halves
        term = u + u * jnp.tanh(u)
        total = term if total is None else total + term
    return total


def added(refs):
    total = refs[0][...]
    for ref in refs[1:]:
        total = total + ref[...]
    return total


def upward_kernel(nodes, coarse, children, ws, wr, bias, wo, part):
    sender_high, sender_low = split(0.5 * dot3(nodes[...], *split(ws[...])))
    receivers = 0.5 * (dot3(coarse[...], *split(wr[...])) + bias[...])
    wanted = children[...]
    names = lax.broadcasted_iota(jnp.int32, (wanted.shape[0], nodes.shape[0]), 1)
    picks = one_hot(wanted, names)
    picked = dot(picks, sender_high) + dot(picks, sender_low)
    hidden = silu_sum(picked, receivers, wanted.shape[1])
    part[...] = dot3(hidden, *split(wo[...]))


def coarse_project_kernel(count, *refs):
    parts, (coarse, gain, ws, wr, bias, updated, senders, receivers) = refs[:count], refs[count:]
    rows = coarse[...] + gain[...] * normed(added(parts))
    updated[...] = rows
    senders[...] = 0.5 * dot3(rows, *split(ws[...]))
    receivers[...] = 0.5 * (dot3(rows, *split(wr[...])) + bias[...])


def coarse_kernel(count, *refs):
    pieces, (links, names, receivers, wo, part) = refs[:count], refs[count:]
    senders = jnp.concatenate([piece[...] for piece in pieces], axis=0)
    sender_high, sender_low = split(senders)
    wanted = links[...]
    picks = one_hot(wanted, jnp.broadcast_to(names[...], (wanted.shape[0], names.shape[1])))
    picked = dot(picks, sender_high) + dot(picks, sender_low)
    hidden = silu_sum(picked, receivers[...], wanted.shape[1])
    part[...] = dot3(hidden, *split(wo[...]))


def collect(own, packs, outs):
    ws, wr, bias, wo = own
    ws_high, ws_low, wr_high, wr_low, wo_high, wo_low, bias_all = outs
    subs, lvls = lax.axis_size("sub"), lax.axis_size("lvl")
    sub, lvl = lax.axis_index("sub"), lax.axis_index("lvl")
    depth, width = ws.shape
    ws_high[sub], ws_low[sub] = split(ws[...])
    wr_high[sub], wr_low[sub] = split(wr[...])
    rows = pl.ds(pl.multiple_of(sub * width, width), width)
    wo_high[rows, :], wo_low[rows, :] = split(wo[...])
    bias_all[sub] = jnp.broadcast_to(bias[...], (8, width))
    share, thin = depth // lvls, width // lvls
    for s in range(1, subs):
        block = lax.rem(sub + subs - s, subs)
        for t in range(lvls):
            pack = packs[(s - 1) * lvls + t]
            level = lax.rem(lvl + lvls - t, lvls)
            rows = pl.ds(pl.multiple_of(level * share, share), share)
            ws_high[block, rows, :], ws_low[block, rows, :] = split(pack[0:share, :])
            wr_high[block, rows, :], wr_low[block, rows, :] = split(pack[share : 2 * share, :])
            rows = pl.ds(pl.multiple_of(block * width + level * thin, thin), thin)
            for j in range(wo.shape[1] // width):
                high, low = split(pack[2 * share + j * thin : 2 * share + (j + 1) * thin, :])
                wo_high[rows, j * width : (j + 1) * width] = high
                wo_low[rows, j * width : (j + 1) * width] = low
            if t == 0:
                bias_all[block] = pack[pack.shape[0] - 8 :, :]


def down_ready_kernel(count, nodes, ws, wr, bias, wo, *refs):
    packs = refs[:count]
    receivers, ws_high, ws_low, wo_high, wo_low, wr_high, wr_low, bias_all = refs[count:]
    collect(
        (ws, wr, bias, wo), packs, (ws_high, ws_low, wr_high, wr_low, wo_high, wo_low, bias_all)
    )
    width = ws.shape[1]
    for g in range(ws_high.shape[0]):
        product = dot3(nodes[...], wr_high[g], wr_low[g])
        receivers[:, g * width : (g + 1) * width] = 0.5 * (product + bias_all[g][0:1])


def bottom_ready_kernel(count, ws, wr, bias, wo, *refs):
    collect((ws, wr, bias, wo), refs[:count], refs[count:])


def down_rows(nodes, receivers, sources, senders, wo_high, wo_low, gain):
    blocks = senders.shape[0] // 2
    column = lax.broadcasted_iota(jnp.int32, (nodes.shape[0], 2 * blocks), 1)
    names = jnp.where(column < blocks, column, column - blocks)
    picked = dot(one_hot(sources, names), senders)
    hidden = silu_sum(picked, receivers, sources.shape[1])
    return nodes + gain * normed(dot3(hidden, wo_high, wo_low))


def down_edge_kernel(count, rim, *refs):
    parts, refs = refs[:count], refs[count:]
    (coarse_up, coarse_gain, nodes, receivers, sources, ws_high, ws_low, wo_high, wo_low, gain) = refs[:10]
    new_coarse, senders, head, tail = refs[10:]
    rows = coarse_up[...] + coarse_gain[...] * normed(added(parts))
    new_coarse[...] = rows
    blocks = rows.shape[0]
    width = ws_high.shape[2]
    for g in range(ws_high.shape[0]):
        columns = slice(g * width, (g + 1) * width)
        high, low = split(0.5 * dot3(rows, ws_high[g], ws_low[g]))
        senders[0:blocks, columns] = high
        senders[blocks : 2 * blocks, columns] = low
    total = nodes.shape[0]
    for out, place in ((head, slice(0, rim)), (tail, slice(total - rim, total))):
        out[...] = down_rows(
            nodes[place], receivers[place], sources[place], senders[...], wo_high[...], wo_low[...], gain[...]
        )


def down_middle_kernel(rim, nodes, receivers, sources, senders, wo_high, wo_low, gain, middle):
    place = slice(rim, nodes.shape[0] - rim)
    middle[...] = down_rows(
        nodes[place], receivers[place], sources[place], senders[...], wo_high[...], wo_low[...], gain[...]
    )


def bottom_rows(nodes, receivers, links, start, sender_high, sender_low, wo_high, wo_low, gain):
    rows, reach = nodes.shape[0], sender_high.shape[0]
    names = start + lax.broadcasted_iota(jnp.int32, (rows, reach), 1)
    picks = one_hot(links, names)
    half = wo_high.shape[0] // 2
    hidden = []
    for place in (slice(0, half), slice(half, 2 * half)):
        picked = dot(picks, sender_high[:, place]) + dot(picks, sender_low[:, place])
        hidden.append(silu_sum(picked, receivers[:, place], links.shape[1]))
    return nodes + gain * normed(dot3(jnp.concatenate(hidden, axis=1), wo_high, wo_low))


def bottom_middle_kernel(rim, head, middle, tail, links, ws_high, ws_low, wr_high, wr_low, wo_high, wo_low, bias, gain, senders_high, senders_low, receivers, out):
    nodes = jnp.concatenate([head[...], middle[...], tail[...]], axis=0)
    nodes_high, nodes_low = split(nodes)
    width = ws_high.shape[2]
    for g in range(ws_high.shape[0]):
        columns = slice(g * width, (g + 1) * width)
        product = dot(nodes_high, ws_high[g]) + (dot(nodes_high, ws_low[g]) + dot(nodes_low, ws_high[g]))
        senders_high[:, columns], senders_low[:, columns] = split(0.5 * product)
        product = dot(nodes_high, wr_high[g]) + (dot(nodes_high, wr_low[g]) + dot(nodes_low, wr_high[g]))
        receivers[:, columns] = 0.5 * (product + bias[g][0:1])
    total = nodes.shape[0]
    for first in range(rim, total - rim, rim):
        place = slice(first, first + rim)
        reach = slice(first - rim, first + 2 * rim)
        out[first - rim : first, :] = bottom_rows(
            middle[first - rim : first], receivers[place], links[place], first,
            senders_high[reach], senders_low[reach], wo_high[...], wo_low[...], gain[...],
        )


def bottom_edge_kernel(rim, before, after, head, tail, inner, links, senders_high, senders_low, receivers, ws_high, ws_low, wo_high, wo_low, gain, out):
    total = links.shape[0]
    out[rim : total - rim, :] = inner[...]
    edges = ((before, head, slice(0, rim), slice(0, 2 * rim)), (after, tail, slice(total - rim, total), slice(total - 2 * rim, total)))
    outer = split(jnp.concatenate([before[...], after[...]], axis=0))
    projected = jnp.concatenate(
        [
            dot(outer[0], ws_high[g]) + (dot(outer[0], ws_low[g]) + dot(outer[1], ws_high[g]))
            for g in range(ws_high.shape[0])
        ],
        axis=1,
    )
    outer_high, outer_low = split(0.5 * projected)
    for side, (nodes, place, reach) in enumerate(
        ((head, slice(0, rim), slice(0, 2 * rim)), (tail, slice(total - rim, total), slice(total - 2 * rim, total)))
    ):
        strip = slice(side * rim, (side + 1) * rim)
        order = (lambda a, b: [a, b]) if side == 0 else (lambda a, b: [b, a])
        high = jnp.concatenate(order(outer_high[strip], senders_high[reach]), axis=0)
        low = jnp.concatenate(order(outer_low[strip], senders_low[reach]), axis=0)
        out[place, :] = bottom_rows(
            nodes[...], receivers[place], links[place], 0 if side == 0 else total - rim,
            high, low, wo_high[...], wo_low[...], gain[...],
        )


def call(kernel, outs, operands, flops, scratch=()):
    moved = sum(x.size * x.dtype.itemsize for x in (*outs, *operands))
    whole = pl.BlockSpec(memory_space=pltpu.VMEM)
    return pl.pallas_call(
        kernel,
        out_shape=tuple(outs),
        in_specs=[whole] * len(operands),
        out_specs=tuple([whole] * len(outs)),
        scratch_shapes=list(scratch),
        compiler_params=pltpu.CompilerParams(vmem_limit_bytes=limit_bytes),
        cost_estimate=pl.CostEstimate(flops=int(flops), bytes_accessed=moved, transcendentals=0),
    )(*operands)


def like(shape, kind=f32):
    return jax.ShapeDtypeStruct(tuple(shape), kind)


def shifted(values, axis, step):
    count = lax.axis_size(axis)
    return lax.ppermute(values, axis, [(i, (i + step) % count) for i in range(count)])


def sub_parts(part):
    if lax.axis_size("sub") == 2:
        return [part, shifted(part, "sub", 1)]
    return [lax.psum(part, "sub")]


def coarse_pieces(senders):
    patches, lvls = lax.axis_size("patch"), lax.axis_size("lvl")
    rows = senders.shape[0]
    if patches > most_direct:
        return (
            [lax.all_gather(senders, ("patch", "lvl"), axis=0, tiled=True)],
            jnp.arange(rows * patches * lvls, dtype=jnp.int32)[None],
        )
    pieces = [senders] + [shifted(senders, "patch", s) for s in range(1, patches)]
    everything = list(pieces)
    for t in range(1, lvls):
        everything += [shifted(piece, "lvl", t) for piece in pieces]
    place = jnp.arange(rows * patches * lvls, dtype=jnp.int32)
    step, away = (place // rows) % patches, place // (rows * patches)
    patch = (lax.axis_index("patch") - step) % patches
    lvl = (lax.axis_index("lvl") - away) % lvls
    return everything, ((patch * lvls + lvl) * rows + place % rows)[None].astype(jnp.int32)


def packed(ws, wr, bias, wo):
    lvls, lvl = lax.axis_size("lvl"), lax.axis_index("lvl")
    depth, width = ws.shape
    share, thin = depth // lvls, width // lvls
    strip = lax.dynamic_slice_in_dim(wo, lvl * thin, thin, axis=0)
    return jnp.concatenate(
        [
            lax.dynamic_slice_in_dim(ws, lvl * share, share, axis=0),
            lax.dynamic_slice_in_dim(wr, lvl * share, share, axis=0),
            *(strip[:, j * width : (j + 1) * width] for j in range(wo.shape[1] // width)),
            jnp.broadcast_to(bias[None], (8, width)),
        ],
        axis=0,
    )


def fetched(pack):
    packs = []
    for s in range(1, lax.axis_size("sub")):
        share = shifted(pack, "sub", s)
        packs += [share] + [shifted(share, "lvl", t) for t in range(1, lax.axis_size("lvl"))]
    return packs


def body(
    node_states,
    coarse_states,
    children,
    down_sources,
    bottom_links,
    coarse_links,
    upward_sender,
    upward_receiver,
    upward_bias,
    upward_output,
    upward_gain,
    coarse_sender,
    coarse_receiver,
    coarse_bias,
    coarse_output,
    coarse_gain,
    downward_sender,
    downward_receiver,
    downward_bias,
    downward_output,
    downward_gain,
    bottom_sender,
    bottom_receiver,
    bottom_bias,
    bottom_output,
    bottom_gain,
):
    rows, latent = node_states.shape
    blocks = coarse_states.shape[0]
    width = upward_sender.shape[1]
    subs = lax.axis_size("sub")
    hidden = width * subs
    rim = rows // 4
    weights = [like((subs, latent, width), bf16)] * 2
    outputs = [like((hidden, latent), bf16)] * 2
    biases = like((subs, 8, width))

    down_packs = fetched(packed(downward_sender, downward_receiver, downward_bias, downward_output))
    bottom_packs = fetched(packed(bottom_sender, bottom_receiver, bottom_bias, bottom_output))

    (part,) = call(
        upward_kernel,
        [like((blocks, latent))],
        [node_states, coarse_states, children, upward_sender, upward_receiver, upward_bias[None], upward_output],
        6 * rows * latent * width + 4 * children.size * rows * width,
    )
    parts = sub_parts(part)
    coarse_up, senders, receivers = call(
        functools.partial(coarse_project_kernel, len(parts)),
        [like((blocks, latent)), like((blocks, width)), like((blocks, width))],
        [*parts, coarse_states, upward_gain[None], coarse_sender, coarse_receiver, coarse_bias[None]],
        12 * blocks * latent * width,
    )
    pieces, names = coarse_pieces(senders)
    (part,) = call(
        functools.partial(coarse_kernel, len(pieces)),
        [like((blocks, latent))],
        [*pieces, coarse_links, names, receivers, coarse_output],
        4 * coarse_links.size * names.size * width,
    )
    parts = sub_parts(part)

    receivers, ws_high, ws_low, wo_high, wo_low = call(
        functools.partial(down_ready_kernel, len(down_packs)),
        [like((rows, hidden)), *weights, *outputs],
        [node_states, downward_sender, downward_receiver, downward_bias[None], downward_output, *down_packs],
        6 * rows * latent * hidden,
        [pltpu.VMEM((subs, latent, width), bf16)] * 2 + [pltpu.VMEM((subs, 8, width), f32)],
    )
    new_coarse, senders, head, tail = call(
        functools.partial(down_edge_kernel, len(parts), rim),
        [like((blocks, latent)), like((2 * blocks, hidden), bf16), like((rim, latent)), like((rim, latent))],
        [*parts, coarse_up, coarse_gain[None], node_states, receivers, down_sources, ws_high, ws_low, wo_high, wo_low, downward_gain[None]],
        6 * 2 * rim * latent * hidden,
    )
    ring = ("patch", "lvl")
    before, after = shifted(tail, ring, 1), shifted(head, ring, -1)
    (middle,) = call(
        functools.partial(down_middle_kernel, rim),
        [like((rows - 2 * rim, latent))],
        [node_states, receivers, down_sources, senders, wo_high, wo_low, downward_gain[None]],
        6 * (rows - 2 * rim) * latent * hidden,
    )

    ws_high, ws_low, wr_high, wr_low, wo_high, wo_low, bias = call(
        functools.partial(bottom_ready_kernel, len(bottom_packs)),
        [*weights, *weights, *outputs, biases],
        [bottom_sender, bottom_receiver, bottom_bias[None], bottom_output, *bottom_packs],
        latent * hidden,
    )
    senders_high, senders_low, receivers, inner = call(
        functools.partial(bottom_middle_kernel, rim),
        [like((rows, hidden), bf16), like((rows, hidden), bf16), like((rows, hidden)), like((rows - 2 * rim, latent))],
        [head, middle, tail, bottom_links, ws_high, ws_low, wr_high, wr_low, wo_high, wo_low, bias, bottom_gain[None]],
        (12 * rows + 12 * rows) * latent * hidden,
    )
    (new_nodes,) = call(
        functools.partial(bottom_edge_kernel, rim),
        [like((rows, latent))],
        [before, after, head, tail, inner, bottom_links, senders_high, senders_low, receivers, ws_high, ws_low, wo_high, wo_low, bottom_gain[None]],
        24 * rim * latent * hidden,
    )
    return (new_nodes, new_coarse)


def solution(mesh):
    split_rows, level_rows = P(("parts", "patch", "lvl"), None), P(("patch", "lvl"), None)
    weights = (P(None, "sub"), P(None, "sub"), P("sub"), P("sub", None), P())
    in_specs = (split_rows, split_rows, *([level_rows] * 4), *(weights * 4))
    out_specs = (split_rows, split_rows)
    return jax.shard_map(body, mesh=mesh, in_specs=in_specs, out_specs=out_specs, check_vma=False)
```

```python
import functools

import jax
import jax.numpy as jnp
from jax import lax
from jax.experimental import pallas as pl
from jax.experimental.pallas import tpu as pltpu
from jax.sharding import PartitionSpec as P

epsilon = 1e-05
f32 = jnp.float32
bf16 = jnp.bfloat16
limit_bytes = 40 * 1024 * 1024
large_limit = 60 * 1024 * 1024
most_direct = 4


def split(values):
    high = values.astype(bf16)
    return high, (values - high.astype(f32)).astype(bf16)


def dot(a, b):
    return jnp.dot(a, b, preferred_element_type=f32)


def dot3(a, b_high, b_low):
    a_high, a_low = split(a)
    return dot(a_high, b_high) + (dot(a_high, b_low) + dot(a_low, b_high))


def normed(values):
    center = values - jnp.mean(values, axis=-1, keepdims=True)
    spread = jnp.mean(center * center, axis=-1, keepdims=True)
    return center * lax.rsqrt(spread + epsilon)


def one_hot(wanted, names):
    return jnp.concatenate(
        [
            jnp.where(wanted[:, k : k + 1] == names, 1.0, 0.0).astype(bf16)
            for k in range(wanted.shape[1])
        ],
        axis=0,
    )


def silu_sum(picked, halves, count):
    rows = halves.shape[0]
    total = None
    for k in range(count):
        u = picked[k * rows : (k + 1) * rows] + halves
        term = u + u * jnp.tanh(u)
        total = term if total is None else total + term
    return total


def added(refs):
    total = refs[0][...]
    for ref in refs[1:]:
        total = total + ref[...]
    return total


def started(copies, sems):
    moves = [pltpu.make_async_copy(a, b, sems.at[i]) for i, (a, b) in enumerate(copies)]
    for move in moves:
        move.start()
    return moves


def strips(source, target, count):
    rows = source.shape[0] // count
    return [
        (source.at[pl.ds(i * rows, rows)], target.at[pl.ds(i * rows, rows)]) for i in range(count)
    ]


def upward_kernel(nodes_hbm, coarse, children, ws_hbm, wr_hbm, bias, wo_hbm, part, nodes, ws, wr, wo, sems):
    moves = started(
        strips(ws_hbm, ws, 2)
        + strips(nodes_hbm, nodes, 4)
        + strips(wr_hbm, wr, 2)
        + strips(wo_hbm, wo, 2),
        sems,
    )
    wanted = children[...]
    names = lax.broadcasted_iota(jnp.int32, (wanted.shape[0], nodes.shape[0]), 1)
    picks = one_hot(wanted, names)
    for move in moves[:6]:
        move.wait()
    sender_high, sender_low = split(0.5 * dot3(nodes[...], *split(ws[...])))
    for move in moves[6:8]:
        move.wait()
    receivers = 0.5 * (dot3(coarse[...], *split(wr[...])) + bias[...])
    picked = dot(picks, sender_high) + dot(picks, sender_low)
    hidden = silu_sum(picked, receivers, wanted.shape[1])
    for move in moves[8:]:
        move.wait()
    part[...] = dot3(hidden, *split(wo[...]))


def coarse_ready_kernel(after, ws, wr, wo, ws_high, ws_low, wr_high, wr_low, wo_high, wo_low):
    del after
    ws_high[...], ws_low[...] = split(ws[...])
    wr_high[...], wr_low[...] = split(wr[...])
    wo_high[...], wo_low[...] = split(wo[...])


def share_copies(ws, wr, bias, wo, pack):
    parts, lvls = lax.axis_size("parts"), lax.axis_size("lvl")
    mine = lax.axis_index("parts") * lvls + lax.axis_index("lvl")
    depth, width = ws.shape
    share, thin = depth // (parts * lvls), width // (parts * lvls)
    rows = pl.ds(pl.multiple_of(mine * share, share), share)
    strip = pl.ds(pl.multiple_of(mine * thin, thin), thin)
    columns = range(wo.shape[1] // width)
    return [
        (ws.at[rows], pack.at[pl.ds(0, share)]),
        (wr.at[rows], pack.at[pl.ds(share, share)]),
        *(
            (wo.at[strip, pl.ds(j * width, width)], pack.at[pl.ds(2 * share + j * thin, thin)])
            for j in columns
        ),
        (bias, pack.at[pl.ds(2 * share + len(columns) * thin, 1)]),
    ]


def share_kernel(*refs):
    own, (down_pack, bottom_pack, sems) = refs[:8], refs[8:]
    for move in started(share_copies(*own[:4], down_pack) + share_copies(*own[4:], bottom_pack), sems):
        move.wait()


def picks_kernel(after, links, names, picks):
    del after
    wanted = links[...]
    picks[...] = one_hot(wanted, jnp.broadcast_to(names[...], (wanted.shape[0], names.shape[1])))


def coarse_project_kernel(count, *refs):
    parts, refs = refs[:count], refs[count:]
    coarse, gain, ws_high, ws_low, wr_high, wr_low, bias, updated, senders, receivers = refs
    rows = coarse[...] + gain[...] * normed(added(parts))
    updated[...] = rows
    senders[...] = 0.5 * dot3(rows, ws_high[...], ws_low[...])
    receivers[...] = 0.5 * (dot3(rows, wr_high[...], wr_low[...]) + bias[...])


def coarse_kernel(count, *refs):
    pieces, (all_picks, receivers, wo_high, wo_low, part) = refs[:count], refs[count:]
    senders = jnp.concatenate([piece[...] for piece in pieces], axis=0)
    sender_high, sender_low = split(senders)
    picks = all_picks[...]
    picked = dot(picks, sender_high) + dot(picks, sender_low)
    hidden = silu_sum(picked, receivers[...], picks.shape[0] // receivers.shape[0])
    part[...] = dot3(hidden, wo_high[...], wo_low[...])


def collect(own, packs, outs):
    ws, wr, bias, wo = own
    ws_high, ws_low, wr_high, wr_low, wo_high, wo_low, bias_all = outs
    subs, parts, lvls = lax.axis_size("sub"), lax.axis_size("parts"), lax.axis_size("lvl")
    sub, part, lvl = lax.axis_index("sub"), lax.axis_index("parts"), lax.axis_index("lvl")
    depth, width = ws.shape
    ws_high[sub], ws_low[sub] = split(ws[...])
    wr_high[sub], wr_low[sub] = split(wr[...])
    rows = pl.ds(pl.multiple_of(sub * width, width), width)
    wo_high[rows, :], wo_low[rows, :] = split(wo[...])
    bias_all[sub] = jnp.broadcast_to(bias[...], (8, width))
    share, thin = depth // (parts * lvls), width // (parts * lvls)
    columns = wo.shape[1] // width
    place = iter(packs)
    for s in range(1, subs):
        block = lax.rem(sub + subs - s, subs)
        for p in range(parts):
            for t in range(lvls):
                pack = next(place)
                mine = lax.rem(part + parts - p, parts) * lvls + lax.rem(lvl + lvls - t, lvls)
                rows = pl.ds(pl.multiple_of(mine * share, share), share)
                ws_high[block, rows, :], ws_low[block, rows, :] = split(pack[0:share, :])
                wr_high[block, rows, :], wr_low[block, rows, :] = split(pack[share : 2 * share, :])
                rows = pl.ds(pl.multiple_of(block * width + mine * thin, thin), thin)
                for j in range(columns):
                    high, low = split(pack[2 * share + j * thin : 2 * share + (j + 1) * thin, :])
                    wo_high[rows, j * width : (j + 1) * width] = high
                    wo_low[rows, j * width : (j + 1) * width] = low
                if p == 0 and t == 0:
                    last = 2 * share + columns * thin
                    bias_all[block] = jnp.broadcast_to(pack[last : last + 1, :], (8, width))


def down_ready_kernel(count, after, nodes, ws, wr, bias, wo, *refs):
    del after
    packs = refs[:count]
    receivers, ws_high, ws_low, wo_high, wo_low, wr_high, wr_low, bias_all = refs[count:]
    collect(
        (ws, wr, bias, wo), packs, (ws_high, ws_low, wr_high, wr_low, wo_high, wo_low, bias_all)
    )
    width = ws.shape[1]
    for g in range(ws_high.shape[0]):
        product = dot3(nodes[...], wr_high[g], wr_low[g])
        receivers[:, g * width : (g + 1) * width] = 0.5 * (product + bias_all[g][0:1])


def bottom_ready_kernel(count, ws, wr, bias, wo, *refs):
    collect((ws, wr, bias, wo), refs[:count], refs[count:])


def down_rows(nodes, receivers, sources, senders, wo_high, wo_low, gain):
    blocks = senders.shape[0] // 2
    column = lax.broadcasted_iota(jnp.int32, (nodes.shape[0], 2 * blocks), 1)
    names = jnp.where(column < blocks, column, column - blocks)
    picked = dot(one_hot(sources, names), senders)
    hidden = silu_sum(picked, receivers, sources.shape[1])
    return nodes + gain * normed(dot3(hidden, wo_high, wo_low))


def down_edge_kernel(count, rim, *refs):
    parts, refs = refs[:count], refs[count:]
    (coarse_up, coarse_gain, nodes, receivers, sources, ws_high, ws_low, wo_high, wo_low, gain) = refs[:10]
    new_coarse, senders, head, tail = refs[10:]
    rows = coarse_up[...] + coarse_gain[...] * normed(added(parts))
    new_coarse[...] = rows
    blocks = rows.shape[0]
    width = ws_high.shape[2]
    for g in range(ws_high.shape[0]):
        columns = slice(g * width, (g + 1) * width)
        high, low = split(0.5 * dot3(rows, ws_high[g], ws_low[g]))
        senders[0:blocks, columns] = high
        senders[blocks : 2 * blocks, columns] = low
    total = nodes.shape[0]
    for out, place in ((head, slice(0, rim)), (tail, slice(total - rim, total))):
        out[...] = down_rows(
            nodes[place], receivers[place], sources[place], senders[...], wo_high[...], wo_low[...], gain[...]
        )


def down_middle_kernel(rim, nodes, receivers, sources, senders, wo_high, wo_low, gain, middle):
    place = slice(rim, nodes.shape[0] - rim)
    middle[...] = down_rows(
        nodes[place], receivers[place], sources[place], senders[...], wo_high[...], wo_low[...], gain[...]
    )


def bottom_rows(nodes, receivers, links, start, sender_high, sender_low, wo_high, wo_low, gain):
    rows, reach = nodes.shape[0], sender_high.shape[0]
    names = start + lax.broadcasted_iota(jnp.int32, (rows, reach), 1)
    picks = one_hot(links, names)
    half = wo_high.shape[0] // 2
    hidden = []
    for place in (slice(0, half), slice(half, 2 * half)):
        picked = dot(picks, sender_high[:, place]) + dot(picks, sender_low[:, place])
        hidden.append(silu_sum(picked, receivers[:, place], links.shape[1]))
    return nodes + gain * normed(dot3(jnp.concatenate(hidden, axis=1), wo_high, wo_low))


def bottom_middle_kernel(rim, head, middle, tail, links, ws_high, ws_low, wr_high, wr_low, wo_high, wo_low, bias, gain, senders_high, senders_low, receivers, out):
    nodes = jnp.concatenate([head[...], middle[...], tail[...]], axis=0)
    nodes_high, nodes_low = split(nodes)
    width = ws_high.shape[2]
    for g in range(ws_high.shape[0]):
        columns = slice(g * width, (g + 1) * width)
        product = dot(nodes_high, ws_high[g]) + (dot(nodes_high, ws_low[g]) + dot(nodes_low, ws_high[g]))
        senders_high[:, columns], senders_low[:, columns] = split(0.5 * product)
        product = dot(nodes_high, wr_high[g]) + (dot(nodes_high, wr_low[g]) + dot(nodes_low, wr_high[g]))
        receivers[:, columns] = 0.5 * (product + bias[g][0:1])
    total = nodes.shape[0]
    for first in range(rim, total - rim, rim):
        place = slice(first, first + rim)
        reach = slice(first - rim, first + 2 * rim)
        out[first - rim : first, :] = bottom_rows(
            middle[first - rim : first], receivers[place], links[place], first,
            senders_high[reach], senders_low[reach], wo_high[...], wo_low[...], gain[...],
        )


def bottom_edge_kernel(rim, before, after, head, tail, inner, links, senders_high, senders_low, receivers, ws_high, ws_low, wo_high, wo_low, gain, out):
    total = links.shape[0]
    out[rim : total - rim, :] = inner[...]
    edges = ((before, head, slice(0, rim), slice(0, 2 * rim)), (after, tail, slice(total - rim, total), slice(total - 2 * rim, total)))
    outer = split(jnp.concatenate([before[...], after[...]], axis=0))
    projected = jnp.concatenate(
        [
            dot(outer[0], ws_high[g]) + (dot(outer[0], ws_low[g]) + dot(outer[1], ws_high[g]))
            for g in range(ws_high.shape[0])
        ],
        axis=1,
    )
    outer_high, outer_low = split(0.5 * projected)
    for side, (nodes, place, reach) in enumerate(
        ((head, slice(0, rim), slice(0, 2 * rim)), (tail, slice(total - rim, total), slice(total - 2 * rim, total)))
    ):
        strip = slice(side * rim, (side + 1) * rim)
        order = (lambda a, b: [a, b]) if side == 0 else (lambda a, b: [b, a])
        high = jnp.concatenate(order(outer_high[strip], senders_high[reach]), axis=0)
        low = jnp.concatenate(order(outer_low[strip], senders_low[reach]), axis=0)
        out[place, :] = bottom_rows(
            nodes[...], receivers[place], links[place], 0 if side == 0 else total - rim,
            high, low, wo_high[...], wo_low[...], gain[...],
        )


whole = pl.BlockSpec(memory_space=pltpu.VMEM)
away = pl.BlockSpec(memory_space=pl.ANY)


def call(kernel, outs, operands, flops, scratch=(), far=(), far_outs=(), limit=limit_bytes):
    moved = sum(x.size * x.dtype.itemsize for x in (*outs, *operands))
    return pl.pallas_call(
        kernel,
        out_shape=tuple(outs),
        in_specs=[away if i in far else whole for i in range(len(operands))],
        out_specs=tuple(away if i in far_outs else whole for i in range(len(outs))),
        scratch_shapes=list(scratch),
        compiler_params=pltpu.CompilerParams(vmem_limit_bytes=limit),
        cost_estimate=pl.CostEstimate(flops=int(flops), bytes_accessed=moved, transcendentals=0),
    )(*operands)


def like(shape, kind=f32):
    return jax.ShapeDtypeStruct(tuple(shape), kind)


def shifted(values, axis, step):
    count = lax.axis_size(axis)
    return lax.ppermute(values, axis, [(i, (i + step) % count) for i in range(count)])


def sub_parts(part):
    if lax.axis_size("sub") == 2:
        return [part, shifted(part, "sub", 1)]
    return [lax.psum(part, "sub")]


def coarse_pieces(senders):
    patches, lvls = lax.axis_size("patch"), lax.axis_size("lvl")
    if patches > most_direct:
        return [lax.all_gather(senders, ("patch", "lvl"), axis=0, tiled=True)]
    pieces = [senders] + [shifted(senders, "patch", s) for s in range(1, patches)]
    everything = list(pieces)
    for t in range(1, lvls):
        everything += [shifted(piece, "lvl", t) for piece in pieces]
    return everything


def coarse_names(rows):
    patches, lvls = lax.axis_size("patch"), lax.axis_size("lvl")
    place = jnp.arange(rows * patches * lvls, dtype=jnp.int32)
    if patches > most_direct:
        return place[None]
    step, away = (place // rows) % patches, place // (rows * patches)
    patch = (lax.axis_index("patch") - step) % patches
    lvl = (lax.axis_index("lvl") - away) % lvls
    return ((patch * lvls + lvl) * rows + place % rows)[None].astype(jnp.int32)


def held(values, event):
    return lax.optimization_barrier((values, event))[0]


def over_sub(pack):
    return [shifted(pack, "sub", s) for s in range(1, lax.axis_size("sub"))]


def over_parts(shares):
    return [
        [shifted(share, "parts", p) for p in range(1, lax.axis_size("parts"))] for share in shares
    ]


def over_lvl(shares):
    return [
        [share] + [shifted(share, "lvl", t) for t in range(1, lax.axis_size("lvl"))]
        for share in shares
    ]


def all_shares(shares, others):
    near = over_lvl(shares)
    far = [over_lvl(row) for row in others]
    return [x for first, row in zip(near, far) for x in (first + [y for group in row for y in group])]


def body(
    node_states,
    coarse_states,
    children,
    down_sources,
    bottom_links,
    coarse_links,
    upward_sender,
    upward_receiver,
    upward_bias,
    upward_output,
    upward_gain,
    coarse_sender,
    coarse_receiver,
    coarse_bias,
    coarse_output,
    coarse_gain,
    downward_sender,
    downward_receiver,
    downward_bias,
    downward_output,
    downward_gain,
    bottom_sender,
    bottom_receiver,
    bottom_bias,
    bottom_output,
    bottom_gain,
):
    rows, latent = node_states.shape
    blocks = coarse_states.shape[0]
    width = upward_sender.shape[1]
    subs = lax.axis_size("sub")
    hidden = width * subs
    rim = rows // 4
    weights = [like((subs, latent, width), bf16)] * 2
    outputs = [like((hidden, latent), bf16)] * 2
    biases = like((subs, 8, width))

    shares = lax.axis_size("parts") * lax.axis_size("lvl")
    columns = latent // width
    pack = like((2 * latent // shares + (width // shares) * columns + 8, width))
    down_own = (downward_sender, downward_receiver, downward_bias[None], downward_output)
    bottom_own = (bottom_sender, bottom_receiver, bottom_bias[None], bottom_output)

    down_pack, bottom_pack = call(
        share_kernel,
        [pack, pack],
        [*down_own, *bottom_own],
        latent,
        [pltpu.SemaphoreType.DMA((2 * (3 + columns),))],
        far=range(8),
        far_outs=(0, 1),
        limit=large_limit,
    )
    down_near = over_sub(down_pack)
    (part,) = call(
        upward_kernel,
        [like((blocks, latent))],
        [node_states, coarse_states, children, upward_sender, upward_receiver, upward_bias[None], upward_output],
        6 * rows * latent * width + 4 * children.size * rows * width,
        [
            pltpu.VMEM((rows, latent), f32),
            pltpu.VMEM((latent, width), f32),
            pltpu.VMEM((latent, width), f32),
            pltpu.VMEM((width, latent), f32),
            pltpu.SemaphoreType.DMA((10,)),
        ],
        far=(0, 3, 4, 6),
        limit=large_limit,
    )
    parts = sub_parts(part)
    ws_high, ws_low, wr_high, wr_low, wo_high, wo_low = call(
        coarse_ready_kernel,
        [like((latent, width), bf16)] * 4 + [like((width, latent), bf16)] * 2,
        [part, coarse_sender, coarse_receiver, coarse_output],
        latent * hidden,
        far=(0,),
    )
    coarse_up, senders, receivers = call(
        functools.partial(coarse_project_kernel, len(parts)),
        [like((blocks, latent)), like((blocks, width)), like((blocks, width))],
        [*parts, coarse_states, upward_gain[None], ws_high, ws_low, wr_high, wr_low, coarse_bias[None]],
        12 * blocks * latent * width,
    )
    pieces = coarse_pieces(senders)
    names = coarse_names(blocks)
    (picks,) = call(
        picks_kernel,
        [like((coarse_links.size, names.size), bf16)],
        [senders, coarse_links, names],
        coarse_links.size * names.size,
        far=(0,),
    )
    down_near, bottom_pack = held((down_near, bottom_pack), picks)
    down_far = over_parts(down_near)
    bottom_near = over_sub(bottom_pack)
    down_packs = all_shares(down_near, down_far)
    (part,) = call(
        functools.partial(coarse_kernel, len(pieces)),
        [like((blocks, latent))],
        [*pieces, picks, receivers, wo_high, wo_low],
        4 * coarse_links.size * names.size * width,
    )
    parts = sub_parts(part)

    receivers, ws_high, ws_low, wo_high, wo_low = call(
        functools.partial(down_ready_kernel, len(down_packs)),
        [like((rows, hidden)), *weights, *outputs],
        [part, node_states, *down_own, *down_packs],
        6 * rows * latent * hidden,
        [pltpu.VMEM((subs, latent, width), bf16)] * 2 + [pltpu.VMEM((subs, 8, width), f32)],
        far=(0,),
    )
    bottom_near = held(bottom_near, receivers)
    bottom_far = over_parts(bottom_near)
    new_coarse, senders, head, tail = call(
        functools.partial(down_edge_kernel, len(parts), rim),
        [like((blocks, latent)), like((2 * blocks, hidden), bf16), like((rim, latent)), like((rim, latent))],
        [*parts, coarse_up, coarse_gain[None], node_states, receivers, down_sources, ws_high, ws_low, wo_high, wo_low, downward_gain[None]],
        6 * 2 * rim * latent * hidden,
    )
    ring = ("patch", "lvl")
    before, after = shifted(tail, ring, 1), shifted(head, ring, -1)
    (middle,) = call(
        functools.partial(down_middle_kernel, rim),
        [like((rows - 2 * rim, latent))],
        [node_states, receivers, down_sources, senders, wo_high, wo_low, downward_gain[None]],
        6 * (rows - 2 * rim) * latent * hidden,
    )

    bottom_near, bottom_far = held((bottom_near, bottom_far), head)
    bottom_packs = all_shares(bottom_near, bottom_far)
    ws_high, ws_low, wr_high, wr_low, wo_high, wo_low, bias = call(
        functools.partial(bottom_ready_kernel, len(bottom_packs)),
        [*weights, *weights, *outputs, biases],
        [*bottom_own, *bottom_packs],
        latent * hidden,
    )
    senders_high, senders_low, receivers, inner = call(
        functools.partial(bottom_middle_kernel, rim),
        [like((rows, hidden), bf16), like((rows, hidden), bf16), like((rows, hidden)), like((rows - 2 * rim, latent))],
        [head, middle, tail, bottom_links, ws_high, ws_low, wr_high, wr_low, wo_high, wo_low, bias, bottom_gain[None]],
        (12 * rows + 12 * rows) * latent * hidden,
    )
    (new_nodes,) = call(
        functools.partial(bottom_edge_kernel, rim),
        [like((rows, latent))],
        [before, after, head, tail, inner, bottom_links, senders_high, senders_low, receivers, ws_high, ws_low, wo_high, wo_low, bottom_gain[None]],
        24 * rim * latent * hidden,
    )
    return (new_nodes, new_coarse)


def solution(mesh):
    split_rows, level_rows = P(("parts", "patch", "lvl"), None), P(("patch", "lvl"), None)
    weights = (P(None, "sub"), P(None, "sub"), P("sub"), P("sub", None), P())
    in_specs = (split_rows, split_rows, *([level_rows] * 4), *(weights * 4))
    out_specs = (split_rows, split_rows)
    return jax.shard_map(body, mesh=mesh, in_specs=in_specs, out_specs=out_specs, check_vma=False)
```

```python
import functools

import jax
import jax.numpy as jnp
from jax import lax
from jax.experimental import pallas as pl
from jax.experimental.pallas import tpu as pltpu
from jax.sharding import PartitionSpec as P

epsilon = 1e-05
f32 = jnp.float32
bf16 = jnp.bfloat16
limit_bytes = 16 * 1024 * 1024
wide_limit = 50 * 1024 * 1024
large_limit = 60 * 1024 * 1024
most_direct = 4


def split(values):
    high = values.astype(bf16)
    return high, (values - high.astype(f32)).astype(bf16)


def dot(a, b):
    return jnp.dot(a, b, preferred_element_type=f32)


def dot3(a, b_high, b_low):
    a_high, a_low = split(a)
    return dot(a_high, b_high) + (dot(a_high, b_low) + dot(a_low, b_high))


def normed(values):
    center = values - jnp.mean(values, axis=-1, keepdims=True)
    spread = jnp.mean(center * center, axis=-1, keepdims=True)
    return center * lax.rsqrt(spread + epsilon)


def upright(rows):
    count, size = rows.shape
    tall, wide = -count % 8, -size % 128
    if tall:
        rows = jnp.concatenate([rows, jnp.zeros((tall, size), rows.dtype)], axis=0)
    if wide:
        rows = jnp.concatenate([rows, jnp.zeros((count + tall, wide), rows.dtype)], axis=1)
    return jnp.transpose(rows)[:size, :count]


def one_hot(wanted, names):
    return jnp.concatenate(
        [
            jnp.where(wanted[:, k : k + 1] == names, 1.0, 0.0).astype(bf16)
            for k in range(wanted.shape[1])
        ],
        axis=0,
    )


def silu_sum(picked, halves, count):
    rows = halves.shape[0]
    total = None
    for k in range(count):
        u = picked[k * rows : (k + 1) * rows] + halves
        term = u + u * jnp.tanh(u)
        total = term if total is None else total + term
    return total


def added(refs):
    total = refs[0][...]
    for ref in refs[1:]:
        total = total + ref[...]
    return total


def started(copies, sems):
    moves = [pltpu.make_async_copy(a, b, sems.at[i]) for i, (a, b) in enumerate(copies)]
    for move in moves:
        move.start()
    return moves


def upward_kernel(nodes, coarse, children, ws, wr, bias, wo, part):
    wanted = upright(children[...])
    names = lax.broadcasted_iota(jnp.int32, (wanted.shape[0], nodes.shape[0]), 1)
    picks = one_hot(wanted, names)
    sender_high, sender_low = split(0.5 * dot3(nodes[...], *split(ws[...])))
    receivers = 0.5 * (dot3(coarse[...], *split(wr[...])) + bias[...])
    picked = dot(picks, sender_high) + dot(picks, sender_low)
    hidden = silu_sum(picked, receivers, wanted.shape[1])
    part[...] = dot3(hidden, *split(wo[...]))


def coarse_ready_kernel(after, ws, wr, wo, *refs):
    del after
    params, (ws_high, ws_low, wr_high, wr_low, wo_high, wo_low, gains, biases) = refs[:7], refs[7:]
    for i in range(4):
        gains[i : i + 1] = params[i][...]
    for i in range(3):
        biases[i : i + 1] = params[4 + i][...]
    ws_high[...], ws_low[...] = split(ws[...])
    wr_high[...], wr_low[...] = split(wr[...])
    wo_high[...], wo_low[...] = split(wo[...])


def share_copies(ws, wr, bias, wo, pack):
    parts, lvls = lax.axis_size("parts"), lax.axis_size("lvl")
    mine = lax.axis_index("parts") * lvls + lax.axis_index("lvl")
    depth, width = ws.shape
    share, thin = depth // (parts * lvls), width // (parts * lvls)
    rows = pl.ds(pl.multiple_of(mine * share, share), share)
    strip = pl.ds(pl.multiple_of(mine * thin, thin), thin)
    columns = range(wo.shape[1] // width)
    return [
        (ws.at[rows], pack.at[pl.ds(0, share)]),
        (wr.at[rows], pack.at[pl.ds(share, share)]),
        *(
            (wo.at[strip, pl.ds(j * width, width)], pack.at[pl.ds(2 * share + j * thin, thin)])
            for j in columns
        ),
        (bias, pack.at[pl.ds(2 * share + len(columns) * thin, 1)]),
    ]


def share_kernel(*refs):
    own, (down_pack, bottom_pack, sems) = refs[:8], refs[8:]
    for move in started(share_copies(*own[:4], down_pack) + share_copies(*own[4:], bottom_pack), sems):
        move.wait()


def picks_kernel(after, links, names, picks):
    del after
    wanted = upright(links[...])
    picks[...] = one_hot(wanted, jnp.broadcast_to(names[...], (wanted.shape[0], names.shape[1])))


def coarse_project_kernel(count, *refs):
    parts, refs = refs[:count], refs[count:]
    coarse, gains, biases, ws_high, ws_low, wr_high, wr_low, updated, senders, receivers = refs
    rows = coarse[...] + gains[0:1] * normed(added(parts))
    updated[...] = rows
    senders[...] = 0.5 * dot3(rows, ws_high[...], ws_low[...])
    receivers[...] = 0.5 * (dot3(rows, wr_high[...], wr_low[...]) + biases[0:1])


def coarse_kernel(count, *refs):
    pieces, (all_picks, receivers, wo_high, wo_low) = refs[:count], refs[count : count + 4]
    part = refs[-1]
    senders = jnp.concatenate([piece[...] for piece in pieces], axis=0)
    sender_high, sender_low = split(senders)
    picks = all_picks[...]
    picked = dot(picks, sender_high) + dot(picks, sender_low)
    hidden = silu_sum(picked, receivers[...], picks.shape[0] // receivers.shape[0])
    part[...] = dot3(hidden, wo_high[...], wo_low[...])


def collect(own, packs, outs):
    ws, wr, bias, wo = own
    ws_high, ws_low, wr_high, wr_low, wo_high, wo_low, bias_all = outs
    subs, parts, lvls = lax.axis_size("sub"), lax.axis_size("parts"), lax.axis_size("lvl")
    sub, part, lvl = lax.axis_index("sub"), lax.axis_index("parts"), lax.axis_index("lvl")
    depth, width = ws.shape
    ws_high[sub], ws_low[sub] = split(ws[...])
    wr_high[sub], wr_low[sub] = split(wr[...])
    rows = pl.ds(pl.multiple_of(sub * width, width), width)
    wo_high[rows, :], wo_low[rows, :] = split(wo[...])
    bias_all[sub] = jnp.broadcast_to(bias, (8, width))
    share, thin = depth // (parts * lvls), width // (parts * lvls)
    columns = wo.shape[1] // width
    place = iter(packs)
    for s in range(1, subs):
        block = lax.rem(sub + subs - s, subs)
        for p in range(parts):
            for t in range(lvls):
                pack = next(place)
                mine = lax.rem(part + parts - p, parts) * lvls + lax.rem(lvl + lvls - t, lvls)
                rows = pl.ds(pl.multiple_of(mine * share, share), share)
                ws_high[block, rows, :], ws_low[block, rows, :] = split(pack[0:share, :])
                wr_high[block, rows, :], wr_low[block, rows, :] = split(pack[share : 2 * share, :])
                rows = pl.ds(pl.multiple_of(block * width + mine * thin, thin), thin)
                for j in range(columns):
                    high, low = split(pack[2 * share + j * thin : 2 * share + (j + 1) * thin, :])
                    wo_high[rows, j * width : (j + 1) * width] = high
                    wo_low[rows, j * width : (j + 1) * width] = low
                if p == 0 and t == 0:
                    last = 2 * share + columns * thin
                    bias_all[block] = jnp.broadcast_to(pack[last : last + 1, :], (8, width))


def down_ready_kernel(count, nodes, ws, wr, biases, wo, *refs):
    packs = refs[:count]
    receivers, ws_high, ws_low, wo_high, wo_low, wr_high, wr_low, bias_all = refs[count:]
    collect(
        (ws, wr, biases[1:2], wo), packs, (ws_high, ws_low, wr_high, wr_low, wo_high, wo_low, bias_all)
    )
    width = ws.shape[1]
    for g in range(ws_high.shape[0]):
        product = dot3(nodes[...], wr_high[g], wr_low[g])
        receivers[:, g * width : (g + 1) * width] = 0.5 * (product + bias_all[g][0:1])


def bottom_ready_kernel(count, ws, wr, biases, wo, *refs):
    collect((ws, wr, biases[2:3], wo), refs[:count], refs[count:])


def down_rows(nodes, receivers, sources, senders, wo_high, wo_low, gain):
    blocks = senders.shape[0] // 2
    column = lax.broadcasted_iota(jnp.int32, (nodes.shape[0], 2 * blocks), 1)
    names = jnp.where(column < blocks, column, column - blocks)
    picked = dot(one_hot(sources, names), senders)
    hidden = silu_sum(picked, receivers, sources.shape[1])
    return nodes + gain * normed(dot3(hidden, wo_high, wo_low))


def down_edge_kernel(count, rim, *refs):
    parts, refs = refs[:count], refs[count:]
    (coarse_up, gains, nodes, receivers, sources, ws_high, ws_low, wo_high, wo_low) = refs[:9]
    new_coarse, senders, head, tail = refs[9:]
    rows = coarse_up[...] + gains[1:2] * normed(added(parts))
    new_coarse[...] = rows
    blocks = rows.shape[0]
    width = ws_high.shape[2]
    for g in range(ws_high.shape[0]):
        columns = slice(g * width, (g + 1) * width)
        high, low = split(0.5 * dot3(rows, ws_high[g], ws_low[g]))
        senders[0:blocks, columns] = high
        senders[blocks : 2 * blocks, columns] = low
    total = nodes.shape[0]
    wanted = upright(sources[...])
    for out, place in ((head, slice(0, rim)), (tail, slice(total - rim, total))):
        out[...] = down_rows(
            nodes[place], receivers[place], wanted[place], senders[...], wo_high[...], wo_low[...], gains[2:3]
        )


def down_middle_kernel(rim, nodes, receivers, sources, senders, wo_high, wo_low, gains, middle):
    place = slice(rim, nodes.shape[0] - rim)
    middle[...] = down_rows(
        nodes[place], receivers[place], upright(sources[...])[place], senders[...], wo_high[...], wo_low[...], gains[2:3]
    )


def bottom_rows(nodes, receivers, links, start, sender_high, sender_low, wo_high, wo_low, gain):
    rows, reach = nodes.shape[0], sender_high.shape[0]
    names = start + lax.broadcasted_iota(jnp.int32, (rows, reach), 1)
    picks = one_hot(links, names)
    half = wo_high.shape[0] // 2
    hidden = []
    for place in (slice(0, half), slice(half, 2 * half)):
        picked = dot(picks, sender_high[:, place]) + dot(picks, sender_low[:, place])
        hidden.append(silu_sum(picked, receivers[:, place], links.shape[1]))
    return nodes + gain * normed(dot3(jnp.concatenate(hidden, axis=1), wo_high, wo_low))


def bottom_middle_kernel(rim, head, middle, tail, links, ws_high, ws_low, wr_high, wr_low, wo_high, wo_low, bias, gains, senders_high, senders_low, receivers, out):
    nodes = jnp.concatenate([head[...], middle[...], tail[...]], axis=0)
    nodes_high, nodes_low = split(nodes)
    width = ws_high.shape[2]
    for g in range(ws_high.shape[0]):
        columns = slice(g * width, (g + 1) * width)
        product = dot(nodes_high, ws_high[g]) + (dot(nodes_high, ws_low[g]) + dot(nodes_low, ws_high[g]))
        senders_high[:, columns], senders_low[:, columns] = split(0.5 * product)
        product = dot(nodes_high, wr_high[g]) + (dot(nodes_high, wr_low[g]) + dot(nodes_low, wr_high[g]))
        receivers[:, columns] = 0.5 * (product + bias[g][0:1])
    total = nodes.shape[0]
    wanted = upright(links[...])
    for first in range(rim, total - rim, rim):
        place = slice(first, first + rim)
        reach = slice(first - rim, first + 2 * rim)
        out[first - rim : first, :] = bottom_rows(
            middle[first - rim : first], receivers[place], wanted[place], first,
            senders_high[reach], senders_low[reach], wo_high[...], wo_low[...], gains[3:4],
        )


def bottom_edge_kernel(rim, before, after, head, tail, inner, links, senders_high, senders_low, receivers, ws_high, ws_low, wo_high, wo_low, gains, out):
    total = links.shape[1]
    wanted = upright(links[...])
    out[rim : total - rim, :] = inner[...]
    outer = split(jnp.concatenate([before[...], after[...]], axis=0))
    projected = jnp.concatenate(
        [
            dot(outer[0], ws_high[g]) + (dot(outer[0], ws_low[g]) + dot(outer[1], ws_high[g]))
            for g in range(ws_high.shape[0])
        ],
        axis=1,
    )
    outer_high, outer_low = split(0.5 * projected)
    for side, (nodes, place, reach) in enumerate(
        ((head, slice(0, rim), slice(0, 2 * rim)), (tail, slice(total - rim, total), slice(total - 2 * rim, total)))
    ):
        strip = slice(side * rim, (side + 1) * rim)
        order = (lambda a, b: [a, b]) if side == 0 else (lambda a, b: [b, a])
        high = jnp.concatenate(order(outer_high[strip], senders_high[reach]), axis=0)
        low = jnp.concatenate(order(outer_low[strip], senders_low[reach]), axis=0)
        out[place, :] = bottom_rows(
            nodes[...], receivers[place], wanted[place], 0 if side == 0 else total - rim,
            high, low, wo_high[...], wo_low[...], gains[3:4],
        )


whole = pl.BlockSpec(memory_space=pltpu.VMEM)
away = pl.BlockSpec(memory_space=pl.ANY)


def call(kernel, outs, operands, flops, scratch=(), far=(), far_outs=(), limit=limit_bytes):
    moved = sum(x.size * x.dtype.itemsize for x in (*outs, *operands))
    return pl.pallas_call(
        kernel,
        out_shape=tuple(outs),
        in_specs=[away if i in far else whole for i in range(len(operands))],
        out_specs=tuple(away if i in far_outs else whole for i in range(len(outs))),
        scratch_shapes=list(scratch),
        compiler_params=pltpu.CompilerParams(vmem_limit_bytes=limit),
        cost_estimate=pl.CostEstimate(flops=int(flops), bytes_accessed=moved, transcendentals=0),
    )(*operands)


def like(shape, kind=f32):
    return jax.ShapeDtypeStruct(tuple(shape), kind)


def shifted(values, axis, step):
    count = lax.axis_size(axis)
    return lax.ppermute(values, axis, [(i, (i + step) % count) for i in range(count)])


def sub_parts(part):
    if lax.axis_size("sub") == 2:
        return [part, shifted(part, "sub", 1)]
    return [lax.psum(part, "sub")]


def coarse_pieces(senders):
    patches, lvls = lax.axis_size("patch"), lax.axis_size("lvl")
    if patches > most_direct:
        return [lax.all_gather(senders, ("patch", "lvl"), axis=0, tiled=True)]
    near = [[senders] + [shifted(senders, "lvl", t) for t in range(1, lvls)]]
    pieces = lax.optimization_barrier([shifted(senders, "patch", s) for s in range(1, patches)])
    near += [[piece] + [shifted(piece, "lvl", t) for t in range(1, lvls)] for piece in pieces]
    return [row[t] for t in range(lvls) for row in near]


def coarse_names(rows):
    patches, lvls = lax.axis_size("patch"), lax.axis_size("lvl")
    place = jnp.arange(rows * patches * lvls, dtype=jnp.int32)
    if patches > most_direct:
        return place[None]
    step, away = (place // rows) % patches, place // (rows * patches)
    patch = (lax.axis_index("patch") - step) % patches
    lvl = (lax.axis_index("lvl") - away) % lvls
    return ((patch * lvls + lvl) * rows + place % rows)[None].astype(jnp.int32)


def held(values, event):
    return lax.optimization_barrier((values, event))[0]


def over_sub(pack):
    return [shifted(pack, "sub", s) for s in range(1, lax.axis_size("sub"))]


def over_parts(shares):
    return [
        [shifted(share, "parts", p) for p in range(1, lax.axis_size("parts"))] for share in shares
    ]


def over_lvl(shares):
    return [
        [share] + [shifted(share, "lvl", t) for t in range(1, lax.axis_size("lvl"))]
        for share in shares
    ]


def all_shares(shares, others):
    near = over_lvl(shares)
    far = [over_lvl(row) for row in others]
    return [x for first, row in zip(near, far) for x in (first + [y for group in row for y in group])]


def body(
    node_states,
    coarse_states,
    children,
    down_sources,
    bottom_links,
    coarse_links,
    upward_sender,
    upward_receiver,
    upward_bias,
    upward_output,
    upward_gain,
    coarse_sender,
    coarse_receiver,
    coarse_bias,
    coarse_output,
    coarse_gain,
    downward_sender,
    downward_receiver,
    downward_bias,
    downward_output,
    downward_gain,
    bottom_sender,
    bottom_receiver,
    bottom_bias,
    bottom_output,
    bottom_gain,
):
    rows, latent = node_states.shape
    blocks = coarse_states.shape[0]
    width = upward_sender.shape[1]
    subs = lax.axis_size("sub")
    hidden = width * subs
    rim = rows // 4
    weights = [like((subs, latent, width), bf16)] * 2
    outputs = [like((hidden, latent), bf16)] * 2
    bias_rows = like((subs, 8, width))

    shares = lax.axis_size("parts") * lax.axis_size("lvl")
    columns = latent // width
    pack = like((2 * latent // shares + (width // shares) * columns + 8, width))
    down_own = (downward_sender, downward_receiver, downward_bias[None], downward_output)
    bottom_own = (bottom_sender, bottom_receiver, bottom_bias[None], bottom_output)

    down_pack, bottom_pack = call(
        share_kernel,
        [pack, pack],
        [*down_own, *bottom_own],
        latent,
        [pltpu.SemaphoreType.DMA((2 * (3 + columns),))],
        far=range(8),
        limit=large_limit,
    )
    down_near = over_sub(down_pack)
    (part,) = call(
        upward_kernel,
        [like((blocks, latent))],
        [node_states, coarse_states, children.T, upward_sender, upward_receiver, upward_bias[None], upward_output],
        6 * rows * latent * width + 4 * children.size * rows * width,
        limit=wide_limit,
    )
    parts = sub_parts(part)
    ws_high, ws_low, wr_high, wr_low, wo_high, wo_low, gains, biases = call(
        coarse_ready_kernel,
        [like((latent, width), bf16)] * 4 + [like((width, latent), bf16)] * 2 + [like((4, latent)), like((3, width))],
        [
            part, coarse_sender, coarse_receiver, coarse_output,
            upward_gain[None], coarse_gain[None], downward_gain[None], bottom_gain[None],
            coarse_bias[None], downward_bias[None], bottom_bias[None],
        ],
        latent * hidden,
        far=(0,),
    )
    coarse_up, senders, receivers = call(
        functools.partial(coarse_project_kernel, len(parts)),
        [like((blocks, latent)), like((blocks, width)), like((blocks, width))],
        [*parts, coarse_states, gains, biases, ws_high, ws_low, wr_high, wr_low],
        12 * blocks * latent * width,
    )
    pieces = coarse_pieces(senders)
    names = coarse_names(blocks)
    (picks,) = call(
        picks_kernel,
        [like((coarse_links.size, names.size), bf16)],
        [senders, coarse_links.T, names],
        coarse_links.size * names.size,
        far=(0,),
    )
    down_near, bottom_pack = held((down_near, bottom_pack), pieces[len(pieces) // 2])
    down_far = over_parts(down_near)
    bottom_near = over_sub(bottom_pack)
    down_near, down_far, bottom_near = held(
        (down_near, down_far, bottom_near), pieces[min(1, len(pieces) - 1)]
    )
    down_packs = all_shares(down_near, down_far)
    down_receivers, ws_high, ws_low, down_high, down_low = call(
        functools.partial(down_ready_kernel, len(down_packs)),
        [like((rows, hidden)), *weights, *outputs],
        [node_states, downward_sender, downward_receiver, biases, downward_output, *down_packs],
        6 * rows * latent * hidden,
        [pltpu.VMEM((subs, latent, width), bf16)] * 2 + [pltpu.VMEM((subs, 8, width), f32)],
    )
    (part,) = call(
        functools.partial(coarse_kernel, len(pieces)),
        [like((blocks, latent))],
        [*pieces, picks, receivers, wo_high, wo_low, down_receivers],
        4 * coarse_links.size * names.size * width,
        far=(len(pieces) + 4,),
    )
    parts = sub_parts(part)
    receivers, wo_high, wo_low = down_receivers, down_high, down_low

    bottom_near = held(bottom_near, part)
    bottom_far = over_parts(bottom_near)
    new_coarse, senders, head, tail = call(
        functools.partial(down_edge_kernel, len(parts), rim),
        [like((blocks, latent)), like((2 * blocks, hidden), bf16), like((rim, latent)), like((rim, latent))],
        [*parts, coarse_up, gains, node_states, receivers, down_sources.T, ws_high, ws_low, wo_high, wo_low],
        6 * 2 * rim * latent * hidden,
    )
    ring = ("patch", "lvl")
    before, after = shifted(tail, ring, 1), shifted(head, ring, -1)
    (middle,) = call(
        functools.partial(down_middle_kernel, rim),
        [like((rows - 2 * rim, latent))],
        [node_states, receivers, down_sources.T, senders, wo_high, wo_low, gains],
        6 * (rows - 2 * rim) * latent * hidden,
    )

    bottom_near, bottom_far = held((bottom_near, bottom_far), head)
    bottom_packs = all_shares(bottom_near, bottom_far)
    ws_high, ws_low, wr_high, wr_low, wo_high, wo_low, bias = call(
        functools.partial(bottom_ready_kernel, len(bottom_packs)),
        [*weights, *weights, *outputs, bias_rows],
        [bottom_sender, bottom_receiver, biases, bottom_output, *bottom_packs],
        latent * hidden,
    )
    senders_high, senders_low, receivers, inner = call(
        functools.partial(bottom_middle_kernel, rim),
        [like((rows, hidden), bf16), like((rows, hidden), bf16), like((rows, hidden)), like((rows - 2 * rim, latent))],
        [head, middle, tail, bottom_links.T, ws_high, ws_low, wr_high, wr_low, wo_high, wo_low, bias, gains],
        (12 * rows + 12 * rows) * latent * hidden,
    )
    (new_nodes,) = call(
        functools.partial(bottom_edge_kernel, rim),
        [like((rows, latent))],
        [before, after, head, tail, inner, bottom_links.T, senders_high, senders_low, receivers, ws_high, ws_low, wo_high, wo_low, gains],
        24 * rim * latent * hidden,
    )
    return (new_nodes, new_coarse)


def solution(mesh):
    split_rows, level_rows = P(("parts", "patch", "lvl"), None), P(("patch", "lvl"), None)
    weights = (P(None, "sub"), P(None, "sub"), P("sub"), P("sub", None), P())
    in_specs = (split_rows, split_rows, *([level_rows] * 4), *(weights * 4))
    out_specs = (split_rows, split_rows)
    return jax.shard_map(body, mesh=mesh, in_specs=in_specs, out_specs=out_specs, check_vma=False)
```

```python
import functools

import jax
import jax.numpy as jnp
from jax import lax
from jax.experimental import pallas as pl
from jax.experimental.pallas import tpu as pltpu
from jax.sharding import PartitionSpec as P

epsilon = 1e-05
f32 = jnp.float32
bf16 = jnp.bfloat16
limit_bytes = 16 * 1024 * 1024
wide_limit = 50 * 1024 * 1024
large_limit = 60 * 1024 * 1024
most_direct = 4


def split(values):
    high = values.astype(bf16)
    return high, (values - high.astype(f32)).astype(bf16)


def dot(a, b):
    return jnp.dot(a, b, preferred_element_type=f32)


def dot3(a, b_high, b_low):
    a_high, a_low = split(a)
    return dot(a_high, b_high) + (dot(a_high, b_low) + dot(a_low, b_high))


def normed(values):
    center = values - jnp.mean(values, axis=-1, keepdims=True)
    spread = jnp.mean(center * center, axis=-1, keepdims=True)
    return center * lax.rsqrt(spread + epsilon)


def upright(rows):
    count, size = rows.shape
    tall, wide = -count % 8, -size % 128
    if tall:
        rows = jnp.concatenate([rows, jnp.zeros((tall, size), rows.dtype)], axis=0)
    if wide:
        rows = jnp.concatenate([rows, jnp.zeros((count + tall, wide), rows.dtype)], axis=1)
    return jnp.transpose(rows)[:size, :count]


def one_hot(wanted, names):
    return jnp.concatenate(
        [
            jnp.where(wanted[:, k : k + 1] == names, 1.0, 0.0).astype(bf16)
            for k in range(wanted.shape[1])
        ],
        axis=0,
    )


def silu_sum(picked, halves, count):
    rows = halves.shape[0]
    total = None
    for k in range(count):
        u = picked[k * rows : (k + 1) * rows] + halves
        term = u + u * jnp.tanh(u)
        total = term if total is None else total + term
    return total


def added(refs):
    total = refs[0][...]
    for ref in refs[1:]:
        total = total + ref[...]
    return total


def started(copies, sems):
    moves = [pltpu.make_async_copy(a, b, sems.at[i]) for i, (a, b) in enumerate(copies)]
    for move in moves:
        move.start()
    return moves


def upward_kernel(nodes, coarse, children, ws, wr, bias, wo, part):
    wanted = upright(children[...])
    names = lax.broadcasted_iota(jnp.int32, (wanted.shape[0], nodes.shape[0]), 1)
    picks = one_hot(wanted, names)
    sender_high, sender_low = split(0.5 * dot3(nodes[...], *split(ws[...])))
    receivers = 0.5 * (dot3(coarse[...], *split(wr[...])) + bias[...])
    picked = dot(picks, sender_high) + dot(picks, sender_low)
    hidden = silu_sum(picked, receivers, wanted.shape[1])
    part[...] = dot3(hidden, *split(wo[...]))


def coarse_ready_kernel(parts, after, ws, wr, wo, *refs):
    del after
    params, own, refs = refs[:7], refs[7:11], refs[11:]
    ws_high, ws_low, wr_high, wr_low, wo_high, wo_low, gains, biases, pack, sems = refs
    moves = started(share_copies(own, pack, parts), sems)
    for i in range(4):
        gains[i : i + 1] = params[i][...]
    for i in range(3):
        biases[i : i + 1] = params[4 + i][...]
    ws_high[...], ws_low[...] = split(ws[...])
    wr_high[...], wr_low[...] = split(wr[...])
    wo_high[...], wo_low[...] = split(wo[...])
    for move in moves:
        move.wait()


def shares(parts):
    lvls = lax.axis_size("lvl")
    mine = lax.axis_index("lvl")
    if parts > 1:
        mine = lax.axis_index("parts") * lvls + mine
    return mine, parts * lvls


def share_copies(sources, pack, parts):
    mine, count = shares(parts)
    width = pack.shape[1]
    copies, at = [], 0
    for source in sources:
        rows = source.shape[0] // count
        if source.shape[0] == 1:
            copies.append((source, pack.at[pl.ds(at, 1)]))
            at += 8
            continue
        strip = pl.ds(pl.multiple_of(mine * rows, rows), rows)
        for j in range(source.shape[1] // width):
            copies.append((source.at[strip, pl.ds(j * width, width)], pack.at[pl.ds(at, rows)]))
            at += rows
    return copies


def share_kernel(parts, *refs):
    for move in started(share_copies(refs[:-2], refs[-2], parts), refs[-1]):
        move.wait()


def picks_kernel(after, links, names, picks):
    del after
    wanted = upright(links[...])
    picks[...] = one_hot(wanted, jnp.broadcast_to(names[...], (wanted.shape[0], names.shape[1])))


def coarse_project_kernel(count, *refs):
    parts, refs = refs[:count], refs[count:]
    coarse, gains, biases, ws_high, ws_low, wr_high, wr_low, updated, senders, receivers = refs
    rows = coarse[...] + gains[0:1] * normed(added(parts))
    updated[...] = rows
    senders[...] = 0.5 * dot3(rows, ws_high[...], ws_low[...])
    receivers[...] = 0.5 * (dot3(rows, wr_high[...], wr_low[...]) + biases[0:1])


def coarse_kernel(count, *refs):
    pieces, (all_picks, receivers, wo_high, wo_low) = refs[:count], refs[count : count + 4]
    part = refs[-1]
    senders = jnp.concatenate([piece[...] for piece in pieces], axis=0)
    sender_high, sender_low = split(senders)
    picks = all_picks[...]
    picked = dot(picks, sender_high) + dot(picks, sender_low)
    hidden = silu_sum(picked, receivers[...], picks.shape[0] // receivers.shape[0])
    part[...] = dot3(hidden, wo_high[...], wo_low[...])


def shared_among(packs):
    return max(1, len(packs) // max(1, lax.axis_size("sub") - 1))


def fetched_shares(packs):
    subs, lvls = lax.axis_size("sub"), lax.axis_size("lvl")
    parts = len(packs) // max(1, (subs - 1) * lvls)
    sub, part, lvl = lax.axis_index("sub"), lax.axis_index("parts"), lax.axis_index("lvl")
    place = iter(packs)
    for s in range(1, subs):
        for p in range(parts):
            for t in range(lvls):
                mine = lax.rem(part + parts - p, parts) * lvls + lax.rem(lvl + lvls - t, lvls)
                yield next(place), lax.rem(sub + subs - s, subs), mine, p == 0 and t == 0


def collect_in(own, packs, at, high, low):
    sub = lax.axis_index("sub")
    count = shared_among(packs)
    high[sub], low[sub] = split(own[...])
    share = own.shape[0] // count
    for pack, block, mine, _ in fetched_shares(packs):
        rows = pl.ds(pl.multiple_of(mine * share, share), share)
        high[block, rows, :], low[block, rows, :] = split(pack[at : at + share, :])


def collect_out(own, packs, at, high, low):
    sub = lax.axis_index("sub")
    count = shared_among(packs)
    width, latent = own.shape
    rows = pl.ds(pl.multiple_of(sub * width, width), width)
    high[rows, :], low[rows, :] = split(own[...])
    thin = width // count
    for pack, block, mine, _ in fetched_shares(packs):
        rows = pl.ds(pl.multiple_of(block * width + mine * thin, thin), thin)
        for j in range(latent // width):
            first, second = split(pack[at + j * thin : at + (j + 1) * thin, :])
            high[rows, j * width : (j + 1) * width] = first
            low[rows, j * width : (j + 1) * width] = second


def collect_bias(own, packs, at, out):
    out[lax.axis_index("sub")] = jnp.broadcast_to(own, (8, own.shape[1]))
    for pack, block, _, whole_row in fetched_shares(packs):
        if whole_row:
            out[block] = jnp.broadcast_to(pack[at : at + 1, :], (8, own.shape[1]))


def down_weights_kernel(count, after, nodes, ws, wr, biases, wo, *refs):
    del after
    packs, refs = refs[:count], refs[count:]
    receivers, ws_high, ws_low, wo_high, wo_low, wr_high, wr_low, bias_all = refs
    width = ws.shape[1]
    share = ws.shape[0] // shared_among(packs)
    collect_in(ws, packs, 0, ws_high, ws_low)
    collect_in(wr, packs, share, wr_high, wr_low)
    collect_out(wo, packs, 2 * share, wo_high, wo_low)
    collect_bias(biases[1:2], packs, 3 * share, bias_all)
    for g in range(wr_high.shape[0]):
        product = dot3(nodes[...], wr_high[g], wr_low[g])
        receivers[:, g * width : (g + 1) * width] = 0.5 * (product + bias_all[g][0:1])


def bottom_weights_kernel(count, ws, wr, biases, wo, *refs):
    packs, (ws_high, ws_low, wr_high, wr_low, wo_high, wo_low, bias_all) = refs[:count], refs[count:]
    share = ws.shape[0] // shared_among(packs)
    collect_in(ws, packs, 0, ws_high, ws_low)
    collect_in(wr, packs, share, wr_high, wr_low)
    collect_out(wo, packs, 2 * share, wo_high, wo_low)
    collect_bias(biases[2:3], packs, 3 * share, bias_all)


def bottom_picks_kernel(rim, after, links, picks):
    del after
    wanted = upright(links[...])
    size = rim * wanted.shape[1]
    names = lax.broadcasted_iota(jnp.int32, (rim, 3 * rim), 1)
    for i in range(wanted.shape[0] // rim):
        strip = wanted[i * rim : (i + 1) * rim]
        picks[i * size : (i + 1) * size, :] = one_hot(strip, names + i * rim)


def down_rows(nodes, receivers, sources, senders, wo_high, wo_low, gain):
    blocks = senders.shape[0] // 2
    column = lax.broadcasted_iota(jnp.int32, (nodes.shape[0], 2 * blocks), 1)
    names = jnp.where(column < blocks, column, column - blocks)
    picked = dot(one_hot(sources, names), senders)
    hidden = silu_sum(picked, receivers, sources.shape[1])
    return nodes + gain * normed(dot3(hidden, wo_high, wo_low))


def down_edge_kernel(count, rim, *refs):
    parts, refs = refs[:count], refs[count:]
    (coarse_up, gains, nodes, receivers, sources, ws_high, ws_low, wo_high, wo_low) = refs[:9]
    new_coarse, senders, head, tail = refs[9:]
    rows = coarse_up[...] + gains[1:2] * normed(added(parts))
    new_coarse[...] = rows
    blocks = rows.shape[0]
    width = ws_high.shape[2]
    for g in range(ws_high.shape[0]):
        columns = slice(g * width, (g + 1) * width)
        high, low = split(0.5 * dot3(rows, ws_high[g], ws_low[g]))
        senders[0:blocks, columns] = high
        senders[blocks : 2 * blocks, columns] = low
    total = nodes.shape[0]
    wanted = upright(sources[...])
    for out, place in ((head, slice(0, rim)), (tail, slice(total - rim, total))):
        out[...] = down_rows(
            nodes[place], receivers[place], wanted[place], senders[...], wo_high[...], wo_low[...], gains[2:3]
        )


def down_middle_kernel(rim, nodes, receivers, sources, senders, wo_high, wo_low, gains, middle):
    place = slice(rim, nodes.shape[0] - rim)
    middle[...] = down_rows(
        nodes[place], receivers[place], upright(sources[...])[place], senders[...], wo_high[...], wo_low[...], gains[2:3]
    )


def bottom_rows(nodes, receivers, picks, sender_high, sender_low, wo_high, wo_low, gain):
    half = wo_high.shape[0] // 2
    hidden = []
    for place in (slice(0, half), slice(half, 2 * half)):
        picked = dot(picks, sender_high[:, place]) + dot(picks, sender_low[:, place])
        hidden.append(silu_sum(picked, receivers[:, place], picks.shape[0] // nodes.shape[0]))
    return nodes + gain * normed(dot3(jnp.concatenate(hidden, axis=1), wo_high, wo_low))


def bottom_middle_kernel(rim, head, middle, tail, picks, ws_high, ws_low, wr_high, wr_low, wo_high, wo_low, bias, gains, senders_high, senders_low, receivers, out):
    nodes = jnp.concatenate([head[...], middle[...], tail[...]], axis=0)
    nodes_high, nodes_low = split(nodes)
    width = ws_high.shape[2]
    for g in range(ws_high.shape[0]):
        columns = slice(g * width, (g + 1) * width)
        product = dot(nodes_high, ws_high[g]) + (dot(nodes_high, ws_low[g]) + dot(nodes_low, ws_high[g]))
        senders_high[:, columns], senders_low[:, columns] = split(0.5 * product)
        product = dot(nodes_high, wr_high[g]) + (dot(nodes_high, wr_low[g]) + dot(nodes_low, wr_high[g]))
        receivers[:, columns] = 0.5 * (product + bias[g][0:1])
    total = nodes.shape[0]
    size = picks.shape[0] * rim // total
    for first in range(rim, total - rim, rim):
        place = slice(first, first + rim)
        reach = slice(first - rim, first + 2 * rim)
        out[first - rim : first, :] = bottom_rows(
            middle[first - rim : first], receivers[place], picks[first // rim * size : (first // rim + 1) * size],
            senders_high[reach], senders_low[reach], wo_high[...], wo_low[...], gains[3:4],
        )


def bottom_edge_kernel(rim, before, after, head, tail, inner, picks, senders_high, senders_low, receivers, ws_high, ws_low, wo_high, wo_low, gains, out):
    total = out.shape[0]
    size = picks.shape[0] * rim // total
    out[rim : total - rim, :] = inner[...]
    outer = split(jnp.concatenate([before[...], after[...]], axis=0))
    projected = jnp.concatenate(
        [
            dot(outer[0], ws_high[g]) + (dot(outer[0], ws_low[g]) + dot(outer[1], ws_high[g]))
            for g in range(ws_high.shape[0])
        ],
        axis=1,
    )
    outer_high, outer_low = split(0.5 * projected)
    for side, (nodes, place, reach) in enumerate(
        ((head, slice(0, rim), slice(0, 2 * rim)), (tail, slice(total - rim, total), slice(total - 2 * rim, total)))
    ):
        strip = slice(side * rim, (side + 1) * rim)
        order = (lambda a, b: [a, b]) if side == 0 else (lambda a, b: [b, a])
        high = jnp.concatenate(order(outer_high[strip], senders_high[reach]), axis=0)
        low = jnp.concatenate(order(outer_low[strip], senders_low[reach]), axis=0)
        out[place, :] = bottom_rows(
            nodes[...], receivers[place], picks[place.start // rim * size : (place.start // rim + 1) * size],
            high, low, wo_high[...], wo_low[...], gains[3:4],
        )


whole = pl.BlockSpec(memory_space=pltpu.VMEM)
away = pl.BlockSpec(memory_space=pl.ANY)


def call(kernel, outs, operands, flops, scratch=(), far=(), far_outs=(), limit=limit_bytes):
    moved = sum(x.size * x.dtype.itemsize for x in (*outs, *operands))
    return pl.pallas_call(
        kernel,
        out_shape=tuple(outs),
        in_specs=[away if i in far else whole for i in range(len(operands))],
        out_specs=tuple(away if i in far_outs else whole for i in range(len(outs))),
        scratch_shapes=list(scratch),
        compiler_params=pltpu.CompilerParams(vmem_limit_bytes=limit),
        cost_estimate=pl.CostEstimate(flops=int(flops), bytes_accessed=moved, transcendentals=0),
    )(*operands)


def like(shape, kind=f32):
    return jax.ShapeDtypeStruct(tuple(shape), kind)


def shifted(values, axis, step):
    count = lax.axis_size(axis)
    return lax.ppermute(values, axis, [(i, (i + step) % count) for i in range(count)])


def sub_parts(part):
    if lax.axis_size("sub") == 2:
        return [part, shifted(part, "sub", 1)]
    return [lax.psum(part, "sub")]


def coarse_pieces(senders, others):
    patches, lvls = lax.axis_size("patch"), lax.axis_size("lvl")
    if patches > most_direct:
        return [lax.all_gather(senders, ("patch", "lvl"), axis=0, tiled=True)], others
    near = [[senders] + [shifted(senders, "lvl", t) for t in range(1, lvls)]]
    pieces = [shifted(senders, "patch", s) for s in range(1, patches)]
    pieces, others = lax.optimization_barrier((pieces, others))
    near += [[piece] + [shifted(piece, "lvl", t) for t in range(1, lvls)] for piece in pieces]
    return [row[t] for t in range(lvls) for row in near], others


def coarse_names(rows):
    patches, lvls = lax.axis_size("patch"), lax.axis_size("lvl")
    place = jnp.arange(rows * patches * lvls, dtype=jnp.int32)
    if patches > most_direct:
        return place[None]
    step, away = (place // rows) % patches, place // (rows * patches)
    patch = (lax.axis_index("patch") - step) % patches
    lvl = (lax.axis_index("lvl") - away) % lvls
    return ((patch * lvls + lvl) * rows + place % rows)[None].astype(jnp.int32)


def held(values, event):
    return lax.optimization_barrier((values, event))[0]


def over_sub(pack):
    return [shifted(pack, "sub", s) for s in range(1, lax.axis_size("sub"))]


def over_parts(shares):
    return [
        [shifted(share, "parts", p) for p in range(1, lax.axis_size("parts"))] for share in shares
    ]


def over_lvl(shares):
    return [
        [share] + [shifted(share, "lvl", t) for t in range(1, lax.axis_size("lvl"))]
        for share in shares
    ]


def all_shares(shares, others):
    near = over_lvl(shares)
    far = [over_lvl(row) for row in others]
    return [x for first, row in zip(near, far) for x in (first + [y for group in row for y in group])]


def body(
    node_states,
    coarse_states,
    children,
    down_sources,
    bottom_links,
    coarse_links,
    upward_sender,
    upward_receiver,
    upward_bias,
    upward_output,
    upward_gain,
    coarse_sender,
    coarse_receiver,
    coarse_bias,
    coarse_output,
    coarse_gain,
    downward_sender,
    downward_receiver,
    downward_bias,
    downward_output,
    downward_gain,
    bottom_sender,
    bottom_receiver,
    bottom_bias,
    bottom_output,
    bottom_gain,
):
    rows, latent = node_states.shape
    blocks = coarse_states.shape[0]
    width = upward_sender.shape[1]
    subs = lax.axis_size("sub")
    hidden = width * subs
    rim = rows // 4
    weights = [like((subs, latent, width), bf16)] * 2
    outputs = [like((hidden, latent), bf16)] * 2
    bias_rows = like((subs, 8, width))

    columns = latent // width
    ensemble, lvls = lax.axis_size("parts"), lax.axis_size("lvl")
    share = latent // (ensemble * lvls)
    row = 8
    pack = like((3 * share + row, width))
    copying = [pltpu.SemaphoreType.DMA((3 + columns,))]
    (down_pack,) = call(
        functools.partial(share_kernel, ensemble),
        [pack],
        [downward_sender, downward_receiver, downward_output, downward_bias[None]],
        latent,
        copying,
        far=range(4),
        limit=large_limit,
    )
    down_near = over_sub(down_pack)
    (part,) = call(
        upward_kernel,
        [like((blocks, latent))],
        [node_states, coarse_states, children.T, upward_sender, upward_receiver, upward_bias[None], upward_output],
        6 * rows * latent * width + 4 * children.size * rows * width,
        limit=wide_limit,
    )
    parts = sub_parts(part)
    ws_high, ws_low, wr_high, wr_low, wo_high, wo_low, gains, biases, bottom_pack = call(
        functools.partial(coarse_ready_kernel, ensemble),
        [like((latent, width), bf16)] * 4
        + [like((width, latent), bf16)] * 2
        + [like((4, latent)), like((3, width)), pack],
        [
            part, coarse_sender, coarse_receiver, coarse_output,
            upward_gain[None], coarse_gain[None], downward_gain[None], bottom_gain[None],
            coarse_bias[None], downward_bias[None], bottom_bias[None],
            bottom_sender, bottom_receiver, bottom_output, bottom_bias[None],
        ],
        latent * hidden,
        copying,
        far=(0, 11, 12, 13, 14),
    )
    bottom_near = over_sub(held(bottom_pack, parts[-1]))
    down_far = over_parts(down_near)
    coarse_up, senders, receivers = call(
        functools.partial(coarse_project_kernel, len(parts)),
        [like((blocks, latent)), like((blocks, width)), like((blocks, width))],
        [*parts, coarse_states, gains, biases, ws_high, ws_low, wr_high, wr_low],
        12 * blocks * latent * width,
    )
    names = coarse_names(blocks)
    (picks,) = call(
        picks_kernel,
        [like((coarse_links.size, names.size), bf16)],
        [senders, coarse_links.T, names],
        coarse_links.size * names.size,
        far=(0,),
    )
    (bottom_picks,) = call(
        functools.partial(bottom_picks_kernel, rim),
        [like((bottom_links.size, 3 * rim), bf16)],
        [senders, bottom_links.T],
        bottom_links.size * 3 * rim,
        far=(0,),
    )
    pieces, (picks, bottom_picks, down_near, down_far, bottom_near) = coarse_pieces(
        senders, (picks, bottom_picks, down_near, down_far, bottom_near)
    )
    down_packs = all_shares(down_near, down_far)
    bottom_far = over_parts(bottom_near)
    (part,) = call(
        functools.partial(coarse_kernel, len(pieces)),
        [like((blocks, latent))],
        [*pieces, picks, receivers, wo_high, wo_low, *down_packs],
        4 * coarse_links.size * names.size * width,
        far=range(len(pieces) + 4, len(pieces) + 4 + len(down_packs)),
    )
    parts = sub_parts(part)
    receivers, ws_high, ws_low, wo_high, wo_low = call(
        functools.partial(down_weights_kernel, len(down_packs)),
        [like((rows, hidden)), *weights, *outputs],
        [part, node_states, downward_sender, downward_receiver, biases, downward_output, *down_packs],
        6 * rows * latent * hidden,
        [pltpu.VMEM((subs, latent, width), bf16)] * 2 + [pltpu.VMEM((subs, 8, width), f32)],
        far=(0,),
    )
    parts, bottom_far = lax.optimization_barrier((parts, bottom_far))
    new_coarse, senders, head, tail = call(
        functools.partial(down_edge_kernel, len(parts), rim),
        [like((blocks, latent)), like((2 * blocks, hidden), bf16), like((rim, latent)), like((rim, latent))],
        [*parts, coarse_up, gains, node_states, receivers, down_sources.T, ws_high, ws_low, wo_high, wo_low],
        6 * 2 * rim * latent * hidden,
    )
    ring = ("patch", "lvl")
    before, after = shifted(tail, ring, 1), shifted(head, ring, -1)
    (middle,) = call(
        functools.partial(down_middle_kernel, rim),
        [like((rows - 2 * rim, latent))],
        [node_states, receivers, down_sources.T, senders, wo_high, wo_low, gains],
        6 * (rows - 2 * rim) * latent * hidden,
    )

    bottom_near, bottom_far = held((bottom_near, bottom_far), head)
    bottom_packs = all_shares(bottom_near, bottom_far)
    ws_high, ws_low, wr_high, wr_low, wo_high, wo_low, bias = call(
        functools.partial(bottom_weights_kernel, len(bottom_packs)),
        [*weights, *weights, *outputs, bias_rows],
        [bottom_sender, bottom_receiver, biases, bottom_output, *bottom_packs],
        latent * hidden,
    )
    senders_high, senders_low, receivers, inner = call(
        functools.partial(bottom_middle_kernel, rim),
        [like((rows, hidden), bf16), like((rows, hidden), bf16), like((rows, hidden)), like((rows - 2 * rim, latent))],
        [head, middle, tail, bottom_picks, ws_high, ws_low, wr_high, wr_low, wo_high, wo_low, bias, gains],
        (12 * rows + 12 * rows) * latent * hidden,
    )
    (new_nodes,) = call(
        functools.partial(bottom_edge_kernel, rim),
        [like((rows, latent))],
        [before, after, head, tail, inner, bottom_picks, senders_high, senders_low, receivers, ws_high, ws_low, wo_high, wo_low, gains],
        24 * rim * latent * hidden,
    )
    return (new_nodes, new_coarse)


def solution(mesh):
    split_rows, level_rows = P(("parts", "patch", "lvl"), None), P(("patch", "lvl"), None)
    weights = (P(None, "sub"), P(None, "sub"), P("sub"), P("sub", None), P())
    in_specs = (split_rows, split_rows, *([level_rows] * 4), *(weights * 4))
    out_specs = (split_rows, split_rows)
    return jax.shard_map(body, mesh=mesh, in_specs=in_specs, out_specs=out_specs, check_vma=False)
```

```python
import functools

import jax
import jax.numpy as jnp
from jax import lax
from jax.experimental import pallas as pl
from jax.experimental.pallas import tpu as pltpu
from jax.sharding import PartitionSpec as P

epsilon = 1e-05
f32 = jnp.float32
bf16 = jnp.bfloat16
limit_bytes = 12 * 1024 * 1024
tight_limit = 60 * 1024 * 1024
most_direct = 4


def split(values):
    high = values.astype(bf16)
    return high, (values - high.astype(f32)).astype(bf16)


def dot(a, b):
    return jnp.dot(a, b, preferred_element_type=f32)


def dot3(a, b_high, b_low):
    a_high, a_low = split(a)
    return dot(a_high, b_high) + (dot(a_high, b_low) + dot(a_low, b_high))


def normed(values):
    center = values - jnp.mean(values, axis=-1, keepdims=True)
    spread = jnp.mean(center * center, axis=-1, keepdims=True)
    return center * lax.rsqrt(spread + epsilon)


def upright(rows):
    count, size = rows.shape
    tall, wide = -count % 8, -size % 128
    if tall:
        rows = jnp.concatenate([rows, jnp.zeros((tall, size), rows.dtype)], axis=0)
    if wide:
        rows = jnp.concatenate([rows, jnp.zeros((count + tall, wide), rows.dtype)], axis=1)
    return jnp.transpose(rows)[:size, :count]


def one_hot(wanted, names):
    return jnp.concatenate(
        [
            jnp.where(wanted[:, k : k + 1] == names, 1.0, 0.0).astype(bf16)
            for k in range(wanted.shape[1])
        ],
        axis=0,
    )


def silu_sum(picked, halves, count):
    rows = halves.shape[0]
    total = None
    for k in range(count):
        u = picked[k * rows : (k + 1) * rows] + halves
        term = u + u * jnp.tanh(u)
        total = term if total is None else total + term
    return total


def added(refs):
    total = refs[0][...]
    for ref in refs[1:]:
        total = total + ref[...]
    return total


def started(copies, sems):
    moves = [pltpu.make_async_copy(a, b, sems.at[i]) for i, (a, b) in enumerate(copies)]
    for move in moves:
        move.start()
    return moves


def strips(source, target, count):
    rows = source.shape[0] // count
    return [
        (source.at[pl.ds(i * rows, rows)], target.at[pl.ds(i * rows, rows)]) for i in range(count)
    ]


def upward_kernel(nodes_hbm, coarse_hbm, ws_hbm, wr_hbm, wo_hbm, children, bias, part, nodes, coarse, ws, wr, wo, high, low, sems):
    cuts = 4
    moves = started(
        strips(ws_hbm, ws, cuts)
        + strips(nodes_hbm, nodes, cuts)
        + [(coarse_hbm, coarse)]
        + strips(wr_hbm, wr, cuts)
        + strips(wo_hbm, wo, cuts),
        sems,
    )
    wanted = upright(children[...])
    names = lax.broadcasted_iota(jnp.int32, (wanted.shape[0], nodes.shape[0]), 1)
    picks = one_hot(wanted, names)
    for move in moves[:cuts]:
        move.wait()
    ws_high, ws_low = split(ws[...])
    rows = nodes.shape[0] // cuts
    for i in range(cuts):
        moves[cuts + i].wait()
        place = slice(i * rows, (i + 1) * rows)
        high[place], low[place] = split(0.5 * dot3(nodes[place], ws_high, ws_low))
    for move in moves[2 * cuts : 3 * cuts + 1]:
        move.wait()
    receivers = 0.5 * (dot3(coarse[...], *split(wr[...])) + bias[...])
    picked = dot(picks, high[...]) + dot(picks, low[...])
    hidden = silu_sum(picked, receivers, wanted.shape[1])
    for move in moves[3 * cuts + 1 :]:
        move.wait()
    part[...] = dot3(hidden, *split(wo[...]))


def coarse_ready_kernel(ws, wr, wo, *refs):
    params, (ws_high, ws_low, wr_high, wr_low, wo_high, wo_low, gains, biases) = refs[:7], refs[7:]
    for i in range(4):
        gains[i : i + 1] = params[i][...]
    for i in range(3):
        biases[i : i + 1] = params[4 + i][...]
    ws_high[...], ws_low[...] = split(ws[...])
    wr_high[...], wr_low[...] = split(wr[...])
    wo_high[...], wo_low[...] = split(wo[...])


def share_kernel(parts, *refs):
    down_own, bottom_own, (down_pack, bottom_pack, sems) = refs[:4], refs[4:8], refs[8:]
    copies = share_copies(down_own, down_pack, parts) + share_copies(bottom_own, bottom_pack, parts)
    for move in started(copies, sems):
        move.wait()


def shares(parts):
    lvls = lax.axis_size("lvl")
    mine = lax.axis_index("lvl")
    if parts > 1:
        mine = lax.axis_index("parts") * lvls + mine
    return mine, parts * lvls


def share_copies(sources, pack, parts):
    mine, count = shares(parts)
    width = pack.shape[1]
    copies, at = [], 0
    for source in sources:
        rows = source.shape[0] // count
        if source.shape[0] == 1:
            copies.append((source, pack.at[pl.ds(at, 1)]))
            at += 8
            continue
        strip = pl.ds(pl.multiple_of(mine * rows, rows), rows)
        for j in range(source.shape[1] // width):
            copies.append((source.at[strip, pl.ds(j * width, width)], pack.at[pl.ds(at, rows)]))
            at += rows
    return copies


def picks_kernel(rim, patches, blocks, coarse_links, bottom_links, coarse_picks, bottom_picks):
    wanted = upright(coarse_links[...])
    rows = wanted.shape[0]
    lvls = lax.axis_size("lvl")
    column = lax.broadcasted_iota(jnp.int32, (rows, blocks), 1)
    for t in range(lvls):
        for s in range(patches):
            patch = lax.rem(lax.axis_index("patch") + patches - s, patches)
            lvl = lax.rem(lax.axis_index("lvl") + lvls - t, lvls)
            first = (patch * lvls + lvl) * blocks
            at = (t * patches + s) * blocks
            coarse_picks[:, at : at + blocks] = one_hot(wanted, column + first)
    wanted = upright(bottom_links[...])
    size = rim * wanted.shape[1]
    names = lax.broadcasted_iota(jnp.int32, (rim, 3 * rim), 1)
    for i in range(wanted.shape[0] // rim):
        strip = wanted[i * rim : (i + 1) * rim]
        bottom_picks[i * size : (i + 1) * size, :] = one_hot(strip, names + i * rim)


def coarse_project_kernel(count, *refs):
    parts, refs = refs[:count], refs[count:]
    coarse, gains, biases, ws_high, ws_low, wr_high, wr_low, updated, senders, receivers = refs
    rows = coarse[...] + gains[0:1] * normed(added(parts))
    updated[...] = rows
    senders[...] = 0.5 * dot3(rows, ws_high[...], ws_low[...])
    receivers[...] = 0.5 * (dot3(rows, wr_high[...], wr_low[...]) + biases[0:1])


def coarse_kernel(count, *refs):
    pieces, (all_picks, receivers, wo_high, wo_low) = refs[:count], refs[count : count + 4]
    part = refs[-1]
    senders = jnp.concatenate([piece[...] for piece in pieces], axis=0)
    sender_high, sender_low = split(senders)
    picks = all_picks[...]
    picked = dot(picks, sender_high) + dot(picks, sender_low)
    hidden = silu_sum(picked, receivers[...], picks.shape[0] // receivers.shape[0])
    part[...] = dot3(hidden, wo_high[...], wo_low[...])


def shared_among(packs):
    return max(1, len(packs) // max(1, lax.axis_size("sub") - 1))


def fetched_shares(packs):
    subs, lvls = lax.axis_size("sub"), lax.axis_size("lvl")
    parts = len(packs) // max(1, (subs - 1) * lvls)
    sub, part, lvl = lax.axis_index("sub"), lax.axis_index("parts"), lax.axis_index("lvl")
    place = iter(packs)
    for s in range(1, subs):
        for p in range(parts):
            for t in range(lvls):
                mine = lax.rem(part + parts - p, parts) * lvls + lax.rem(lvl + lvls - t, lvls)
                yield next(place), lax.rem(sub + subs - s, subs), mine, p == 0 and t == 0


def collect_in(own, packs, at, high, low):
    sub = lax.axis_index("sub")
    count = shared_among(packs)
    high[sub], low[sub] = split(own[...])
    share = own.shape[0] // count
    for pack, block, mine, _ in fetched_shares(packs):
        rows = pl.ds(pl.multiple_of(mine * share, share), share)
        high[block, rows, :], low[block, rows, :] = split(pack[at : at + share, :])


def collect_out(own, packs, at, high, low):
    sub = lax.axis_index("sub")
    count = shared_among(packs)
    width, latent = own.shape
    rows = pl.ds(pl.multiple_of(sub * width, width), width)
    high[rows, :], low[rows, :] = split(own[...])
    thin = width // count
    for pack, block, mine, _ in fetched_shares(packs):
        rows = pl.ds(pl.multiple_of(block * width + mine * thin, thin), thin)
        for j in range(latent // width):
            first, second = split(pack[at + j * thin : at + (j + 1) * thin, :])
            high[rows, j * width : (j + 1) * width] = first
            low[rows, j * width : (j + 1) * width] = second


def collect_bias(own, packs, at, out):
    out[lax.axis_index("sub")] = jnp.broadcast_to(own, (8, own.shape[1]))
    for pack, block, _, whole_row in fetched_shares(packs):
        if whole_row:
            out[block] = jnp.broadcast_to(pack[at : at + 1, :], (8, own.shape[1]))


def down_weights_kernel(count, nodes, ws, wr, biases, wo, *refs):
    packs, refs = refs[:count], refs[count:]
    receivers, ws_high, ws_low, wo_high, wo_low, wr_high, wr_low, bias_all = refs
    width = ws.shape[1]
    share = ws.shape[0] // shared_among(packs)
    collect_in(ws, packs, 0, ws_high, ws_low)
    collect_in(wr, packs, share, wr_high, wr_low)
    collect_out(wo, packs, 2 * share, wo_high, wo_low)
    collect_bias(biases[1:2], packs, 3 * share, bias_all)
    for g in range(wr_high.shape[0]):
        product = dot3(nodes[...], wr_high[g], wr_low[g])
        receivers[:, g * width : (g + 1) * width] = 0.5 * (product + bias_all[g][0:1])


def bottom_weights_kernel(count, ws, wr, biases, wo, *refs):
    packs, (ws_high, ws_low, wr_high, wr_low, wo_high, wo_low, bias_all) = refs[:count], refs[count:]
    share = ws.shape[0] // shared_among(packs)
    collect_in(ws, packs, 0, ws_high, ws_low)
    collect_in(wr, packs, share, wr_high, wr_low)
    collect_out(wo, packs, 2 * share, wo_high, wo_low)
    collect_bias(biases[2:3], packs, 3 * share, bias_all)


def down_rows(nodes, receivers, sources, senders, wo_high, wo_low, gain):
    blocks = senders.shape[0] // 2
    column = lax.broadcasted_iota(jnp.int32, (nodes.shape[0], 2 * blocks), 1)
    names = jnp.where(column < blocks, column, column - blocks)
    picked = dot(one_hot(sources, names), senders)
    hidden = silu_sum(picked, receivers, sources.shape[1])
    return nodes + gain * normed(dot3(hidden, wo_high, wo_low))


def down_edge_kernel(count, rim, *refs):
    parts, refs = refs[:count], refs[count:]
    (coarse_up, gains, nodes, receivers, sources, ws_high, ws_low, wo_high, wo_low) = refs[:9]
    new_coarse, senders, head, tail = refs[9:]
    rows = coarse_up[...] + gains[1:2] * normed(added(parts))
    new_coarse[...] = rows
    blocks = rows.shape[0]
    width = ws_high.shape[2]
    for g in range(ws_high.shape[0]):
        columns = slice(g * width, (g + 1) * width)
        high, low = split(0.5 * dot3(rows, ws_high[g], ws_low[g]))
        senders[0:blocks, columns] = high
        senders[blocks : 2 * blocks, columns] = low
    total = nodes.shape[0]
    wanted = upright(sources[...])
    for out, place in ((head, slice(0, rim)), (tail, slice(total - rim, total))):
        out[...] = down_rows(
            nodes[place], receivers[place], wanted[place], senders[...], wo_high[...], wo_low[...], gains[2:3]
        )


def down_middle_kernel(rim, nodes, receivers, sources, senders, wo_high, wo_low, gains, middle):
    place = slice(rim, nodes.shape[0] - rim)
    middle[...] = down_rows(
        nodes[place], receivers[place], upright(sources[...])[place], senders[...], wo_high[...], wo_low[...], gains[2:3]
    )


def bottom_rows(nodes, receivers, picks, sender_high, sender_low, wo_high, wo_low, gain):
    half = wo_high.shape[0] // 2
    hidden = []
    for place in (slice(0, half), slice(half, 2 * half)):
        picked = dot(picks, sender_high[:, place]) + dot(picks, sender_low[:, place])
        hidden.append(silu_sum(picked, receivers[:, place], picks.shape[0] // nodes.shape[0]))
    return nodes + gain * normed(dot3(jnp.concatenate(hidden, axis=1), wo_high, wo_low))


def bottom_middle_kernel(rim, head, middle, tail, picks, ws_high, ws_low, wr_high, wr_low, wo_high, wo_low, bias, gains, senders_high, senders_low, receivers, out):
    nodes = jnp.concatenate([head[...], middle[...], tail[...]], axis=0)
    nodes_high, nodes_low = split(nodes)
    width = ws_high.shape[2]
    for g in range(ws_high.shape[0]):
        columns = slice(g * width, (g + 1) * width)
        product = dot(nodes_high, ws_high[g]) + (dot(nodes_high, ws_low[g]) + dot(nodes_low, ws_high[g]))
        senders_high[:, columns], senders_low[:, columns] = split(0.5 * product)
        product = dot(nodes_high, wr_high[g]) + (dot(nodes_high, wr_low[g]) + dot(nodes_low, wr_high[g]))
        receivers[:, columns] = 0.5 * (product + bias[g][0:1])
    total = nodes.shape[0]
    size = picks.shape[0] * rim // total
    for first in range(rim, total - rim, rim):
        place = slice(first, first + rim)
        reach = slice(first - rim, first + 2 * rim)
        out[first - rim : first, :] = bottom_rows(
            middle[first - rim : first], receivers[place], picks[first // rim * size : (first // rim + 1) * size],
            senders_high[reach], senders_low[reach], wo_high[...], wo_low[...], gains[3:4],
        )


def bottom_edge_kernel(rim, before, after, head, tail, inner, picks, senders_high, senders_low, receivers, ws_high, ws_low, wo_high, wo_low, gains, out):
    total = out.shape[0]
    size = picks.shape[0] * rim // total
    out[rim : total - rim, :] = inner[...]
    outer = split(jnp.concatenate([before[...], after[...]], axis=0))
    projected = jnp.concatenate(
        [
            dot(outer[0], ws_high[g]) + (dot(outer[0], ws_low[g]) + dot(outer[1], ws_high[g]))
            for g in range(ws_high.shape[0])
        ],
        axis=1,
    )
    outer_high, outer_low = split(0.5 * projected)
    for side, (nodes, place, reach) in enumerate(
        ((head, slice(0, rim), slice(0, 2 * rim)), (tail, slice(total - rim, total), slice(total - 2 * rim, total)))
    ):
        strip = slice(side * rim, (side + 1) * rim)
        order = (lambda a, b: [a, b]) if side == 0 else (lambda a, b: [b, a])
        high = jnp.concatenate(order(outer_high[strip], senders_high[reach]), axis=0)
        low = jnp.concatenate(order(outer_low[strip], senders_low[reach]), axis=0)
        out[place, :] = bottom_rows(
            nodes[...], receivers[place], picks[place.start // rim * size : (place.start // rim + 1) * size],
            high, low, wo_high[...], wo_low[...], gains[3:4],
        )


whole = pl.BlockSpec(memory_space=pltpu.VMEM)
away = pl.BlockSpec(memory_space=pl.ANY)


def call(kernel, outs, operands, flops, scratch=(), far=(), unread=0, limit=limit_bytes):
    moved = sum(x.size * x.dtype.itemsize for x in (*outs, *operands))
    read = len(operands) - unread
    specs = [away if i in far else whole for i in range(read)] + [away] * unread
    return pl.pallas_call(
        (lambda *refs: kernel(*refs[:read], *refs[read + unread :])) if unread else kernel,
        out_shape=tuple(outs),
        in_specs=specs,
        out_specs=tuple([whole] * len(outs)),
        scratch_shapes=list(scratch),
        compiler_params=pltpu.CompilerParams(vmem_limit_bytes=limit),
        cost_estimate=pl.CostEstimate(flops=int(flops), bytes_accessed=moved, transcendentals=0),
    )(*operands)


def like(shape, kind=f32):
    return jax.ShapeDtypeStruct(tuple(shape), kind)


def shifted(values, axis, step):
    count = lax.axis_size(axis)
    return lax.ppermute(values, axis, [(i, (i + step) % count) for i in range(count)])


def sub_parts(part):
    if lax.axis_size("sub") == 2:
        return [part, shifted(part, "sub", 1)]
    return [lax.psum(part, "sub")]


def coarse_pieces(senders, others):
    patches, lvls = lax.axis_size("patch"), lax.axis_size("lvl")
    if patches > most_direct:
        return [lax.all_gather(senders, ("patch", "lvl"), axis=0, tiled=True)], others
    near = [[senders] + [shifted(senders, "lvl", t) for t in range(1, lvls)]]
    pieces = [shifted(senders, "patch", s) for s in range(1, patches)]
    pieces, others = lax.optimization_barrier((pieces, others))
    near += [[piece] + [shifted(piece, "lvl", t) for t in range(1, lvls)] for piece in pieces]
    return [row[t] for t in range(lvls) for row in near], others


def held(values, event):
    return lax.optimization_barrier((values, event))[0]


def over_sub(pack):
    return [shifted(pack, "sub", s) for s in range(1, lax.axis_size("sub"))]


def over_parts(shares):
    return [
        [shifted(share, "parts", p) for p in range(1, lax.axis_size("parts"))] for share in shares
    ]


def over_lvl(shares):
    return [
        [share] + [shifted(share, "lvl", t) for t in range(1, lax.axis_size("lvl"))]
        for share in shares
    ]


def all_shares(shares, others):
    near = over_lvl(shares)
    far = [over_lvl(row) for row in others]
    return [x for first, row in zip(near, far) for x in (first + [y for group in row for y in group])]


def body(
    node_states,
    coarse_states,
    children,
    down_sources,
    bottom_links,
    coarse_links,
    upward_sender,
    upward_receiver,
    upward_bias,
    upward_output,
    upward_gain,
    coarse_sender,
    coarse_receiver,
    coarse_bias,
    coarse_output,
    coarse_gain,
    downward_sender,
    downward_receiver,
    downward_bias,
    downward_output,
    downward_gain,
    bottom_sender,
    bottom_receiver,
    bottom_bias,
    bottom_output,
    bottom_gain,
):
    rows, latent = node_states.shape
    blocks = coarse_states.shape[0]
    width = upward_sender.shape[1]
    subs = lax.axis_size("sub")
    hidden = width * subs
    rim = rows // 4
    weights = [like((subs, latent, width), bf16)] * 2
    outputs = [like((hidden, latent), bf16)] * 2
    bias_rows = like((subs, 8, width))

    columns = latent // width
    ensemble, lvls = lax.axis_size("parts"), lax.axis_size("lvl")
    share = latent // (ensemble * lvls)
    pack = like((3 * share + 8, width))

    down_pack, bottom_pack = call(
        functools.partial(share_kernel, ensemble),
        [pack, pack],
        [
            downward_sender, downward_receiver, downward_output, downward_bias[None],
            bottom_sender, bottom_receiver, bottom_output, bottom_bias[None],
        ],
        latent,
        [pltpu.SemaphoreType.DMA((6 + 2 * columns,))],
        far=range(8),
        limit=tight_limit,
    )
    down_near = over_sub(down_pack)
    (part,) = call(
        upward_kernel,
        [like((blocks, latent))],
        [
            node_states, coarse_states, upward_sender, upward_receiver, upward_output,
            children.T, upward_bias[None],
        ],
        6 * rows * latent * width + 4 * children.size * rows * width,
        [
            pltpu.VMEM((rows, latent), f32),
            pltpu.VMEM((blocks, latent), f32),
            pltpu.VMEM((latent, width), f32),
            pltpu.VMEM((latent, width), f32),
            pltpu.VMEM((width, latent), f32),
            pltpu.VMEM((rows, width), bf16),
            pltpu.VMEM((rows, width), bf16),
            pltpu.SemaphoreType.DMA((17,)),
        ],
        far=range(5),
        limit=tight_limit,
    )
    parts = sub_parts(part)
    ws_high, ws_low, wr_high, wr_low, wo_high, wo_low, gains, biases = call(
        coarse_ready_kernel,
        [like((latent, width), bf16)] * 4
        + [like((width, latent), bf16)] * 2
        + [like((4, latent)), like((3, width))],
        [
            coarse_sender, coarse_receiver, coarse_output,
            upward_gain[None], coarse_gain[None], downward_gain[None], bottom_gain[None],
            coarse_bias[None], downward_bias[None], bottom_bias[None], part,
        ],
        latent * hidden,
        unread=1,
    )
    bottom_near = over_sub(held(bottom_pack, (parts[-1], gains)))
    down_far = over_parts(down_near)
    coarse_up, senders, receivers = call(
        functools.partial(coarse_project_kernel, len(parts)),
        [like((blocks, latent)), like((blocks, width)), like((blocks, width))],
        [*parts, coarse_states, gains, biases, ws_high, ws_low, wr_high, wr_low],
        12 * blocks * latent * width,
    )
    patches = lax.axis_size("patch")
    names = blocks * patches * lvls
    picks, bottom_picks = call(
        functools.partial(picks_kernel, rim, patches, blocks),
        [like((coarse_links.size, names), bf16), like((bottom_links.size, 3 * rim), bf16)],
        [coarse_links.T, bottom_links.T, senders],
        coarse_links.size * names,
        unread=1,
    )
    pieces, (picks, bottom_picks, down_near, down_far, bottom_near) = coarse_pieces(
        senders, (picks, bottom_picks, down_near, down_far, bottom_near)
    )
    down_packs = all_shares(down_near, down_far)
    bottom_far = over_parts(bottom_near)
    (part,) = call(
        functools.partial(coarse_kernel, len(pieces)),
        [like((blocks, latent))],
        [*pieces, picks, receivers, wo_high, wo_low, *down_packs],
        4 * coarse_links.size * names * width,
        unread=len(down_packs),
    )
    parts = sub_parts(part)
    receivers, ws_high, ws_low, wo_high, wo_low = call(
        functools.partial(down_weights_kernel, len(down_packs)),
        [like((rows, hidden)), *weights, *outputs],
        [node_states, downward_sender, downward_receiver, biases, downward_output, *down_packs, part],
        6 * rows * latent * hidden,
        [pltpu.VMEM((subs, latent, width), bf16)] * 2 + [pltpu.VMEM((subs, 8, width), f32)],
        unread=1,
    )
    parts, bottom_far = lax.optimization_barrier((parts, bottom_far))
    new_coarse, senders, head, tail = call(
        functools.partial(down_edge_kernel, len(parts), rim),
        [like((blocks, latent)), like((2 * blocks, hidden), bf16), like((rim, latent)), like((rim, latent))],
        [*parts, coarse_up, gains, node_states, receivers, down_sources.T, ws_high, ws_low, wo_high, wo_low],
        6 * 2 * rim * latent * hidden,
    )
    ring = ("patch", "lvl")
    before, after = shifted(tail, ring, 1), shifted(head, ring, -1)
    (middle,) = call(
        functools.partial(down_middle_kernel, rim),
        [like((rows - 2 * rim, latent))],
        [node_states, receivers, down_sources.T, senders, wo_high, wo_low, gains],
        6 * (rows - 2 * rim) * latent * hidden,
    )

    bottom_near, bottom_far = held((bottom_near, bottom_far), head)
    bottom_packs = all_shares(bottom_near, bottom_far)
    ws_high, ws_low, wr_high, wr_low, wo_high, wo_low, bias = call(
        functools.partial(bottom_weights_kernel, len(bottom_packs)),
        [*weights, *weights, *outputs, bias_rows],
        [bottom_sender, bottom_receiver, biases, bottom_output, *bottom_packs],
        latent * hidden,
    )
    senders_high, senders_low, receivers, inner = call(
        functools.partial(bottom_middle_kernel, rim),
        [like((rows, hidden), bf16), like((rows, hidden), bf16), like((rows, hidden)), like((rows - 2 * rim, latent))],
        [head, middle, tail, bottom_picks, ws_high, ws_low, wr_high, wr_low, wo_high, wo_low, bias, gains],
        (12 * rows + 12 * rows) * latent * hidden,
    )
    (new_nodes,) = call(
        functools.partial(bottom_edge_kernel, rim),
        [like((rows, latent))],
        [before, after, head, tail, inner, bottom_picks, senders_high, senders_low, receivers, ws_high, ws_low, wo_high, wo_low, gains],
        24 * rim * latent * hidden,
    )
    return (new_nodes, new_coarse)


def solution(mesh):
    split_rows, level_rows = P(("parts", "patch", "lvl"), None), P(("patch", "lvl"), None)
    weights = (P(None, "sub"), P(None, "sub"), P("sub"), P("sub", None), P())
    in_specs = (split_rows, split_rows, *([level_rows] * 4), *(weights * 4))
    out_specs = (split_rows, split_rows)
    return jax.shard_map(body, mesh=mesh, in_specs=in_specs, out_specs=out_specs, check_vma=False)
```

```python
import functools

import jax
import jax.numpy as jnp
from jax import lax
from jax.experimental import pallas as pl
from jax.experimental.pallas import tpu as pltpu
from jax.sharding import PartitionSpec as P

epsilon = 1e-05
f32 = jnp.float32
bf16 = jnp.bfloat16
limit_bytes = 12 * 1024 * 1024
tight_limit = 64 * 1000 * 1000
most_direct = 4


def split(values):
    high = values.astype(bf16)
    return high, (values - high.astype(f32)).astype(bf16)


def dot(a, b):
    return jnp.dot(a, b, preferred_element_type=f32)


def dot3(a, b_high, b_low):
    a_high, a_low = split(a)
    return dot(a_high, b_high) + (dot(a_high, b_low) + dot(a_low, b_high))


def normed(values):
    center = values - jnp.mean(values, axis=-1, keepdims=True)
    spread = jnp.mean(center * center, axis=-1, keepdims=True)
    return center * lax.rsqrt(spread + epsilon)


def upright(rows):
    count, size = rows.shape
    tall, wide = -count % 8, -size % 128
    if tall:
        rows = jnp.concatenate([rows, jnp.zeros((tall, size), rows.dtype)], axis=0)
    if wide:
        rows = jnp.concatenate([rows, jnp.zeros((count + tall, wide), rows.dtype)], axis=1)
    return jnp.transpose(rows)[:size, :count]


def one_hot(wanted, names):
    return jnp.concatenate(
        [
            jnp.where(wanted[:, k : k + 1] == names, 1.0, 0.0).astype(bf16)
            for k in range(wanted.shape[1])
        ],
        axis=0,
    )


def silu_sum(picked, halves, count):
    rows = halves.shape[0]
    total = None
    for k in range(count):
        u = picked[k * rows : (k + 1) * rows] + halves
        term = u + u * jnp.tanh(u)
        total = term if total is None else total + term
    return total


def added(refs):
    total = refs[0][...]
    for ref in refs[1:]:
        total = total + ref[...]
    return total


def started(copies, sems):
    moves = [pltpu.make_async_copy(a, b, sems.at[i]) for i, (a, b) in enumerate(copies)]
    for move in moves:
        move.start()
    return moves


def strips(source, target, count):
    rows = source.shape[0] // count
    return [
        (source.at[pl.ds(i * rows, rows)], target.at[pl.ds(i * rows, rows)]) for i in range(count)
    ]


def upward_kernel(nodes_hbm, coarse_hbm, ws_hbm, wr_hbm, wo_hbm, children, bias, part, nodes, coarse, ws, wr, wo, high, low, sems):
    cuts = 8
    moves = started(
        strips(ws_hbm, ws, cuts)
        + strips(nodes_hbm, nodes, cuts)
        + [(coarse_hbm, coarse)]
        + strips(wr_hbm, wr, cuts)
        + strips(wo_hbm, wo, cuts),
        sems,
    )
    wanted = upright(children[...])
    names = lax.broadcasted_iota(jnp.int32, (wanted.shape[0], nodes.shape[0]), 1)
    picks = one_hot(wanted, names)
    for move in moves[:cuts]:
        move.wait()
    ws_high, ws_low = split(ws[...])
    rows = nodes.shape[0] // cuts
    for i in range(cuts):
        moves[cuts + i].wait()
        place = slice(i * rows, (i + 1) * rows)
        high[place], low[place] = split(0.5 * dot3(nodes[place], ws_high, ws_low))
    for move in moves[2 * cuts : 3 * cuts + 1]:
        move.wait()
    receivers = 0.5 * (dot3(coarse[...], *split(wr[...])) + bias[...])
    picked = dot(picks, high[...]) + dot(picks, low[...])
    hidden = silu_sum(picked, receivers, wanted.shape[1])
    for move in moves[3 * cuts + 1 :]:
        move.wait()
    part[...] = dot3(hidden, *split(wo[...]))


def share_kernel(*refs):
    params, down_own, bottom_own, refs = refs[:7], refs[7:11], refs[11:15], refs[15:]
    gains, biases, down_pack, bottom_pack, sems = refs
    moves = started(
        share_copies(down_own, down_pack, "parts") + share_copies(bottom_own, bottom_pack, "patch"), sems
    )
    for i in range(4):
        gains[i : i + 1] = params[i][...]
    for i in range(3):
        biases[i : i + 1] = params[4 + i][...]
    for move in moves:
        move.wait()


def shares(axis):
    lvls = lax.axis_size("lvl")
    place, count = partners(axis)
    return place * lvls + lax.axis_index("lvl"), count * lvls


def share_copies(sources, pack, axis):
    mine, count = shares(axis)
    width = pack.shape[1]
    copies, at = [], 0
    for source in sources:
        rows = source.shape[0] // count
        if source.shape[0] == 1:
            copies.append((source, pack.at[pl.ds(at, 1)]))
            at += 8
            continue
        strip = pl.ds(pl.multiple_of(mine * rows, rows), rows)
        for j in range(source.shape[1] // width):
            copies.append((source.at[strip, pl.ds(j * width, width)], pack.at[pl.ds(at, rows)]))
            at += rows
    return copies


def picks_kernel(rim, patches, blocks, coarse_links, bottom_links, coarse_picks, bottom_picks):
    wanted = upright(coarse_links[...])
    rows = wanted.shape[0]
    lvls = lax.axis_size("lvl")
    column = lax.broadcasted_iota(jnp.int32, (rows, blocks), 1)
    for t in range(lvls):
        for s in range(patches):
            patch = lax.rem(lax.axis_index("patch") + patches - s, patches)
            lvl = lax.rem(lax.axis_index("lvl") + lvls - t, lvls)
            first = (patch * lvls + lvl) * blocks
            at = (t * patches + s) * blocks
            coarse_picks[:, at : at + blocks] = one_hot(wanted, column + first)
    wanted = upright(bottom_links[...])
    size = rim * wanted.shape[1]
    names = lax.broadcasted_iota(jnp.int32, (rim, 3 * rim), 1)
    for i in range(wanted.shape[0] // rim):
        strip = wanted[i * rim : (i + 1) * rim]
        bottom_picks[i * size : (i + 1) * size, :] = one_hot(strip, names + i * rim)


def coarse_project_kernel(count, *refs):
    parts, refs = refs[:count], refs[count:]
    coarse, gains, biases, ws, wr, updated, senders, receivers = refs
    rows = coarse[...] + gains[0:1] * normed(added(parts))
    updated[...] = rows
    senders[...] = 0.5 * dot3(rows, *split(ws[...]))
    receivers[...] = 0.5 * (dot3(rows, *split(wr[...])) + biases[0:1])


def coarse_kernel(count, *refs):
    pieces, (all_picks, receivers, wo) = refs[:count], refs[count : count + 3]
    part = refs[-1]
    senders = jnp.concatenate([piece[...] for piece in pieces], axis=0)
    sender_high, sender_low = split(senders)
    picks = all_picks[...]
    picked = dot(picks, sender_high) + dot(picks, sender_low)
    hidden = silu_sum(picked, receivers[...], picks.shape[0] // receivers.shape[0])
    part[...] = dot3(hidden, *split(wo[...]))


def fetched_shares(packs, axis):
    subs, lvls = lax.axis_size("sub"), lax.axis_size("lvl")
    sub, lvl = lax.axis_index("sub"), lax.axis_index("lvl")
    place, count = partners(axis)
    left = iter(packs)
    for s in range(1, subs):
        for p in range(count):
            for t in range(lvls):
                mine = lax.rem(place + count - p, count) * lvls + lax.rem(lvl + lvls - t, lvls)
                yield next(left), lax.rem(sub + subs - s, subs), mine, p == 0 and t == 0


def collect_in(own, packs, axis, at, high, low):
    sub = lax.axis_index("sub")
    high[sub], low[sub] = split(own[...])
    share = own.shape[0] // shares(axis)[1]
    for pack, block, mine, _ in fetched_shares(packs, axis):
        rows = pl.ds(pl.multiple_of(mine * share, share), share)
        high[block, rows, :], low[block, rows, :] = split(pack[at : at + share, :])


def collect_out(own, packs, axis, at, high, low):
    sub = lax.axis_index("sub")
    width, latent = own.shape
    rows = pl.ds(pl.multiple_of(sub * width, width), width)
    high[rows, :], low[rows, :] = split(own[...])
    thin = width // shares(axis)[1]
    for pack, block, mine, _ in fetched_shares(packs, axis):
        rows = pl.ds(pl.multiple_of(block * width + mine * thin, thin), thin)
        for j in range(latent // width):
            first, second = split(pack[at + j * thin : at + (j + 1) * thin, :])
            high[rows, j * width : (j + 1) * width] = first
            low[rows, j * width : (j + 1) * width] = second


def collect_bias(own, packs, axis, at, out):
    out[lax.axis_index("sub")] = jnp.broadcast_to(own, (8, own.shape[1]))
    for pack, block, _, whole_row in fetched_shares(packs, axis):
        if whole_row:
            out[block] = jnp.broadcast_to(pack[at : at + 1, :], (8, own.shape[1]))


def down_weights_kernel(count, nodes, ws, wr, biases, wo, *refs):
    packs, refs = refs[:count], refs[count:]
    receivers, ws_high, ws_low, wo_high, wo_low, wr_high, wr_low, bias_all = refs
    width = ws.shape[1]
    share = ws.shape[0] // shares("parts")[1]
    collect_in(ws, packs, "parts", 0, ws_high, ws_low)
    collect_in(wr, packs, "parts", share, wr_high, wr_low)
    collect_out(wo, packs, "parts", 2 * share, wo_high, wo_low)
    collect_bias(biases[1:2], packs, "parts", 3 * share, bias_all)
    for g in range(wr_high.shape[0]):
        product = dot3(nodes[...], wr_high[g], wr_low[g])
        receivers[:, g * width : (g + 1) * width] = 0.5 * (product + bias_all[g][0:1])


def bottom_weights_kernel(count, ws, wr, biases, wo, *refs):
    packs, (ws_high, ws_low, wr_high, wr_low, wo_high, wo_low, bias_all) = refs[:count], refs[count:]
    share = ws.shape[0] // shares("patch")[1]
    collect_in(ws, packs, "patch", 0, ws_high, ws_low)
    collect_in(wr, packs, "patch", share, wr_high, wr_low)
    collect_out(wo, packs, "patch", 2 * share, wo_high, wo_low)
    collect_bias(biases[2:3], packs, "patch", 3 * share, bias_all)


def down_rows(nodes, receivers, sources, senders, wo_high, wo_low, gain):
    blocks = senders.shape[0] // 2
    column = lax.broadcasted_iota(jnp.int32, (nodes.shape[0], 2 * blocks), 1)
    names = jnp.where(column < blocks, column, column - blocks)
    picked = dot(one_hot(sources, names), senders)
    hidden = silu_sum(picked, receivers, sources.shape[1])
    return nodes + gain * normed(dot3(hidden, wo_high, wo_low))


def down_edge_kernel(count, rim, *refs):
    parts, refs = refs[:count], refs[count:]
    (coarse_up, gains, nodes, receivers, sources, ws_high, ws_low, wo_high, wo_low) = refs[:9]
    new_coarse, senders, head, tail = refs[9:]
    rows = coarse_up[...] + gains[1:2] * normed(added(parts))
    new_coarse[...] = rows
    blocks = rows.shape[0]
    width = ws_high.shape[2]
    for g in range(ws_high.shape[0]):
        columns = slice(g * width, (g + 1) * width)
        high, low = split(0.5 * dot3(rows, ws_high[g], ws_low[g]))
        senders[0:blocks, columns] = high
        senders[blocks : 2 * blocks, columns] = low
    total = nodes.shape[0]
    wanted = upright(sources[...])
    for out, place in ((head, slice(0, rim)), (tail, slice(total - rim, total))):
        out[...] = down_rows(
            nodes[place], receivers[place], wanted[place], senders[...], wo_high[...], wo_low[...], gains[2:3]
        )


def down_middle_kernel(rim, nodes, receivers, sources, senders, wo_high, wo_low, gains, middle):
    place = slice(rim, nodes.shape[0] - rim)
    middle[...] = down_rows(
        nodes[place], receivers[place], upright(sources[...])[place], senders[...], wo_high[...], wo_low[...], gains[2:3]
    )


def bottom_rows(nodes, receivers, picks, sender_high, sender_low, wo_high, wo_low, gain):
    half = wo_high.shape[0] // 2
    hidden = []
    for place in (slice(0, half), slice(half, 2 * half)):
        picked = dot(picks, sender_high[:, place]) + dot(picks, sender_low[:, place])
        hidden.append(silu_sum(picked, receivers[:, place], picks.shape[0] // nodes.shape[0]))
    return nodes + gain * normed(dot3(jnp.concatenate(hidden, axis=1), wo_high, wo_low))


def bottom_middle_kernel(rim, head, middle, tail, picks, ws_high, ws_low, wr_high, wr_low, wo_high, wo_low, bias, gains, senders_high, senders_low, receivers, out):
    nodes = jnp.concatenate([head[...], middle[...], tail[...]], axis=0)
    nodes_high, nodes_low = split(nodes)
    width = ws_high.shape[2]
    for g in range(ws_high.shape[0]):
        columns = slice(g * width, (g + 1) * width)
        product = dot(nodes_high, ws_high[g]) + (dot(nodes_high, ws_low[g]) + dot(nodes_low, ws_high[g]))
        senders_high[:, columns], senders_low[:, columns] = split(0.5 * product)
        product = dot(nodes_high, wr_high[g]) + (dot(nodes_high, wr_low[g]) + dot(nodes_low, wr_high[g]))
        receivers[:, columns] = 0.5 * (product + bias[g][0:1])
    total = nodes.shape[0]
    size = picks.shape[0] * rim // total
    for first in range(rim, total - rim, rim):
        place = slice(first, first + rim)
        reach = slice(first - rim, first + 2 * rim)
        out[first - rim : first, :] = bottom_rows(
            middle[first - rim : first], receivers[place], picks[first // rim * size : (first // rim + 1) * size],
            senders_high[reach], senders_low[reach], wo_high[...], wo_low[...], gains[3:4],
        )


def bottom_edge_kernel(rim, before, after, head, tail, inner, picks, senders_high, senders_low, receivers, ws_high, ws_low, wo_high, wo_low, gains, out):
    total = out.shape[0]
    size = picks.shape[0] * rim // total
    out[rim : total - rim, :] = inner[...]
    outer = split(jnp.concatenate([before[...], after[...]], axis=0))
    projected = jnp.concatenate(
        [
            dot(outer[0], ws_high[g]) + (dot(outer[0], ws_low[g]) + dot(outer[1], ws_high[g]))
            for g in range(ws_high.shape[0])
        ],
        axis=1,
    )
    outer_high, outer_low = split(0.5 * projected)
    for side, (nodes, place, reach) in enumerate(
        ((head, slice(0, rim), slice(0, 2 * rim)), (tail, slice(total - rim, total), slice(total - 2 * rim, total)))
    ):
        strip = slice(side * rim, (side + 1) * rim)
        order = (lambda a, b: [a, b]) if side == 0 else (lambda a, b: [b, a])
        high = jnp.concatenate(order(outer_high[strip], senders_high[reach]), axis=0)
        low = jnp.concatenate(order(outer_low[strip], senders_low[reach]), axis=0)
        out[place, :] = bottom_rows(
            nodes[...], receivers[place], picks[place.start // rim * size : (place.start // rim + 1) * size],
            high, low, wo_high[...], wo_low[...], gains[3:4],
        )


whole = pl.BlockSpec(memory_space=pltpu.VMEM)
away = pl.BlockSpec(memory_space=pl.ANY)


def call(kernel, outs, operands, flops, scratch=(), far=(), unread=0, limit=limit_bytes):
    moved = sum(x.size * x.dtype.itemsize for x in (*outs, *operands))
    read = len(operands) - unread
    specs = [away if i in far else whole for i in range(read)] + [away] * unread
    return pl.pallas_call(
        (lambda *refs: kernel(*refs[:read], *refs[read + unread :])) if unread else kernel,
        out_shape=tuple(outs),
        in_specs=specs,
        out_specs=tuple([whole] * len(outs)),
        scratch_shapes=list(scratch),
        compiler_params=pltpu.CompilerParams(vmem_limit_bytes=limit),
        cost_estimate=pl.CostEstimate(flops=int(flops), bytes_accessed=moved, transcendentals=0),
    )(*operands)


def like(shape, kind=f32):
    return jax.ShapeDtypeStruct(tuple(shape), kind)


def shifted(values, axis, step):
    count = lax.axis_size(axis)
    return lax.ppermute(values, axis, [(i, (i + step) % count) for i in range(count)])


def sub_parts(part):
    if lax.axis_size("sub") == 2:
        return [part, shifted(part, "sub", 1)]
    return [lax.psum(part, "sub")]


def coarse_pieces(senders, others):
    patches, lvls = lax.axis_size("patch"), lax.axis_size("lvl")
    if patches > most_direct:
        return [lax.all_gather(senders, ("patch", "lvl"), axis=0, tiled=True)], others
    near = [[senders] + [shifted(senders, "lvl", t) for t in range(1, lvls)]]
    pieces = [shifted(senders, "patch", s) for s in range(1, patches)]
    pieces, others = lax.optimization_barrier((pieces, others))
    near += [[piece] + [shifted(piece, "lvl", t) for t in range(1, lvls)] for piece in pieces]
    return [row[t] for t in range(lvls) for row in near], others


def held(values, event):
    return lax.optimization_barrier((values, event))[0]


def over_sub(pack):
    return [shifted(pack, "sub", s) for s in range(1, lax.axis_size("sub"))]


def partners(axis):
    if axis == "parts":
        return lax.axis_index(axis), lax.axis_size(axis)
    count = 2 if lax.axis_size(axis) % 2 == 0 else 1
    return lax.rem(lax.axis_index(axis), count), count


def over_partners(share_list, axis):
    size, count = lax.axis_size(axis), partners(axis)[1]
    return [
        [
            lax.ppermute(share, axis, [(i, i - i % count + (i + p) % count) for i in range(size)])
            for p in range(1, count)
        ]
        for share in share_list
    ]


def over_lvl(shares):
    return [
        [share] + [shifted(share, "lvl", t) for t in range(1, lax.axis_size("lvl"))]
        for share in shares
    ]


def all_shares(shares, others):
    near = over_lvl(shares)
    far = [over_lvl(row) for row in others]
    return [x for first, row in zip(near, far) for x in (first + [y for group in row for y in group])]


def body(
    node_states,
    coarse_states,
    children,
    down_sources,
    bottom_links,
    coarse_links,
    upward_sender,
    upward_receiver,
    upward_bias,
    upward_output,
    upward_gain,
    coarse_sender,
    coarse_receiver,
    coarse_bias,
    coarse_output,
    coarse_gain,
    downward_sender,
    downward_receiver,
    downward_bias,
    downward_output,
    downward_gain,
    bottom_sender,
    bottom_receiver,
    bottom_bias,
    bottom_output,
    bottom_gain,
):
    rows, latent = node_states.shape
    blocks = coarse_states.shape[0]
    width = upward_sender.shape[1]
    subs = lax.axis_size("sub")
    hidden = width * subs
    rim = rows // 4
    weights = [like((subs, latent, width), bf16)] * 2
    outputs = [like((hidden, latent), bf16)] * 2
    bias_rows = like((subs, 8, width))

    columns = latent // width
    lvls = lax.axis_size("lvl")

    def pack(axis):
        count = shares(axis)[1]
        return like((2 * latent // count + width // count * columns + 8, width))

    (part,) = call(
        upward_kernel,
        [like((blocks, latent))],
        [
            node_states, coarse_states, upward_sender, upward_receiver, upward_output,
            children.T, upward_bias[None],
        ],
        6 * rows * latent * width + 4 * children.size * rows * width,
        [
            pltpu.VMEM((rows, latent), f32),
            pltpu.VMEM((blocks, latent), f32),
            pltpu.VMEM((latent, width), f32),
            pltpu.VMEM((latent, width), f32),
            pltpu.VMEM((width, latent), f32),
            pltpu.VMEM((rows, width), bf16),
            pltpu.VMEM((rows, width), bf16),
            pltpu.SemaphoreType.DMA((33,)),
        ],
        far=range(5),
        limit=tight_limit,
    )
    parts = sub_parts(part)
    down_own = (downward_sender, downward_receiver, downward_output, downward_bias[None])
    bottom_own = (bottom_sender, bottom_receiver, bottom_output, bottom_bias[None])
    gains, biases, down_pack, bottom_pack = call(
        share_kernel,
        [like((4, latent)), like((3, width)), pack("parts"), pack("patch")],
        [
            upward_gain[None], coarse_gain[None], downward_gain[None], bottom_gain[None],
            coarse_bias[None], downward_bias[None], bottom_bias[None],
            *down_own, *bottom_own, part,
        ],
        latent * hidden,
        [pltpu.SemaphoreType.DMA((6 + 2 * columns,))],
        far=range(7, 15),
        unread=1,
        limit=tight_limit,
    )
    down_near, bottom_near = map(over_sub, held((down_pack, bottom_pack), parts[-1]))
    coarse_up, senders, receivers = call(
        functools.partial(coarse_project_kernel, len(parts)),
        [like((blocks, latent)), like((blocks, width)), like((blocks, width))],
        [*parts, coarse_states, gains, biases, coarse_sender, coarse_receiver],
        12 * blocks * latent * width,
    )
    patches = lax.axis_size("patch")
    names = blocks * patches * lvls
    picks, bottom_picks = call(
        functools.partial(picks_kernel, rim, patches, blocks),
        [like((coarse_links.size, names), bf16), like((bottom_links.size, 3 * rim), bf16)],
        [coarse_links.T, bottom_links.T, senders],
        coarse_links.size * names,
        unread=1,
    )
    pieces, (picks, bottom_picks, down_near) = coarse_pieces(
        senders, (picks, bottom_picks, down_near)
    )
    down_far = over_partners(down_near, "parts")
    (part,) = call(
        functools.partial(coarse_kernel, len(pieces)),
        [like((blocks, latent))],
        [*pieces, picks, receivers, coarse_output, *bottom_near],
        4 * coarse_links.size * names * width,
        unread=len(bottom_near),
    )
    bottom_near = held(bottom_near, part)
    parts = sub_parts(part)
    bottom_far = over_partners(bottom_near, "patch")
    down_packs = all_shares(*held((down_near, down_far), parts[-1]))
    receivers, ws_high, ws_low, wo_high, wo_low = call(
        functools.partial(down_weights_kernel, len(down_packs)),
        [like((rows, hidden)), *weights, *outputs],
        [node_states, downward_sender, downward_receiver, biases, downward_output, *down_packs, part, *(x for row in bottom_far for x in row)],
        6 * rows * latent * hidden,
        [pltpu.VMEM((subs, latent, width), bf16)] * 2 + [pltpu.VMEM((subs, 8, width), f32)],
        unread=1 + sum(map(len, bottom_far)),
    )
    new_coarse, senders, head, tail = call(
        functools.partial(down_edge_kernel, len(parts), rim),
        [like((blocks, latent)), like((2 * blocks, hidden), bf16), like((rim, latent)), like((rim, latent))],
        [*parts, coarse_up, gains, node_states, receivers, down_sources.T, ws_high, ws_low, wo_high, wo_low],
        6 * 2 * rim * latent * hidden,
    )
    ring = ("patch", "lvl")
    before, after = shifted(tail, ring, 1), shifted(head, ring, -1)
    (middle,) = call(
        functools.partial(down_middle_kernel, rim),
        [like((rows - 2 * rim, latent))],
        [node_states, receivers, down_sources.T, senders, wo_high, wo_low, gains],
        6 * (rows - 2 * rim) * latent * hidden,
    )

    bottom_near, bottom_far = held((bottom_near, bottom_far), head)
    bottom_packs = all_shares(bottom_near, bottom_far)
    ws_high, ws_low, wr_high, wr_low, wo_high, wo_low, bias = call(
        functools.partial(bottom_weights_kernel, len(bottom_packs)),
        [*weights, *weights, *outputs, bias_rows],
        [bottom_sender, bottom_receiver, biases, bottom_output, *bottom_packs],
        latent * hidden,
    )
    senders_high, senders_low, receivers, inner = call(
        functools.partial(bottom_middle_kernel, rim),
        [like((rows, hidden), bf16), like((rows, hidden), bf16), like((rows, hidden)), like((rows - 2 * rim, latent))],
        [head, middle, tail, bottom_picks, ws_high, ws_low, wr_high, wr_low, wo_high, wo_low, bias, gains],
        (12 * rows + 12 * rows) * latent * hidden,
    )
    (new_nodes,) = call(
        functools.partial(bottom_edge_kernel, rim),
        [like((rows, latent))],
        [before, after, head, tail, inner, bottom_picks, senders_high, senders_low, receivers, ws_high, ws_low, wo_high, wo_low, gains],
        24 * rim * latent * hidden,
    )
    return (new_nodes, new_coarse)


def solution(mesh):
    split_rows, level_rows = P(("parts", "patch", "lvl"), None), P(("patch", "lvl"), None)
    weights = (P(None, "sub"), P(None, "sub"), P("sub"), P("sub", None), P())
    in_specs = (split_rows, split_rows, *([level_rows] * 4), *(weights * 4))
    out_specs = (split_rows, split_rows)
    return jax.shard_map(body, mesh=mesh, in_specs=in_specs, out_specs=out_specs, check_vma=False)
```

```python
import functools

import jax
import jax.numpy as jnp
from jax import lax
from jax.experimental import pallas as pl
from jax.experimental.pallas import tpu as pltpu
from jax.sharding import PartitionSpec as P

epsilon = 1e-05
f32 = jnp.float32
bf16 = jnp.bfloat16
limit_bytes = 12 * 1024 * 1024
share_limit = 58 * 1000 * 1000
up_limit = 50 * 1000 * 1000
most_direct = 4


def split(values):
    high = values.astype(bf16)
    return high, (values - high.astype(f32)).astype(bf16)


def dot(a, b):
    return jnp.dot(a, b, preferred_element_type=f32)


def dot3(a, b_high, b_low):
    a_high, a_low = split(a)
    return dot(a_high, b_high) + (dot(a_high, b_low) + dot(a_low, b_high))


def normed(values):
    center = values - jnp.mean(values, axis=-1, keepdims=True)
    spread = jnp.mean(center * center, axis=-1, keepdims=True)
    return center * lax.rsqrt(spread + epsilon)


def upright(rows):
    count, size = rows.shape
    tall, wide = -count % 8, -size % 128
    if tall:
        rows = jnp.concatenate([rows, jnp.zeros((tall, size), rows.dtype)], axis=0)
    if wide:
        rows = jnp.concatenate([rows, jnp.zeros((count + tall, wide), rows.dtype)], axis=1)
    return jnp.transpose(rows)[:size, :count]


def one_hot(wanted, names):
    return jnp.concatenate(
        [
            jnp.where(wanted[:, k : k + 1] == names, 1.0, 0.0).astype(bf16)
            for k in range(wanted.shape[1])
        ],
        axis=0,
    )


def silu_sum(picked, halves, count):
    rows = halves.shape[0]
    total = None
    for k in range(count):
        u = picked[k * rows : (k + 1) * rows] + halves
        term = u + u * jnp.tanh(u)
        total = term if total is None else total + term
    return total


def added(refs):
    total = refs[0][...]
    for ref in refs[1:]:
        total = total + ref[...]
    return total


def started(copies, sems):
    moves = [pltpu.make_async_copy(a, b, sems.at[i]) for i, (a, b) in enumerate(copies)]
    for move in moves:
        move.start()
    return moves


def upward_kernel(nodes, coarse, children, ws, wr, bias, wo, part):
    wanted = upright(children[...])
    names = lax.broadcasted_iota(jnp.int32, (wanted.shape[0], nodes.shape[0]), 1)
    picks = one_hot(wanted, names)
    sender_high, sender_low = split(0.5 * dot3(nodes[...], *split(ws[...])))
    receivers = 0.5 * (dot3(coarse[...], *split(wr[...])) + bias[...])
    picked = dot(picks, sender_high) + dot(picks, sender_low)
    hidden = silu_sum(picked, receivers, wanted.shape[1])
    part[...] = dot3(hidden, *split(wo[...]))


def stack_kernel(*refs):
    params, (gains, biases) = refs[:7], refs[7:]
    for i in range(4):
        gains[i : i + 1] = params[i][...]
    for i in range(3):
        biases[i : i + 1] = params[4 + i][...]


def share_kernel(*refs):
    down_own, bottom_own, (down_pack, bottom_pack, sems) = refs[:4], refs[4:8], refs[8:]
    copies = share_copies(down_own, down_pack, "parts") + share_copies(bottom_own, bottom_pack, "patch")
    for move in started(copies, sems):
        move.wait()


def shares(axis):
    lvls = lax.axis_size("lvl")
    place, count = partners(axis)
    return place * lvls + lax.axis_index("lvl"), count * lvls


def share_copies(sources, pack, axis):
    mine, count = shares(axis)
    width = pack.shape[1]
    copies, at = [], 0
    for source in sources:
        rows = source.shape[0] // count
        if source.shape[0] == 1:
            copies.append((source, pack.at[pl.ds(at, 1)]))
            at += 8
            continue
        strip = pl.ds(pl.multiple_of(mine * rows, rows), rows)
        for j in range(source.shape[1] // width):
            copies.append((source.at[strip, pl.ds(j * width, width)], pack.at[pl.ds(at, rows)]))
            at += rows
    return copies


def picks_kernel(rim, patches, blocks, coarse_links, bottom_links, coarse_picks, bottom_picks):
    wanted = upright(coarse_links[...])
    rows = wanted.shape[0]
    lvls = lax.axis_size("lvl")
    column = lax.broadcasted_iota(jnp.int32, (rows, blocks), 1)
    for t in range(lvls):
        for s in range(patches):
            patch = lax.rem(lax.axis_index("patch") + patches - s, patches)
            lvl = lax.rem(lax.axis_index("lvl") + lvls - t, lvls)
            first = (patch * lvls + lvl) * blocks
            at = (t * patches + s) * blocks
            coarse_picks[:, at : at + blocks] = one_hot(wanted, column + first)
    wanted = upright(bottom_links[...])
    size = rim * wanted.shape[1]
    names = lax.broadcasted_iota(jnp.int32, (rim, 3 * rim), 1)
    for i in range(wanted.shape[0] // rim):
        strip = wanted[i * rim : (i + 1) * rim]
        bottom_picks[i * size : (i + 1) * size, :] = one_hot(strip, names + i * rim)


def coarse_project_kernel(count, *refs):
    parts, refs = refs[:count], refs[count:]
    coarse, gains, biases, ws, wr, updated, senders, receivers = refs
    rows = coarse[...] + gains[0:1] * normed(added(parts))
    updated[...] = rows
    senders[...] = 0.5 * dot3(rows, *split(ws[...]))
    receivers[...] = 0.5 * (dot3(rows, *split(wr[...])) + biases[0:1])


def coarse_kernel(count, *refs):
    pieces, (all_picks, receivers, wo) = refs[:count], refs[count : count + 3]
    part = refs[-1]
    senders = jnp.concatenate([piece[...] for piece in pieces], axis=0)
    sender_high, sender_low = split(senders)
    picks = all_picks[...]
    picked = dot(picks, sender_high) + dot(picks, sender_low)
    hidden = silu_sum(picked, receivers[...], picks.shape[0] // receivers.shape[0])
    part[...] = dot3(hidden, *split(wo[...]))


def fetched_shares(packs, axis):
    subs, lvls = lax.axis_size("sub"), lax.axis_size("lvl")
    sub, lvl = lax.axis_index("sub"), lax.axis_index("lvl")
    place, count = partners(axis)
    left = iter(packs)
    for s in range(1, subs):
        for p in range(count):
            for t in range(lvls):
                mine = lax.rem(place + count - p, count) * lvls + lax.rem(lvl + lvls - t, lvls)
                yield next(left), lax.rem(sub + subs - s, subs), mine, p == 0 and t == 0


def collect_in(own, packs, axis, at, high, low):
    sub = lax.axis_index("sub")
    high[sub], low[sub] = split(own[...])
    share = own.shape[0] // shares(axis)[1]
    for pack, block, mine, _ in fetched_shares(packs, axis):
        rows = pl.ds(pl.multiple_of(mine * share, share), share)
        high[block, rows, :], low[block, rows, :] = split(pack[at : at + share, :])


def collect_out(own, packs, axis, at, high, low):
    sub = lax.axis_index("sub")
    width, latent = own.shape
    rows = pl.ds(pl.multiple_of(sub * width, width), width)
    high[rows, :], low[rows, :] = split(own[...])
    thin = width // shares(axis)[1]
    for pack, block, mine, _ in fetched_shares(packs, axis):
        rows = pl.ds(pl.multiple_of(block * width + mine * thin, thin), thin)
        for j in range(latent // width):
            first, second = split(pack[at + j * thin : at + (j + 1) * thin, :])
            high[rows, j * width : (j + 1) * width] = first
            low[rows, j * width : (j + 1) * width] = second


def collect_bias(own, packs, axis, at, out):
    out[lax.axis_index("sub")] = jnp.broadcast_to(own, (8, own.shape[1]))
    for pack, block, _, whole_row in fetched_shares(packs, axis):
        if whole_row:
            out[block] = jnp.broadcast_to(pack[at : at + 1, :], (8, own.shape[1]))


def down_weights_kernel(count, nodes, ws, wr, biases, wo, *refs):
    packs, refs = refs[:count], refs[count:]
    receivers, ws_high, ws_low, wo_high, wo_low, wr_high, wr_low, bias_all = refs
    width = ws.shape[1]
    share = ws.shape[0] // shares("parts")[1]
    collect_in(ws, packs, "parts", 0, ws_high, ws_low)
    collect_in(wr, packs, "parts", share, wr_high, wr_low)
    collect_out(wo, packs, "parts", 2 * share, wo_high, wo_low)
    collect_bias(biases[1:2], packs, "parts", 3 * share, bias_all)
    for g in range(wr_high.shape[0]):
        product = dot3(nodes[...], wr_high[g], wr_low[g])
        receivers[:, g * width : (g + 1) * width] = 0.5 * (product + bias_all[g][0:1])


def bottom_weights_kernel(count, ws, wr, biases, wo, *refs):
    packs, (ws_high, ws_low, wr_high, wr_low, wo_high, wo_low, bias_all) = refs[:count], refs[count:]
    share = ws.shape[0] // shares("patch")[1]
    collect_in(ws, packs, "patch", 0, ws_high, ws_low)
    collect_in(wr, packs, "patch", share, wr_high, wr_low)
    collect_out(wo, packs, "patch", 2 * share, wo_high, wo_low)
    collect_bias(biases[2:3], packs, "patch", 3 * share, bias_all)


def down_rows(nodes, receivers, sources, senders, wo_high, wo_low, gain):
    blocks = senders.shape[0] // 2
    column = lax.broadcasted_iota(jnp.int32, (nodes.shape[0], 2 * blocks), 1)
    names = jnp.where(column < blocks, column, column - blocks)
    picked = dot(one_hot(sources, names), senders)
    hidden = silu_sum(picked, receivers, sources.shape[1])
    return nodes + gain * normed(dot3(hidden, wo_high, wo_low))


def down_edge_kernel(count, rim, *refs):
    parts, refs = refs[:count], refs[count:]
    (coarse_up, gains, nodes, receivers, sources, ws_high, ws_low, wo_high, wo_low) = refs[:9]
    new_coarse, senders, head, tail = refs[9:]
    rows = coarse_up[...] + gains[1:2] * normed(added(parts))
    new_coarse[...] = rows
    blocks = rows.shape[0]
    width = ws_high.shape[2]
    for g in range(ws_high.shape[0]):
        columns = slice(g * width, (g + 1) * width)
        high, low = split(0.5 * dot3(rows, ws_high[g], ws_low[g]))
        senders[0:blocks, columns] = high
        senders[blocks : 2 * blocks, columns] = low
    total = nodes.shape[0]
    wanted = upright(sources[...])
    for out, place in ((head, slice(0, rim)), (tail, slice(total - rim, total))):
        out[...] = down_rows(
            nodes[place], receivers[place], wanted[place], senders[...], wo_high[...], wo_low[...], gains[2:3]
        )


def down_middle_kernel(rim, nodes, receivers, sources, senders, wo_high, wo_low, gains, middle):
    place = slice(rim, nodes.shape[0] - rim)
    middle[...] = down_rows(
        nodes[place], receivers[place], upright(sources[...])[place], senders[...], wo_high[...], wo_low[...], gains[2:3]
    )


def bottom_rows(nodes, receivers, picks, sender_high, sender_low, wo_high, wo_low, gain):
    half = wo_high.shape[0] // 2
    hidden = []
    for place in (slice(0, half), slice(half, 2 * half)):
        picked = dot(picks, sender_high[:, place]) + dot(picks, sender_low[:, place])
        hidden.append(silu_sum(picked, receivers[:, place], picks.shape[0] // nodes.shape[0]))
    return nodes + gain * normed(dot3(jnp.concatenate(hidden, axis=1), wo_high, wo_low))


def bottom_middle_kernel(rim, head, middle, tail, picks, ws_high, ws_low, wr_high, wr_low, wo_high, wo_low, bias, gains, senders_high, senders_low, receivers, out):
    nodes = jnp.concatenate([head[...], middle[...], tail[...]], axis=0)
    nodes_high, nodes_low = split(nodes)
    width = ws_high.shape[2]
    for g in range(ws_high.shape[0]):
        columns = slice(g * width, (g + 1) * width)
        product = dot(nodes_high, ws_high[g]) + (dot(nodes_high, ws_low[g]) + dot(nodes_low, ws_high[g]))
        senders_high[:, columns], senders_low[:, columns] = split(0.5 * product)
        product = dot(nodes_high, wr_high[g]) + (dot(nodes_high, wr_low[g]) + dot(nodes_low, wr_high[g]))
        receivers[:, columns] = 0.5 * (product + bias[g][0:1])
    total = nodes.shape[0]
    size = picks.shape[0] * rim // total
    for first in range(rim, total - rim, rim):
        place = slice(first, first + rim)
        reach = slice(first - rim, first + 2 * rim)
        out[first - rim : first, :] = bottom_rows(
            middle[first - rim : first], receivers[place], picks[first // rim * size : (first // rim + 1) * size],
            senders_high[reach], senders_low[reach], wo_high[...], wo_low[...], gains[3:4],
        )


def bottom_edge_kernel(rim, before, after, head, tail, inner, picks, senders_high, senders_low, receivers, ws_high, ws_low, wo_high, wo_low, gains, out):
    total = out.shape[0]
    size = picks.shape[0] * rim // total
    out[rim : total - rim, :] = inner[...]
    outer = split(jnp.concatenate([before[...], after[...]], axis=0))
    projected = jnp.concatenate(
        [
            dot(outer[0], ws_high[g]) + (dot(outer[0], ws_low[g]) + dot(outer[1], ws_high[g]))
            for g in range(ws_high.shape[0])
        ],
        axis=1,
    )
    outer_high, outer_low = split(0.5 * projected)
    for side, (nodes, place, reach) in enumerate(
        ((head, slice(0, rim), slice(0, 2 * rim)), (tail, slice(total - rim, total), slice(total - 2 * rim, total)))
    ):
        strip = slice(side * rim, (side + 1) * rim)
        order = (lambda a, b: [a, b]) if side == 0 else (lambda a, b: [b, a])
        high = jnp.concatenate(order(outer_high[strip], senders_high[reach]), axis=0)
        low = jnp.concatenate(order(outer_low[strip], senders_low[reach]), axis=0)
        out[place, :] = bottom_rows(
            nodes[...], receivers[place], picks[place.start // rim * size : (place.start // rim + 1) * size],
            high, low, wo_high[...], wo_low[...], gains[3:4],
        )


whole = pl.BlockSpec(memory_space=pltpu.VMEM)
away = pl.BlockSpec(memory_space=pl.ANY)


def call(kernel, outs, operands, flops, scratch=(), far=(), unread=0, limit=limit_bytes):
    moved = sum(x.size * x.dtype.itemsize for x in (*outs, *operands))
    read = len(operands) - unread
    specs = [away if i in far else whole for i in range(read)] + [away] * unread
    return pl.pallas_call(
        (lambda *refs: kernel(*refs[:read], *refs[read + unread :])) if unread else kernel,
        out_shape=tuple(outs),
        in_specs=specs,
        out_specs=tuple([whole] * len(outs)),
        scratch_shapes=list(scratch),
        compiler_params=pltpu.CompilerParams(vmem_limit_bytes=limit),
        cost_estimate=pl.CostEstimate(flops=int(flops), bytes_accessed=moved, transcendentals=0),
    )(*operands)


def like(shape, kind=f32):
    return jax.ShapeDtypeStruct(tuple(shape), kind)


def shifted(values, axis, step):
    count = lax.axis_size(axis)
    return lax.ppermute(values, axis, [(i, (i + step) % count) for i in range(count)])


def sub_parts(part):
    if lax.axis_size("sub") == 2:
        return [part, shifted(part, "sub", 1)]
    return [lax.psum(part, "sub")]


def coarse_pieces(senders, others):
    patches, lvls = lax.axis_size("patch"), lax.axis_size("lvl")
    if patches > most_direct:
        return [lax.all_gather(senders, ("patch", "lvl"), axis=0, tiled=True)], others
    near = [[senders] + [shifted(senders, "lvl", t) for t in range(1, lvls)]]
    pieces = [shifted(senders, "patch", s) for s in range(1, patches)]
    pieces, others = lax.optimization_barrier((pieces, others))
    near += [[piece] + [shifted(piece, "lvl", t) for t in range(1, lvls)] for piece in pieces]
    return [row[t] for t in range(lvls) for row in near], others


def held(values, event):
    return lax.optimization_barrier((values, event))[0]


def over_sub(pack):
    return [shifted(pack, "sub", s) for s in range(1, lax.axis_size("sub"))]


def partners(axis):
    if axis == "parts":
        return lax.axis_index(axis), lax.axis_size(axis)
    count = 2 if lax.axis_size(axis) % 2 == 0 else 1
    return lax.rem(lax.axis_index(axis), count), count


def over_partners(share_list, axis):
    size, count = lax.axis_size(axis), partners(axis)[1]
    return [
        [
            lax.ppermute(share, axis, [(i, i - i % count + (i + p) % count) for i in range(size)])
            for p in range(1, count)
        ]
        for share in share_list
    ]


def over_lvl(shares):
    return [
        [share] + [shifted(share, "lvl", t) for t in range(1, lax.axis_size("lvl"))]
        for share in shares
    ]


def all_shares(shares, others):
    near = over_lvl(shares)
    far = [over_lvl(row) for row in others]
    return [x for first, row in zip(near, far) for x in (first + [y for group in row for y in group])]


def body(
    node_states,
    coarse_states,
    children,
    down_sources,
    bottom_links,
    coarse_links,
    upward_sender,
    upward_receiver,
    upward_bias,
    upward_output,
    upward_gain,
    coarse_sender,
    coarse_receiver,
    coarse_bias,
    coarse_output,
    coarse_gain,
    downward_sender,
    downward_receiver,
    downward_bias,
    downward_output,
    downward_gain,
    bottom_sender,
    bottom_receiver,
    bottom_bias,
    bottom_output,
    bottom_gain,
):
    rows, latent = node_states.shape
    blocks = coarse_states.shape[0]
    width = upward_sender.shape[1]
    subs = lax.axis_size("sub")
    hidden = width * subs
    rim = rows // 4
    weights = [like((subs, latent, width), bf16)] * 2
    outputs = [like((hidden, latent), bf16)] * 2
    bias_rows = like((subs, 8, width))

    columns = latent // width
    lvls = lax.axis_size("lvl")

    def pack(axis):
        count = shares(axis)[1]
        return like((2 * latent // count + width // count * columns + 8, width))

    (part,) = call(
        upward_kernel,
        [like((blocks, latent))],
        [
            node_states, coarse_states, children.T, upward_sender, upward_receiver,
            upward_bias[None], upward_output,
        ],
        6 * rows * latent * width,
        limit=up_limit,
    )
    parts = sub_parts(part)
    down_own = (downward_sender, downward_receiver, downward_output, downward_bias[None])
    bottom_own = (bottom_sender, bottom_receiver, bottom_output, bottom_bias[None])
    down_pack, bottom_pack = call(
        share_kernel,
        [pack("parts"), pack("patch")],
        [*down_own, *bottom_own],
        latent,
        [pltpu.SemaphoreType.DMA((6 + 2 * columns,))],
        far=range(8),
        limit=share_limit,
    )
    gains, biases = call(
        stack_kernel,
        [like((4, latent)), like((3, width))],
        [
            upward_gain[None], coarse_gain[None], downward_gain[None], bottom_gain[None],
            coarse_bias[None], downward_bias[None], bottom_bias[None], part,
        ],
        latent * hidden,
        unread=1,
    )
    down_near = over_sub(down_pack)
    down_near = held(down_near, parts[-1])
    bottom_near = over_sub(bottom_pack)
    down_far = over_partners(down_near, "parts")
    coarse_up, senders, receivers = call(
        functools.partial(coarse_project_kernel, len(parts)),
        [like((blocks, latent)), like((blocks, width)), like((blocks, width))],
        [*parts, coarse_states, gains, biases, coarse_sender, coarse_receiver],
        12 * blocks * latent * width,
    )
    patches = lax.axis_size("patch")
    names = blocks * patches * lvls
    picks, bottom_picks = call(
        functools.partial(picks_kernel, rim, patches, blocks),
        [like((coarse_links.size, names), bf16), like((bottom_links.size, 3 * rim), bf16)],
        [coarse_links.T, bottom_links.T, senders],
        coarse_links.size * names,
        unread=1,
    )
    pieces, (picks, bottom_picks, down_near, down_far, bottom_near) = coarse_pieces(
        senders, (picks, bottom_picks, down_near, down_far, bottom_near)
    )
    down_packs = all_shares(down_near, down_far)
    bottom_far = over_partners(bottom_near, "patch")
    (part,) = call(
        functools.partial(coarse_kernel, len(pieces)),
        [like((blocks, latent))],
        [*pieces, picks, receivers, coarse_output],
        4 * coarse_links.size * names * width,
    )
    parts = sub_parts(part)
    receivers, ws_high, ws_low, wo_high, wo_low = call(
        functools.partial(down_weights_kernel, len(down_packs)),
        [like((rows, hidden)), *weights, *outputs],
        [node_states, downward_sender, downward_receiver, biases, downward_output, *down_packs, part],
        6 * rows * latent * hidden,
        [pltpu.VMEM((subs, latent, width), bf16)] * 2 + [pltpu.VMEM((subs, 8, width), f32)],
        unread=1,
    )
    new_coarse, senders, head, tail = call(
        functools.partial(down_edge_kernel, len(parts), rim),
        [like((blocks, latent)), like((2 * blocks, hidden), bf16), like((rim, latent)), like((rim, latent))],
        [*parts, coarse_up, gains, node_states, receivers, down_sources.T, ws_high, ws_low, wo_high, wo_low, *(x for row in bottom_far for x in row)],
        6 * 2 * rim * latent * hidden,
        unread=sum(map(len, bottom_far)),
    )
    ring = ("patch", "lvl")
    before, after = shifted(tail, ring, 1), shifted(head, ring, -1)
    (middle,) = call(
        functools.partial(down_middle_kernel, rim),
        [like((rows - 2 * rim, latent))],
        [node_states, receivers, down_sources.T, senders, wo_high, wo_low, gains],
        6 * (rows - 2 * rim) * latent * hidden,
    )

    bottom_near, bottom_far = held((bottom_near, bottom_far), head)
    bottom_packs = all_shares(bottom_near, bottom_far)
    ws_high, ws_low, wr_high, wr_low, wo_high, wo_low, bias = call(
        functools.partial(bottom_weights_kernel, len(bottom_packs)),
        [*weights, *weights, *outputs, bias_rows],
        [bottom_sender, bottom_receiver, biases, bottom_output, *bottom_packs],
        latent * hidden,
    )
    senders_high, senders_low, receivers, inner = call(
        functools.partial(bottom_middle_kernel, rim),
        [like((rows, hidden), bf16), like((rows, hidden), bf16), like((rows, hidden)), like((rows - 2 * rim, latent))],
        [head, middle, tail, bottom_picks, ws_high, ws_low, wr_high, wr_low, wo_high, wo_low, bias, gains],
        (12 * rows + 12 * rows) * latent * hidden,
    )
    (new_nodes,) = call(
        functools.partial(bottom_edge_kernel, rim),
        [like((rows, latent))],
        [before, after, head, tail, inner, bottom_picks, senders_high, senders_low, receivers, ws_high, ws_low, wo_high, wo_low, gains],
        24 * rim * latent * hidden,
    )
    return (new_nodes, new_coarse)


def solution(mesh):
    split_rows, level_rows = P(("parts", "patch", "lvl"), None), P(("patch", "lvl"), None)
    weights = (P(None, "sub"), P(None, "sub"), P("sub"), P("sub", None), P())
    in_specs = (split_rows, split_rows, *([level_rows] * 4), *(weights * 4))
    out_specs = (split_rows, split_rows)
    return jax.shard_map(body, mesh=mesh, in_specs=in_specs, out_specs=out_specs, check_vma=False)
```

```python
import functools

import jax
import jax.numpy as jnp
from jax import lax
from jax.experimental import pallas as pl
from jax.experimental.pallas import tpu as pltpu
from jax.sharding import PartitionSpec as P

epsilon = 1e-05
f32 = jnp.float32
bf16 = jnp.bfloat16
limit_bytes = 12 * 1024 * 1024
share_limit = 58 * 1000 * 1000
up_limit = 50 * 1000 * 1000
most_direct = 4


def split(values):
    high = values.astype(bf16)
    return high, (values - high.astype(f32)).astype(bf16)


def dot(a, b):
    return jnp.dot(a, b, preferred_element_type=f32)


def threefold(values):
    high, low = split(values)
    return jnp.concatenate([high, high, low], axis=1)


def stacked(weights):
    high, low = split(weights)
    return jnp.concatenate([high, low, high], axis=0)


def dot3(a, b_stacked):
    return dot(threefold(a), b_stacked)


def normed(values):
    center = values - jnp.mean(values, axis=-1, keepdims=True)
    spread = jnp.mean(center * center, axis=-1, keepdims=True)
    return center * lax.rsqrt(spread + epsilon)


def upright(rows):
    count, size = rows.shape
    tall, wide = -count % 8, -size % 128
    if tall:
        rows = jnp.concatenate([rows, jnp.zeros((tall, size), rows.dtype)], axis=0)
    if wide:
        rows = jnp.concatenate([rows, jnp.zeros((count + tall, wide), rows.dtype)], axis=1)
    return jnp.transpose(rows)[:size, :count]


def one_hot(wanted, names):
    return jnp.concatenate(
        [
            jnp.where(wanted[:, k : k + 1] == names, 1.0, 0.0).astype(bf16)
            for k in range(wanted.shape[1])
        ],
        axis=0,
    )


def silu_sum(picked, halves, count):
    rows = halves.shape[0]
    total = None
    for k in range(count):
        u = picked[k * rows : (k + 1) * rows] + halves
        term = u + u * jnp.tanh(u)
        total = term if total is None else total + term
    return total


def added(refs):
    total = refs[0][...]
    for ref in refs[1:]:
        total = total + ref[...]
    return total


def started(copies, sems):
    moves = [pltpu.make_async_copy(a, b, sems.at[i]) for i, (a, b) in enumerate(copies)]
    for move in moves:
        move.start()
    return moves


def upward_kernel(nodes, coarse, children, ws, wr, bias, wo, part):
    wanted = upright(children[...])
    names = lax.broadcasted_iota(jnp.int32, (wanted.shape[0], nodes.shape[0]), 1)
    picks = one_hot(wanted, names)
    senders = jnp.concatenate(split(0.5 * dot3(nodes[...], stacked(ws[...]))), axis=0)
    receivers = 0.5 * (dot3(coarse[...], stacked(wr[...])) + bias[...])
    picked = dot(jnp.concatenate([picks, picks], axis=1), senders)
    hidden = silu_sum(picked, receivers, wanted.shape[1])
    part[...] = dot3(hidden, stacked(wo[...]))


def stack_kernel(*refs):
    params, (gains, biases) = refs[:7], refs[7:]
    for i in range(4):
        gains[i : i + 1] = params[i][...]
    for i in range(3):
        biases[i : i + 1] = params[4 + i][...]


def share_kernel(*refs):
    down_own, bottom_own, (down_pack, bottom_pack, sems) = refs[:4], refs[4:8], refs[8:]
    copies = share_copies(down_own, down_pack, "parts") + share_copies(bottom_own, bottom_pack, "patch")
    for move in started(copies, sems):
        move.wait()


def shares(axis):
    lvls = lax.axis_size("lvl")
    place, count = partners(axis)
    return place * lvls + lax.axis_index("lvl"), count * lvls


def share_copies(sources, pack, axis):
    mine, count = shares(axis)
    width = pack.shape[1]
    copies, at = [], 0
    for source in sources:
        rows = source.shape[0] // count
        if source.shape[0] == 1:
            copies.append((source, pack.at[pl.ds(at, 1)]))
            at += 8
            continue
        strip = pl.ds(pl.multiple_of(mine * rows, rows), rows)
        for j in range(source.shape[1] // width):
            copies.append((source.at[strip, pl.ds(j * width, width)], pack.at[pl.ds(at, rows)]))
            at += rows
    return copies


def picks_kernel(rim, patches, blocks, coarse_links, bottom_links, coarse_picks, bottom_picks):
    wanted = upright(coarse_links[...])
    rows = wanted.shape[0]
    lvls = lax.axis_size("lvl")
    half = coarse_picks.shape[1] // 2
    column = lax.broadcasted_iota(jnp.int32, (rows, blocks), 1)
    for t in range(lvls):
        for s in range(patches):
            patch = lax.rem(lax.axis_index("patch") + patches - s, patches)
            lvl = lax.rem(lax.axis_index("lvl") + lvls - t, lvls)
            first = (patch * lvls + lvl) * blocks
            at = (t * patches + s) * blocks
            piece = one_hot(wanted, column + first)
            coarse_picks[:, at : at + blocks] = piece
            coarse_picks[:, half + at : half + at + blocks] = piece
    wanted = upright(bottom_links[...])
    size = rim * wanted.shape[1]
    names = lax.broadcasted_iota(jnp.int32, (rim, 3 * rim), 1)
    for i in range(wanted.shape[0] // rim):
        picks = one_hot(wanted[i * rim : (i + 1) * rim], names + i * rim)
        for j in range(6):
            piece = picks[:, j // 2 * rim : (j // 2 + 1) * rim]
            bottom_picks[i * size : (i + 1) * size, j * rim : (j + 1) * rim] = piece


def coarse_project_kernel(count, *refs):
    parts, refs = refs[:count], refs[count:]
    coarse, gains, biases, ws, wr, updated, senders, receivers = refs
    rows = coarse[...] + gains[0:1] * normed(added(parts))
    updated[...] = rows
    senders[...] = 0.5 * dot3(rows, stacked(ws[...]))
    receivers[...] = 0.5 * (dot3(rows, stacked(wr[...])) + biases[0:1])


def coarse_kernel(count, *refs):
    pieces, (all_picks, receivers, wo) = refs[:count], refs[count : count + 3]
    part = refs[-1]
    senders = jnp.concatenate([piece[...] for piece in pieces], axis=0)
    picked = dot(all_picks[...], jnp.concatenate(split(senders), axis=0))
    hidden = silu_sum(picked, receivers[...], all_picks.shape[0] // receivers.shape[0])
    part[...] = dot3(hidden, stacked(wo[...]))


def fetched_shares(packs, axis):
    subs, lvls = lax.axis_size("sub"), lax.axis_size("lvl")
    sub, lvl = lax.axis_index("sub"), lax.axis_index("lvl")
    place, count = partners(axis)
    left = iter(packs)
    for s in range(1, subs):
        for p in range(count):
            for t in range(lvls):
                mine = lax.rem(place + count - p, count) * lvls + lax.rem(lvl + lvls - t, lvls)
                yield next(left), lax.rem(sub + subs - s, subs), mine, p == 0 and t == 0


def put_stacked(values, out, first, columns):
    high, low = split(values)
    depth, rows = out.shape[0] // 3, values.shape[0]
    for i, half in enumerate((high, low, high)):
        out[pl.ds(pl.multiple_of(i * depth + first, 16), rows), columns] = half


def collect_in(own, packs, axis, at, out):
    everything = slice(0, own.shape[1])
    put_stacked(own[...], out.at[lax.axis_index("sub")], 0, everything)
    share = own.shape[0] // shares(axis)[1]
    for pack, block, mine, _ in fetched_shares(packs, axis):
        put_stacked(pack[at : at + share, :], out.at[block], mine * share, everything)


def collect_out(own, packs, axis, at, out):
    width, latent = own.shape
    put_stacked(own[...], out, lax.axis_index("sub") * width, slice(0, latent))
    thin = width // shares(axis)[1]
    for pack, block, mine, _ in fetched_shares(packs, axis):
        for j in range(latent // width):
            part = pack[at + j * thin : at + (j + 1) * thin, :]
            put_stacked(part, out, block * width + mine * thin, slice(j * width, (j + 1) * width))


def collect_bias(own, packs, axis, at, out):
    out[lax.axis_index("sub")] = jnp.broadcast_to(own, (8, own.shape[1]))
    for pack, block, _, whole_row in fetched_shares(packs, axis):
        if whole_row:
            out[block] = jnp.broadcast_to(pack[at : at + 1, :], (8, own.shape[1]))


def down_weights_kernel(count, nodes, ws, wr, biases, wo, *refs):
    packs, (receivers, ws_all, wo_all, wr_all, bias_all) = refs[:count], refs[count:]
    width = ws.shape[1]
    share = ws.shape[0] // shares("parts")[1]
    collect_in(ws, packs, "parts", 0, ws_all)
    collect_in(wr, packs, "parts", share, wr_all)
    collect_out(wo, packs, "parts", 2 * share, wo_all)
    collect_bias(biases[1:2], packs, "parts", 3 * share, bias_all)
    states = threefold(nodes[...])
    for g in range(wr_all.shape[0]):
        receivers[:, g * width : (g + 1) * width] = 0.5 * (dot(states, wr_all[g]) + bias_all[g][0:1])


def bottom_weights_kernel(count, ws, wr, biases, wo, *refs):
    packs, (ws_all, wr_all, wo_all, bias_all) = refs[:count], refs[count:]
    share = ws.shape[0] // shares("patch")[1]
    collect_in(ws, packs, "patch", 0, ws_all)
    collect_in(wr, packs, "patch", share, wr_all)
    collect_out(wo, packs, "patch", 2 * share, wo_all)
    collect_bias(biases[2:3], packs, "patch", 3 * share, bias_all)


def down_rows(nodes, receivers, sources, senders, wo, gain):
    blocks = senders.shape[0] // 2
    column = lax.broadcasted_iota(jnp.int32, (nodes.shape[0], 2 * blocks), 1)
    names = jnp.where(column < blocks, column, column - blocks)
    picked = dot(one_hot(sources, names), senders)
    hidden = silu_sum(picked, receivers, sources.shape[1])
    return nodes + gain * normed(dot3(hidden, wo))


def down_edge_kernel(count, rim, *refs):
    parts, refs = refs[:count], refs[count:]
    coarse_up, gains, nodes, receivers, sources, ws, wo = refs[:7]
    new_coarse, senders, head, tail, held_here, sem = refs[7:]
    rows = coarse_up[...] + gains[1:2] * normed(added(parts))
    held_here[...] = rows
    move = pltpu.make_async_copy(held_here, new_coarse, sem)
    move.start()
    blocks = rows.shape[0]
    width = ws.shape[2]
    left = threefold(rows)
    for g in range(ws.shape[0]):
        columns = slice(g * width, (g + 1) * width)
        high, low = split(0.5 * dot(left, ws[g]))
        senders[0:blocks, columns] = high
        senders[blocks : 2 * blocks, columns] = low
    total = nodes.shape[0]
    wanted = upright(sources[...])
    for out, place in ((head, slice(0, rim)), (tail, slice(total - rim, total))):
        out[...] = down_rows(
            nodes[place], receivers[place], wanted[place], senders[...], wo[...], gains[2:3]
        )
    move.wait()


def down_middle_kernel(rim, nodes, receivers, sources, senders, wo, gains, middle):
    place = slice(rim, nodes.shape[0] - rim)
    middle[...] = down_rows(
        nodes[place], receivers[place], upright(sources[...])[place], senders[...], wo[...], gains[2:3]
    )


def bottom_rows(nodes, receivers, picks, senders, wo, gain):
    half = senders.shape[1] // 2
    hidden = []
    for place in (slice(0, half), slice(half, 2 * half)):
        picked = dot(picks, senders[:, place])
        hidden.append(silu_sum(picked, receivers[:, place], picks.shape[0] // nodes.shape[0]))
    return nodes + gain * normed(dot3(jnp.concatenate(hidden, axis=1), wo))


def put_strips(values, rim, out, columns):
    high, low = split(values)
    for i in range(values.shape[0] // rim):
        strip = slice(i * rim, (i + 1) * rim)
        out[2 * i * rim : (2 * i + 1) * rim, columns] = high[strip]
        out[(2 * i + 1) * rim : (2 * i + 2) * rim, columns] = low[strip]


def bottom_middle_kernel(rim, head, middle, tail, picks, ws, wr, wo, bias, gains, senders, receivers, out):
    nodes = jnp.concatenate([head[...], middle[...], tail[...]], axis=0)
    left = threefold(nodes)
    width = ws.shape[2]
    for g in range(ws.shape[0]):
        columns = slice(g * width, (g + 1) * width)
        put_strips(0.5 * dot(left, ws[g]), rim, senders, columns)
        receivers[:, columns] = 0.5 * (dot(left, wr[g]) + bias[g][0:1])
    total = nodes.shape[0]
    size = picks.shape[0] * rim // total
    for i in range(1, total // rim - 1):
        place = slice(i * rim, (i + 1) * rim)
        inner = slice((i - 1) * rim, i * rim)
        out[inner, :] = bottom_rows(
            middle[inner], receivers[place], picks[i * size : (i + 1) * size],
            senders[2 * (i - 1) * rim : 2 * (i + 2) * rim, :], wo[...], gains[3:4],
        )


def bottom_edge_kernel(rim, before, after, head, tail, inner, picks, senders, receivers, ws, wo, gains, out, outer, strips, sems):
    total = receivers.shape[0]
    size = picks.shape[0] * rim // total
    moves = [pltpu.make_async_copy(inner, out.at[pl.ds(rim, total - 2 * rim)], sems.at[0])]
    moves[0].start()
    left = threefold(jnp.concatenate([before[...], after[...]], axis=0))
    width = ws.shape[2]
    for g in range(ws.shape[0]):
        put_strips(0.5 * dot(left, ws[g]), rim, outer, slice(g * width, (g + 1) * width))
    near = senders.shape[0]
    for side, nodes in enumerate((head, tail)):
        first = 0 if side == 0 else total - rim
        place = slice(first, first + rim)
        beyond = outer[2 * side * rim : 2 * (side + 1) * rim, :]
        reach = (
            [beyond, senders[0 : 4 * rim, :]]
            if side == 0
            else [senders[near - 4 * rim : near, :], beyond]
        )
        strips[side * rim : (side + 1) * rim, :] = bottom_rows(
            nodes[...], receivers[place], picks[first // rim * size : (first // rim + 1) * size],
            jnp.concatenate(reach, axis=0), wo[...], gains[3:4],
        )
        strip = strips.at[pl.ds(side * rim, rim)]
        moves.append(pltpu.make_async_copy(strip, out.at[pl.ds(first, rim)], sems.at[1 + side]))
        moves[-1].start()
    for move in moves:
        move.wait()


whole = pl.BlockSpec(memory_space=pltpu.VMEM)
away = pl.BlockSpec(memory_space=pl.ANY)


def call(kernel, outs, operands, flops, scratch=(), far=(), far_outs=(), unread=0, limit=limit_bytes):
    moved = sum(x.size * x.dtype.itemsize for x in (*outs, *operands))
    read = len(operands) - unread
    specs = [away if i in far else whole for i in range(read)] + [away] * unread
    return pl.pallas_call(
        (lambda *refs: kernel(*refs[:read], *refs[read + unread :])) if unread else kernel,
        out_shape=tuple(outs),
        in_specs=specs,
        out_specs=tuple(away if i in far_outs else whole for i in range(len(outs))),
        scratch_shapes=list(scratch),
        compiler_params=pltpu.CompilerParams(vmem_limit_bytes=limit),
        cost_estimate=pl.CostEstimate(flops=int(flops), bytes_accessed=moved, transcendentals=0),
    )(*operands)


def like(shape, kind=f32):
    return jax.ShapeDtypeStruct(tuple(shape), kind)


def shifted(values, axis, step):
    count = lax.axis_size(axis)
    return lax.ppermute(values, axis, [(i, (i + step) % count) for i in range(count)])


def sub_parts(part):
    if lax.axis_size("sub") == 2:
        return [part, shifted(part, "sub", 1)]
    return [lax.psum(part, "sub")]


def coarse_pieces(senders, others):
    patches, lvls = lax.axis_size("patch"), lax.axis_size("lvl")
    if patches > most_direct:
        return [lax.all_gather(senders, ("patch", "lvl"), axis=0, tiled=True)], others
    near = [[senders] + [shifted(senders, "lvl", t) for t in range(1, lvls)]]
    pieces = [shifted(senders, "patch", s) for s in range(1, patches)]
    pieces, others = lax.optimization_barrier((pieces, others))
    near += [[piece] + [shifted(piece, "lvl", t) for t in range(1, lvls)] for piece in pieces]
    return [row[t] for t in range(lvls) for row in near], others


def held(values, event):
    return lax.optimization_barrier((values, event))[0]


def over_sub(pack):
    return [shifted(pack, "sub", s) for s in range(1, lax.axis_size("sub"))]


def partners(axis):
    if axis == "parts":
        return lax.axis_index(axis), lax.axis_size(axis)
    count = 2 if lax.axis_size(axis) % 2 == 0 else 1
    return lax.rem(lax.axis_index(axis), count), count


def over_partners(share_list, axis):
    size, count = lax.axis_size(axis), partners(axis)[1]
    return [
        [
            lax.ppermute(share, axis, [(i, i - i % count + (i + p) % count) for i in range(size)])
            for p in range(1, count)
        ]
        for share in share_list
    ]


def over_lvl(shares):
    return [
        [share] + [shifted(share, "lvl", t) for t in range(1, lax.axis_size("lvl"))]
        for share in shares
    ]


def all_shares(shares, others):
    near = over_lvl(shares)
    far = [over_lvl(row) for row in others]
    return [x for first, row in zip(near, far) for x in (first + [y for group in row for y in group])]


def body(
    node_states,
    coarse_states,
    children,
    down_sources,
    bottom_links,
    coarse_links,
    upward_sender,
    upward_receiver,
    upward_bias,
    upward_output,
    upward_gain,
    coarse_sender,
    coarse_receiver,
    coarse_bias,
    coarse_output,
    coarse_gain,
    downward_sender,
    downward_receiver,
    downward_bias,
    downward_output,
    downward_gain,
    bottom_sender,
    bottom_receiver,
    bottom_bias,
    bottom_output,
    bottom_gain,
):
    rows, latent = node_states.shape
    blocks = coarse_states.shape[0]
    width = upward_sender.shape[1]
    subs = lax.axis_size("sub")
    hidden = width * subs
    rim = rows // 4
    into = like((subs, 3 * latent, width), bf16)
    out_of = like((3 * hidden, latent), bf16)
    bias_rows = like((subs, 8, width))

    columns = latent // width
    lvls = lax.axis_size("lvl")

    def pack(axis):
        count = shares(axis)[1]
        return like((2 * latent // count + width // count * columns + 8, width))

    (part,) = call(
        upward_kernel,
        [like((blocks, latent))],
        [
            node_states, coarse_states, children.T, upward_sender, upward_receiver,
            upward_bias[None], upward_output,
        ],
        6 * rows * latent * width,
        limit=up_limit,
    )
    parts = sub_parts(part)
    down_own = (downward_sender, downward_receiver, downward_output, downward_bias[None])
    bottom_own = (bottom_sender, bottom_receiver, bottom_output, bottom_bias[None])
    down_pack, bottom_pack = call(
        share_kernel,
        [pack("parts"), pack("patch")],
        [*down_own, *bottom_own],
        latent,
        [pltpu.SemaphoreType.DMA((6 + 2 * columns,))],
        far=range(8),
        limit=share_limit,
    )
    gains, biases = call(
        stack_kernel,
        [like((4, latent)), like((3, width))],
        [
            upward_gain[None], coarse_gain[None], downward_gain[None], bottom_gain[None],
            coarse_bias[None], downward_bias[None], bottom_bias[None], part,
        ],
        latent * hidden,
        unread=1,
    )
    down_near = over_sub(down_pack)
    down_near = held(down_near, parts[-1])
    bottom_near = over_sub(bottom_pack)
    down_far = over_partners(down_near, "parts")
    coarse_up, senders, receivers = call(
        functools.partial(coarse_project_kernel, len(parts)),
        [like((blocks, latent)), like((blocks, width)), like((blocks, width))],
        [*parts, coarse_states, gains, biases, coarse_sender, coarse_receiver],
        12 * blocks * latent * width,
    )
    patches = lax.axis_size("patch")
    names = blocks * patches * lvls
    picks, bottom_picks = call(
        functools.partial(picks_kernel, rim, patches, blocks),
        [like((coarse_links.size, 2 * names), bf16), like((bottom_links.size, 6 * rim), bf16)],
        [coarse_links.T, bottom_links.T, senders],
        coarse_links.size * names,
        unread=1,
    )
    pieces, (picks, bottom_picks, down_near, down_far, bottom_near) = coarse_pieces(
        senders, (picks, bottom_picks, down_near, down_far, bottom_near)
    )
    down_packs = all_shares(down_near, down_far)
    bottom_far = over_partners(bottom_near, "patch")
    (part,) = call(
        functools.partial(coarse_kernel, len(pieces)),
        [like((blocks, latent))],
        [*pieces, picks, receivers, coarse_output],
        4 * coarse_links.size * names * width,
    )
    parts = sub_parts(part)
    receivers, ws, wo = call(
        functools.partial(down_weights_kernel, len(down_packs)),
        [like((rows, hidden)), into, out_of],
        [node_states, downward_sender, downward_receiver, biases, downward_output, *down_packs, part],
        6 * rows * latent * hidden,
        [pltpu.VMEM((subs, 3 * latent, width), bf16), pltpu.VMEM((subs, 8, width), f32)],
        unread=1,
    )
    new_coarse, senders, head, tail = call(
        functools.partial(down_edge_kernel, len(parts), rim),
        [like((blocks, latent)), like((2 * blocks, hidden), bf16), like((rim, latent)), like((rim, latent))],
        [*parts, coarse_up, gains, node_states, receivers, down_sources.T, ws, wo],
        6 * 2 * rim * latent * hidden,
        [pltpu.VMEM((blocks, latent), f32), pltpu.SemaphoreType.DMA],
        far_outs=(0,),
    )
    ring = ("patch", "lvl")
    before, after = shifted(tail, ring, 1), shifted(head, ring, -1)
    (middle,) = call(
        functools.partial(down_middle_kernel, rim),
        [like((rows - 2 * rim, latent))],
        [node_states, receivers, down_sources.T, senders, wo, gains],
        6 * (rows - 2 * rim) * latent * hidden,
    )

    bottom_near, bottom_far = held((bottom_near, bottom_far), head)
    bottom_packs = all_shares(bottom_near, bottom_far)
    ws, wr, wo, bias = call(
        functools.partial(bottom_weights_kernel, len(bottom_packs)),
        [into, into, out_of, bias_rows],
        [bottom_sender, bottom_receiver, biases, bottom_output, *bottom_packs],
        latent * hidden,
    )
    senders, receivers, inner = call(
        functools.partial(bottom_middle_kernel, rim),
        [like((2 * rows, hidden), bf16), like((rows, hidden)), like((rows - 2 * rim, latent))],
        [head, middle, tail, bottom_picks, ws, wr, wo, bias, gains],
        (12 * rows + 12 * rows) * latent * hidden,
    )
    (new_nodes,) = call(
        functools.partial(bottom_edge_kernel, rim),
        [like((rows, latent))],
        [before, after, head, tail, inner, bottom_picks, senders, receivers, ws, wo, gains],
        24 * rim * latent * hidden,
        [
            pltpu.VMEM((4 * rim, hidden), bf16),
            pltpu.VMEM((2 * rim, latent), f32),
            pltpu.SemaphoreType.DMA((3,)),
        ],
        far_outs=(0,),
    )
    return (new_nodes, new_coarse)


def solution(mesh):
    split_rows, level_rows = P(("parts", "patch", "lvl"), None), P(("patch", "lvl"), None)
    weights = (P(None, "sub"), P(None, "sub"), P("sub"), P("sub", None), P())
    in_specs = (split_rows, split_rows, *([level_rows] * 4), *(weights * 4))
    out_specs = (split_rows, split_rows)
    return jax.shard_map(body, mesh=mesh, in_specs=in_specs, out_specs=out_specs, check_vma=False)
```

```python
import functools

import jax
import jax.numpy as jnp
from jax import lax
from jax.experimental import pallas as pl
from jax.experimental.pallas import tpu as pltpu
from jax.sharding import PartitionSpec as P

epsilon = 1e-05
f32 = jnp.float32
bf16 = jnp.bfloat16
limit_bytes = 12 * 1024 * 1024
tight_limit = 64 * 1000 * 1000
most_direct = 4


def split(values):
    high = values.astype(bf16)
    return high, (values - high.astype(f32)).astype(bf16)


def dot(a, b):
    return jnp.dot(a, b, preferred_element_type=f32)


def threefold(values):
    high, low = split(values)
    return jnp.concatenate([high, high, low], axis=1)


def stacked(weights):
    high, low = split(weights)
    return jnp.concatenate([high, low, high], axis=0)


def dot3(a, b_stacked):
    return dot(threefold(a), b_stacked)


def normed(values):
    center = values - jnp.mean(values, axis=-1, keepdims=True)
    spread = jnp.mean(center * center, axis=-1, keepdims=True)
    return center * lax.rsqrt(spread + epsilon)


def upright(rows):
    count, size = rows.shape
    tall, wide = -count % 8, -size % 128
    if tall:
        rows = jnp.concatenate([rows, jnp.zeros((tall, size), rows.dtype)], axis=0)
    if wide:
        rows = jnp.concatenate([rows, jnp.zeros((count + tall, wide), rows.dtype)], axis=1)
    return jnp.transpose(rows)[:size, :count]


def one_hot(wanted, names):
    return jnp.concatenate(
        [
            jnp.where(wanted[:, k : k + 1] == names, 1.0, 0.0).astype(bf16)
            for k in range(wanted.shape[1])
        ],
        axis=0,
    )


def silu_sum(picked, halves, count):
    rows = halves.shape[0]
    total = None
    for k in range(count):
        u = picked[k * rows : (k + 1) * rows] + halves
        term = u + u * jnp.tanh(u)
        total = term if total is None else total + term
    return total


def added(refs):
    total = refs[0][...]
    for ref in refs[1:]:
        total = total + ref[...]
    return total


def started(copies, sems):
    moves = [pltpu.make_async_copy(a, b, sems.at[i]) for i, (a, b) in enumerate(copies)]
    for move in moves:
        move.start()
    return moves


def strips(source, target, count):
    rows = source.shape[0] // count
    return [
        (source.at[pl.ds(i * rows, rows)], target.at[pl.ds(i * rows, rows)]) for i in range(count)
    ]


def upward_kernel(nodes_hbm, coarse_hbm, ws_hbm, wr_hbm, wo_hbm, children, bias, part, nodes, coarse, ws, wr, wo, senders, sems):
    cuts = 4
    moves = started(
        strips(ws_hbm, ws, cuts)
        + strips(nodes_hbm, nodes, cuts)
        + [(coarse_hbm, coarse)]
        + strips(wr_hbm, wr, cuts)
        + strips(wo_hbm, wo, cuts),
        sems,
    )
    wanted = upright(children[...])
    names = lax.broadcasted_iota(jnp.int32, (wanted.shape[0], nodes.shape[0]), 1)
    picks = one_hot(wanted, names)
    picks = jnp.concatenate([picks, picks], axis=1)
    for move in moves[:cuts]:
        move.wait()
    ws_stacked = stacked(ws[...])
    rows, total = nodes.shape[0] // cuts, nodes.shape[0]
    for i in range(cuts):
        moves[cuts + i].wait()
        first, last = i * rows, (i + 1) * rows
        high, low = split(0.5 * dot3(nodes[first:last], ws_stacked))
        senders[first:last] = high
        senders[total + first : total + last] = low
    for move in moves[2 * cuts : 3 * cuts + 1]:
        move.wait()
    receivers = 0.5 * (dot3(coarse[...], stacked(wr[...])) + bias[...])
    hidden = silu_sum(dot(picks, senders[...]), receivers, wanted.shape[1])
    for move in moves[3 * cuts + 1 :]:
        move.wait()
    part[...] = dot3(hidden, stacked(wo[...]))


def stack_kernel(*refs):
    params, (gains, biases) = refs[:7], refs[7:]
    for i in range(4):
        gains[i : i + 1] = params[i][...]
    for i in range(3):
        biases[i : i + 1] = params[4 + i][...]


def share_kernel(*refs):
    down_own, bottom_own, (down_pack, bottom_pack, sems) = refs[:4], refs[4:8], refs[8:]
    copies = share_copies(down_own, down_pack, "parts") + share_copies(bottom_own, bottom_pack, "patch")
    for move in started(copies, sems):
        move.wait()


def shares(axis):
    lvls = lax.axis_size("lvl")
    place, count = partners(axis)
    return place * lvls + lax.axis_index("lvl"), count * lvls


def share_copies(sources, pack, axis):
    mine, count = shares(axis)
    width = pack.shape[1]
    copies, at = [], 0
    for source in sources:
        rows = source.shape[0] // count
        if source.shape[0] == 1:
            copies.append((source, pack.at[pl.ds(at, 1)]))
            at += 8
            continue
        strip = pl.ds(pl.multiple_of(mine * rows, rows), rows)
        for j in range(source.shape[1] // width):
            copies.append((source.at[strip, pl.ds(j * width, width)], pack.at[pl.ds(at, rows)]))
            at += rows
    return copies


def picks_kernel(rim, patches, blocks, coarse_links, bottom_links, coarse_picks, bottom_picks):
    wanted = upright(coarse_links[...])
    rows = wanted.shape[0]
    lvls = lax.axis_size("lvl")
    half = coarse_picks.shape[1] // 2
    column = lax.broadcasted_iota(jnp.int32, (rows, blocks), 1)
    for t in range(lvls):
        for s in range(patches):
            patch = lax.rem(lax.axis_index("patch") + patches - s, patches)
            lvl = lax.rem(lax.axis_index("lvl") + lvls - t, lvls)
            first = (patch * lvls + lvl) * blocks
            at = (t * patches + s) * blocks
            piece = one_hot(wanted, column + first)
            coarse_picks[:, at : at + blocks] = piece
            coarse_picks[:, half + at : half + at + blocks] = piece
    wanted = upright(bottom_links[...])
    size = rim * wanted.shape[1]
    names = lax.broadcasted_iota(jnp.int32, (rim, 3 * rim), 1)
    for i in range(wanted.shape[0] // rim):
        picks = one_hot(wanted[i * rim : (i + 1) * rim], names + i * rim)
        for j in range(6):
            piece = picks[:, j // 2 * rim : (j // 2 + 1) * rim]
            bottom_picks[i * size : (i + 1) * size, j * rim : (j + 1) * rim] = piece


def coarse_project_kernel(count, *refs):
    parts, refs = refs[:count], refs[count:]
    coarse, gains, biases, ws, wr, updated, senders, receivers = refs
    rows = coarse[...] + gains[0:1] * normed(added(parts))
    updated[...] = rows
    senders[...] = 0.5 * dot3(rows, stacked(ws[...]))
    receivers[...] = 0.5 * (dot3(rows, stacked(wr[...])) + biases[0:1])


def coarse_kernel(count, *refs):
    pieces, (all_picks, receivers, wo) = refs[:count], refs[count : count + 3]
    part = refs[-1]
    senders = jnp.concatenate([piece[...] for piece in pieces], axis=0)
    picked = dot(all_picks[...], jnp.concatenate(split(senders), axis=0))
    hidden = silu_sum(picked, receivers[...], all_picks.shape[0] // receivers.shape[0])
    part[...] = dot3(hidden, stacked(wo[...]))


def fetched_shares(packs, axis):
    subs, lvls = lax.axis_size("sub"), lax.axis_size("lvl")
    sub, lvl = lax.axis_index("sub"), lax.axis_index("lvl")
    place, count = partners(axis)
    left = iter(packs)
    for s in range(1, subs):
        for p in range(count):
            for t in range(lvls):
                mine = lax.rem(place + count - p, count) * lvls + lax.rem(lvl + lvls - t, lvls)
                yield next(left), lax.rem(sub + subs - s, subs), mine, p == 0 and t == 0


def put_stacked(values, out, first, columns):
    high, low = split(values)
    depth, rows = out.shape[0] // 3, values.shape[0]
    for i, half in enumerate((high, low, high)):
        out[pl.ds(pl.multiple_of(i * depth + first, 16), rows), columns] = half


def collect_in(own, packs, axis, at, out):
    everything = slice(0, own.shape[1])
    put_stacked(own[...], out.at[lax.axis_index("sub")], 0, everything)
    share = own.shape[0] // shares(axis)[1]
    for pack, block, mine, _ in fetched_shares(packs, axis):
        put_stacked(pack[at : at + share, :], out.at[block], mine * share, everything)


def collect_out(own, packs, axis, at, out):
    width, latent = own.shape
    put_stacked(own[...], out, lax.axis_index("sub") * width, slice(0, latent))
    thin = width // shares(axis)[1]
    for pack, block, mine, _ in fetched_shares(packs, axis):
        for j in range(latent // width):
            part = pack[at + j * thin : at + (j + 1) * thin, :]
            put_stacked(part, out, block * width + mine * thin, slice(j * width, (j + 1) * width))


def collect_bias(own, packs, axis, at, out):
    out[lax.axis_index("sub")] = jnp.broadcast_to(own, (8, own.shape[1]))
    for pack, block, _, whole_row in fetched_shares(packs, axis):
        if whole_row:
            out[block] = jnp.broadcast_to(pack[at : at + 1, :], (8, own.shape[1]))


def down_weights_kernel(count, nodes, ws, wr, biases, wo, *refs):
    packs, (receivers, ws_all, wo_all, wr_all, bias_all) = refs[:count], refs[count:]
    width = ws.shape[1]
    share = ws.shape[0] // shares("parts")[1]
    collect_in(ws, packs, "parts", 0, ws_all)
    collect_in(wr, packs, "parts", share, wr_all)
    collect_out(wo, packs, "parts", 2 * share, wo_all)
    collect_bias(biases[1:2], packs, "parts", 3 * share, bias_all)
    states = threefold(nodes[...])
    for g in range(wr_all.shape[0]):
        receivers[:, g * width : (g + 1) * width] = 0.5 * (dot(states, wr_all[g]) + bias_all[g][0:1])


def bottom_weights_kernel(count, ws, wr, biases, wo, *refs):
    packs, (ws_all, wr_all, wo_all, bias_all) = refs[:count], refs[count:]
    share = ws.shape[0] // shares("patch")[1]
    collect_in(ws, packs, "patch", 0, ws_all)
    collect_in(wr, packs, "patch", share, wr_all)
    collect_out(wo, packs, "patch", 2 * share, wo_all)
    collect_bias(biases[2:3], packs, "patch", 3 * share, bias_all)


def down_rows(nodes, receivers, sources, senders, wo, gain):
    blocks = senders.shape[0] // 2
    column = lax.broadcasted_iota(jnp.int32, (nodes.shape[0], 2 * blocks), 1)
    names = jnp.where(column < blocks, column, column - blocks)
    picked = dot(one_hot(sources, names), senders)
    hidden = silu_sum(picked, receivers, sources.shape[1])
    return nodes + gain * normed(dot3(hidden, wo))


def down_edge_kernel(count, rim, *refs):
    parts, refs = refs[:count], refs[count:]
    coarse_up, gains, nodes, receivers, sources, ws, wo = refs[:7]
    new_coarse, senders, head, tail, held_here, sem = refs[7:]
    rows = coarse_up[...] + gains[1:2] * normed(added(parts))
    held_here[...] = rows
    move = pltpu.make_async_copy(held_here, new_coarse, sem)
    move.start()
    blocks = rows.shape[0]
    width = ws.shape[2]
    left = threefold(rows)
    for g in range(ws.shape[0]):
        columns = slice(g * width, (g + 1) * width)
        high, low = split(0.5 * dot(left, ws[g]))
        senders[0:blocks, columns] = high
        senders[blocks : 2 * blocks, columns] = low
    total = nodes.shape[0]
    wanted = upright(sources[...])
    for out, place in ((head, slice(0, rim)), (tail, slice(total - rim, total))):
        out[...] = down_rows(
            nodes[place], receivers[place], wanted[place], senders[...], wo[...], gains[2:3]
        )
    move.wait()


def down_middle_kernel(rim, nodes, receivers, sources, senders, wo, gains, middle):
    place = slice(rim, nodes.shape[0] - rim)
    middle[...] = down_rows(
        nodes[place], receivers[place], upright(sources[...])[place], senders[...], wo[...], gains[2:3]
    )


def bottom_rows(nodes, receivers, picks, senders, wo, gain):
    half = senders.shape[1] // 2
    hidden = []
    for place in (slice(0, half), slice(half, 2 * half)):
        picked = dot(picks, senders[:, place])
        hidden.append(silu_sum(picked, receivers[:, place], picks.shape[0] // nodes.shape[0]))
    return nodes + gain * normed(dot3(jnp.concatenate(hidden, axis=1), wo))


def put_strips(values, rim, out, columns):
    high, low = split(values)
    for i in range(values.shape[0] // rim):
        strip = slice(i * rim, (i + 1) * rim)
        out[2 * i * rim : (2 * i + 1) * rim, columns] = high[strip]
        out[(2 * i + 1) * rim : (2 * i + 2) * rim, columns] = low[strip]


def bottom_middle_kernel(rim, head, middle, tail, picks, ws, wr, wo, bias, gains, senders, receivers, out):
    nodes = jnp.concatenate([head[...], middle[...], tail[...]], axis=0)
    left = threefold(nodes)
    width = ws.shape[2]
    for g in range(ws.shape[0]):
        columns = slice(g * width, (g + 1) * width)
        put_strips(0.5 * dot(left, ws[g]), rim, senders, columns)
        receivers[:, columns] = 0.5 * (dot(left, wr[g]) + bias[g][0:1])
    total = nodes.shape[0]
    size = picks.shape[0] * rim // total
    for i in range(1, total // rim - 1):
        place = slice(i * rim, (i + 1) * rim)
        inner = slice((i - 1) * rim, i * rim)
        out[inner, :] = bottom_rows(
            middle[inner], receivers[place], picks[i * size : (i + 1) * size],
            senders[2 * (i - 1) * rim : 2 * (i + 2) * rim, :], wo[...], gains[3:4],
        )


def bottom_edge_kernel(rim, before, after, head, tail, inner, picks, senders, receivers, ws, wo, gains, out, outer, strips, sems):
    total = receivers.shape[0]
    size = picks.shape[0] * rim // total
    moves = [pltpu.make_async_copy(inner, out.at[pl.ds(rim, total - 2 * rim)], sems.at[0])]
    moves[0].start()
    left = threefold(jnp.concatenate([before[...], after[...]], axis=0))
    width = ws.shape[2]
    for g in range(ws.shape[0]):
        put_strips(0.5 * dot(left, ws[g]), rim, outer, slice(g * width, (g + 1) * width))
    near = senders.shape[0]
    for side, nodes in enumerate((head, tail)):
        first = 0 if side == 0 else total - rim
        place = slice(first, first + rim)
        beyond = outer[2 * side * rim : 2 * (side + 1) * rim, :]
        reach = (
            [beyond, senders[0 : 4 * rim, :]]
            if side == 0
            else [senders[near - 4 * rim : near, :], beyond]
        )
        strips[side * rim : (side + 1) * rim, :] = bottom_rows(
            nodes[...], receivers[place], picks[first // rim * size : (first // rim + 1) * size],
            jnp.concatenate(reach, axis=0), wo[...], gains[3:4],
        )
        strip = strips.at[pl.ds(side * rim, rim)]
        moves.append(pltpu.make_async_copy(strip, out.at[pl.ds(first, rim)], sems.at[1 + side]))
        moves[-1].start()
    for move in moves:
        move.wait()


whole = pl.BlockSpec(memory_space=pltpu.VMEM)
away = pl.BlockSpec(memory_space=pl.ANY)


def call(kernel, outs, operands, flops, scratch=(), far=(), far_outs=(), unread=0, limit=limit_bytes):
    moved = sum(x.size * x.dtype.itemsize for x in (*outs, *operands))
    read = len(operands) - unread
    specs = [away if i in far else whole for i in range(read)] + [away] * unread
    return pl.pallas_call(
        (lambda *refs: kernel(*refs[:read], *refs[read + unread :])) if unread else kernel,
        out_shape=tuple(outs),
        in_specs=specs,
        out_specs=tuple(away if i in far_outs else whole for i in range(len(outs))),
        scratch_shapes=list(scratch),
        compiler_params=pltpu.CompilerParams(vmem_limit_bytes=limit),
        cost_estimate=pl.CostEstimate(flops=int(flops), bytes_accessed=moved, transcendentals=0),
    )(*operands)


def like(shape, kind=f32):
    return jax.ShapeDtypeStruct(tuple(shape), kind)


def shifted(values, axis, step):
    count = lax.axis_size(axis)
    return lax.ppermute(values, axis, [(i, (i + step) % count) for i in range(count)])


def sub_parts(part):
    if lax.axis_size("sub") == 2:
        return [part, shifted(part, "sub", 1)]
    return [lax.psum(part, "sub")]


def coarse_pieces(senders, others):
    patches, lvls = lax.axis_size("patch"), lax.axis_size("lvl")
    if patches > most_direct:
        return [lax.all_gather(senders, ("patch", "lvl"), axis=0, tiled=True)], others
    near = [[senders] + [shifted(senders, "lvl", t) for t in range(1, lvls)]]
    pieces = [shifted(senders, "patch", s) for s in range(1, patches)]
    pieces, others = lax.optimization_barrier((pieces, others))
    near += [[piece] + [shifted(piece, "lvl", t) for t in range(1, lvls)] for piece in pieces]
    return [row[t] for t in range(lvls) for row in near], others


def held(values, event):
    return lax.optimization_barrier((values, event))[0]


def over_sub(pack):
    return [shifted(pack, "sub", s) for s in range(1, lax.axis_size("sub"))]


def partners(axis):
    if axis == "parts":
        return lax.axis_index(axis), lax.axis_size(axis)
    count = 2 if lax.axis_size(axis) % 2 == 0 else 1
    return lax.rem(lax.axis_index(axis), count), count


def over_partners(share_list, axis):
    size, count = lax.axis_size(axis), partners(axis)[1]
    return [
        [
            lax.ppermute(share, axis, [(i, i - i % count + (i + p) % count) for i in range(size)])
            for p in range(1, count)
        ]
        for share in share_list
    ]


def over_lvl(shares):
    return [
        [share] + [shifted(share, "lvl", t) for t in range(1, lax.axis_size("lvl"))]
        for share in shares
    ]


def all_shares(shares, others):
    near = over_lvl(shares)
    far = [over_lvl(row) for row in others]
    return [x for first, row in zip(near, far) for x in (first + [y for group in row for y in group])]


def body(
    node_states,
    coarse_states,
    children,
    down_sources,
    bottom_links,
    coarse_links,
    upward_sender,
    upward_receiver,
    upward_bias,
    upward_output,
    upward_gain,
    coarse_sender,
    coarse_receiver,
    coarse_bias,
    coarse_output,
    coarse_gain,
    downward_sender,
    downward_receiver,
    downward_bias,
    downward_output,
    downward_gain,
    bottom_sender,
    bottom_receiver,
    bottom_bias,
    bottom_output,
    bottom_gain,
):
    rows, latent = node_states.shape
    blocks = coarse_states.shape[0]
    width = upward_sender.shape[1]
    subs = lax.axis_size("sub")
    hidden = width * subs
    rim = rows // 4
    into = like((subs, 3 * latent, width), bf16)
    out_of = like((3 * hidden, latent), bf16)
    bias_rows = like((subs, 8, width))

    columns = latent // width
    lvls = lax.axis_size("lvl")

    def pack(axis):
        count = shares(axis)[1]
        return like((2 * latent // count + width // count * columns + 8, width))

    (part,) = call(
        upward_kernel,
        [like((blocks, latent))],
        [
            node_states, coarse_states, upward_sender, upward_receiver, upward_output,
            children.T, upward_bias[None],
        ],
        6 * rows * latent * width,
        [
            pltpu.VMEM((rows, latent), f32),
            pltpu.VMEM((blocks, latent), f32),
            pltpu.VMEM((latent, width), f32),
            pltpu.VMEM((latent, width), f32),
            pltpu.VMEM((width, latent), f32),
            pltpu.VMEM((2 * rows, width), bf16),
            pltpu.SemaphoreType.DMA((17,)),
        ],
        far=range(5),
        limit=tight_limit,
    )
    parts = sub_parts(part)
    down_own = (downward_sender, downward_receiver, downward_output, downward_bias[None])
    bottom_own = (bottom_sender, bottom_receiver, bottom_output, bottom_bias[None])
    down_pack, bottom_pack = call(
        share_kernel,
        [pack("parts"), pack("patch")],
        [*down_own, *bottom_own],
        latent,
        [pltpu.SemaphoreType.DMA((6 + 2 * columns,))],
        far=range(8),
        limit=tight_limit,
    )
    gains, biases = call(
        stack_kernel,
        [like((4, latent)), like((3, width))],
        [
            upward_gain[None], coarse_gain[None], downward_gain[None], bottom_gain[None],
            coarse_bias[None], downward_bias[None], bottom_bias[None], part,
        ],
        latent * hidden,
        unread=1,
    )
    down_near, bottom_near = over_sub(down_pack), over_sub(bottom_pack)
    coarse_up, senders, receivers = call(
        functools.partial(coarse_project_kernel, len(parts)),
        [like((blocks, latent)), like((blocks, width)), like((blocks, width))],
        [*parts, coarse_states, gains, biases, coarse_sender, coarse_receiver],
        12 * blocks * latent * width,
    )
    patches = lax.axis_size("patch")
    names = blocks * patches * lvls
    picks, bottom_picks = call(
        functools.partial(picks_kernel, rim, patches, blocks),
        [like((coarse_links.size, 2 * names), bf16), like((bottom_links.size, 6 * rim), bf16)],
        [coarse_links.T, bottom_links.T, senders],
        10**11,
        unread=1,
    )
    pieces, (picks, bottom_picks, down_near) = coarse_pieces(
        senders, (picks, bottom_picks, down_near)
    )
    down_far = over_partners(down_near, "parts")
    (part,) = call(
        functools.partial(coarse_kernel, len(pieces)),
        [like((blocks, latent))],
        [*pieces, picks, receivers, coarse_output, *bottom_near],
        4 * coarse_links.size * names * width,
        unread=len(bottom_near),
    )
    parts = sub_parts(part)
    bottom_near = held(bottom_near, part)
    bottom_far = over_partners(bottom_near, "patch")
    down_packs = all_shares(*held((down_near, down_far), parts[-1]))
    receivers, ws, wo = call(
        functools.partial(down_weights_kernel, len(down_packs)),
        [like((rows, hidden)), into, out_of],
        [node_states, downward_sender, downward_receiver, biases, downward_output, *down_packs, part, *(x for row in bottom_far for x in row)],
        6 * rows * latent * hidden,
        [pltpu.VMEM((subs, 3 * latent, width), bf16), pltpu.VMEM((subs, 8, width), f32)],
        unread=1 + sum(map(len, bottom_far)),
    )
    new_coarse, senders, head, tail = call(
        functools.partial(down_edge_kernel, len(parts), rim),
        [like((blocks, latent)), like((2 * blocks, hidden), bf16), like((rim, latent)), like((rim, latent))],
        [*parts, coarse_up, gains, node_states, receivers, down_sources.T, ws, wo],
        6 * 2 * rim * latent * hidden,
        [pltpu.VMEM((blocks, latent), f32), pltpu.SemaphoreType.DMA],
        far_outs=(0,),
    )
    ring = ("patch", "lvl")
    before, after = shifted(tail, ring, 1), shifted(head, ring, -1)
    (middle,) = call(
        functools.partial(down_middle_kernel, rim),
        [like((rows - 2 * rim, latent))],
        [node_states, receivers, down_sources.T, senders, wo, gains],
        6 * (rows - 2 * rim) * latent * hidden,
    )

    bottom_near, bottom_far = held((bottom_near, bottom_far), head)
    bottom_packs = all_shares(bottom_near, bottom_far)
    ws, wr, wo, bias = call(
        functools.partial(bottom_weights_kernel, len(bottom_packs)),
        [into, into, out_of, bias_rows],
        [bottom_sender, bottom_receiver, biases, bottom_output, *bottom_packs],
        latent * hidden,
    )
    senders, receivers, inner = call(
        functools.partial(bottom_middle_kernel, rim),
        [like((2 * rows, hidden), bf16), like((rows, hidden)), like((rows - 2 * rim, latent))],
        [head, middle, tail, bottom_picks, ws, wr, wo, bias, gains],
        (12 * rows + 12 * rows) * latent * hidden,
    )
    (new_nodes,) = call(
        functools.partial(bottom_edge_kernel, rim),
        [like((rows, latent))],
        [before, after, head, tail, inner, bottom_picks, senders, receivers, ws, wo, gains],
        24 * rim * latent * hidden,
        [
            pltpu.VMEM((4 * rim, hidden), bf16),
            pltpu.VMEM((2 * rim, latent), f32),
            pltpu.SemaphoreType.DMA((3,)),
        ],
        far_outs=(0,),
    )
    return (new_nodes, new_coarse)


def solution(mesh):
    split_rows, level_rows = P(("parts", "patch", "lvl"), None), P(("patch", "lvl"), None)
    weights = (P(None, "sub"), P(None, "sub"), P("sub"), P("sub", None), P())
    in_specs = (split_rows, split_rows, *([level_rows] * 4), *(weights * 4))
    out_specs = (split_rows, split_rows)
    return jax.shard_map(body, mesh=mesh, in_specs=in_specs, out_specs=out_specs, check_vma=False)
```

```python
import functools

import jax
import jax.numpy as jnp
from jax import lax
from jax.experimental import pallas as pl
from jax.experimental.pallas import tpu as pltpu
from jax.sharding import PartitionSpec as P

epsilon = 1e-05
f32 = jnp.float32
bf16 = jnp.bfloat16
limit_bytes = 12 * 1024 * 1024
share_limit = 58 * 1000 * 1000
up_limit = 50 * 1000 * 1000
most_direct = 4


def split(values):
    high = values.astype(bf16)
    return high, (values - high.astype(f32)).astype(bf16)


def dot(a, b):
    return jnp.dot(a, b, preferred_element_type=f32)


def threefold(values):
    high, low = split(values)
    return jnp.concatenate([high, high, low], axis=1)


def stacked(weights):
    high, low = split(weights)
    return jnp.concatenate([high, low, high], axis=0)


def dot3(a, b_stacked):
    return dot(threefold(a), b_stacked)


def normed(values):
    center = values - jnp.mean(values, axis=-1, keepdims=True)
    spread = jnp.mean(center * center, axis=-1, keepdims=True)
    return center * lax.rsqrt(spread + epsilon)


def upright(rows):
    count, size = rows.shape
    tall, wide = -count % 8, -size % 128
    if tall:
        rows = jnp.concatenate([rows, jnp.zeros((tall, size), rows.dtype)], axis=0)
    if wide:
        rows = jnp.concatenate([rows, jnp.zeros((count + tall, wide), rows.dtype)], axis=1)
    return jnp.transpose(rows)[:size, :count]


def one_hot(wanted, names):
    return jnp.concatenate(
        [
            jnp.where(wanted[:, k : k + 1] == names, 1.0, 0.0).astype(bf16)
            for k in range(wanted.shape[1])
        ],
        axis=0,
    )


def silu_sum(picked, halves, count):
    rows = halves.shape[0]
    total = None
    for k in range(count):
        u = picked[k * rows : (k + 1) * rows] + halves
        term = u + u * jnp.tanh(u)
        total = term if total is None else total + term
    return total


def added(refs):
    total = refs[0][...]
    for ref in refs[1:]:
        total = total + ref[...]
    return total


def started(copies, sems):
    moves = [pltpu.make_async_copy(a, b, sems.at[i]) for i, (a, b) in enumerate(copies)]
    for move in moves:
        move.start()
    return moves


def upward_kernel(nodes, coarse, children, ws, wr, bias, wo, part):
    wanted = upright(children[...])
    names = lax.broadcasted_iota(jnp.int32, (wanted.shape[0], nodes.shape[0]), 1)
    picks = one_hot(wanted, names)
    senders = jnp.concatenate(split(0.5 * dot3(nodes[...], stacked(ws[...]))), axis=0)
    receivers = 0.5 * (dot3(coarse[...], stacked(wr[...])) + bias[...])
    picked = dot(jnp.concatenate([picks, picks], axis=1), senders)
    hidden = silu_sum(picked, receivers, wanted.shape[1])
    part[...] = dot3(hidden, stacked(wo[...]))


def stack_kernel(*refs):
    params, (gains, biases) = refs[:7], refs[7:]
    for i in range(4):
        gains[i : i + 1] = params[i][...]
    for i in range(3):
        biases[i : i + 1] = params[4 + i][...]


def share_kernel(axis, *refs):
    for move in started(share_copies(refs[:4], refs[4], axis), refs[5]):
        move.wait()


def shares(axis):
    lvls = lax.axis_size("lvl")
    place, count = partners(axis)
    return place * lvls + lax.axis_index("lvl"), count * lvls


def share_copies(sources, pack, axis):
    mine, count = shares(axis)
    width = pack.shape[1]
    copies, at = [], 0
    for source in sources:
        rows = source.shape[0] // count
        if source.shape[0] == 1:
            copies.append((source, pack.at[pl.ds(at, 1)]))
            at += 8
            continue
        strip = pl.ds(pl.multiple_of(mine * rows, rows), rows)
        for j in range(source.shape[1] // width):
            copies.append((source.at[strip, pl.ds(j * width, width)], pack.at[pl.ds(at, rows)]))
            at += rows
    return copies


def picks_kernel(rim, patches, blocks, coarse_links, bottom_links, coarse_picks, bottom_picks):
    wanted = upright(coarse_links[...])
    rows = wanted.shape[0]
    lvls = lax.axis_size("lvl")
    half = coarse_picks.shape[1] // 2
    column = lax.broadcasted_iota(jnp.int32, (rows, blocks), 1)
    for t in range(lvls):
        for s in range(patches):
            patch = lax.rem(lax.axis_index("patch") + patches - s, patches)
            lvl = lax.rem(lax.axis_index("lvl") + lvls - t, lvls)
            first = (patch * lvls + lvl) * blocks
            at = (t * patches + s) * blocks
            piece = one_hot(wanted, column + first)
            coarse_picks[:, at : at + blocks] = piece
            coarse_picks[:, half + at : half + at + blocks] = piece
    wanted = upright(bottom_links[...])
    size = rim * wanted.shape[1]
    names = lax.broadcasted_iota(jnp.int32, (rim, 3 * rim), 1)
    for i in range(wanted.shape[0] // rim):
        picks = one_hot(wanted[i * rim : (i + 1) * rim], names + i * rim)
        for j in range(6):
            piece = picks[:, j // 2 * rim : (j // 2 + 1) * rim]
            bottom_picks[i * size : (i + 1) * size, j * rim : (j + 1) * rim] = piece


def coarse_project_kernel(count, *refs):
    parts, refs = refs[:count], refs[count:]
    coarse, gains, biases, ws, wr, updated, senders, receivers = refs
    rows = coarse[...] + gains[0:1] * normed(added(parts))
    updated[...] = rows
    senders[...] = 0.5 * dot3(rows, stacked(ws[...]))
    receivers[...] = 0.5 * (dot3(rows, stacked(wr[...])) + biases[0:1])


def coarse_kernel(count, *refs):
    pieces, (all_picks, receivers, wo) = refs[:count], refs[count : count + 3]
    part = refs[-1]
    senders = jnp.concatenate([piece[...] for piece in pieces], axis=0)
    picked = dot(all_picks[...], jnp.concatenate(split(senders), axis=0))
    hidden = silu_sum(picked, receivers[...], all_picks.shape[0] // receivers.shape[0])
    part[...] = dot3(hidden, stacked(wo[...]))


def fetched_shares(packs, axis):
    subs, lvls = lax.axis_size("sub"), lax.axis_size("lvl")
    sub, lvl = lax.axis_index("sub"), lax.axis_index("lvl")
    place, count = partners(axis)
    left = iter(packs)
    for s in range(1, subs):
        for p in range(count):
            for t in range(lvls):
                mine = lax.rem(place + count - p, count) * lvls + lax.rem(lvl + lvls - t, lvls)
                yield next(left), lax.rem(sub + subs - s, subs), mine, p == 0 and t == 0


def put_stacked(values, out, first, columns):
    high, low = split(values)
    depth, rows = out.shape[0] // 3, values.shape[0]
    for i, half in enumerate((high, low, high)):
        out[pl.ds(pl.multiple_of(i * depth + first, 16), rows), columns] = half


def collect_in(own, packs, axis, at, out):
    everything = slice(0, own.shape[1])
    put_stacked(own[...], out.at[lax.axis_index("sub")], 0, everything)
    share = own.shape[0] // shares(axis)[1]
    for pack, block, mine, _ in fetched_shares(packs, axis):
        put_stacked(pack[at : at + share, :], out.at[block], mine * share, everything)


def collect_out(own, packs, axis, at, out):
    width, latent = own.shape
    put_stacked(own[...], out, lax.axis_index("sub") * width, slice(0, latent))
    thin = width // shares(axis)[1]
    for pack, block, mine, _ in fetched_shares(packs, axis):
        for j in range(latent // width):
            part = pack[at + j * thin : at + (j + 1) * thin, :]
            put_stacked(part, out, block * width + mine * thin, slice(j * width, (j + 1) * width))


def collect_bias(own, packs, axis, at, out):
    out[lax.axis_index("sub")] = jnp.broadcast_to(own, (8, own.shape[1]))
    for pack, block, _, whole_row in fetched_shares(packs, axis):
        if whole_row:
            out[block] = jnp.broadcast_to(pack[at : at + 1, :], (8, own.shape[1]))


def down_weights_kernel(count, nodes, ws, wr, biases, wo, *refs):
    packs, (receivers, ws_all, wo_all, wr_all, bias_all) = refs[:count], refs[count:]
    width = ws.shape[1]
    share = ws.shape[0] // shares("parts")[1]
    collect_in(ws, packs, "parts", 0, ws_all)
    collect_in(wr, packs, "parts", share, wr_all)
    collect_out(wo, packs, "parts", 2 * share, wo_all)
    collect_bias(biases[1:2], packs, "parts", 3 * share, bias_all)
    states = threefold(nodes[...])
    for g in range(wr_all.shape[0]):
        receivers[:, g * width : (g + 1) * width] = 0.5 * (dot(states, wr_all[g]) + bias_all[g][0:1])


def bottom_weights_kernel(count, ws, wr, biases, wo, *refs):
    packs, (ws_all, wr_all, wo_all, bias_all) = refs[:count], refs[count:]
    share = ws.shape[0] // shares("patch")[1]
    collect_in(ws, packs, "patch", 0, ws_all)
    collect_in(wr, packs, "patch", share, wr_all)
    collect_out(wo, packs, "patch", 2 * share, wo_all)
    collect_bias(biases[2:3], packs, "patch", 3 * share, bias_all)


def down_rows(nodes, receivers, sources, senders, wo, gain):
    blocks = senders.shape[0] // 2
    column = lax.broadcasted_iota(jnp.int32, (nodes.shape[0], 2 * blocks), 1)
    names = jnp.where(column < blocks, column, column - blocks)
    picked = dot(one_hot(sources, names), senders)
    hidden = silu_sum(picked, receivers, sources.shape[1])
    return nodes + gain * normed(dot3(hidden, wo))


def down_edge_kernel(count, rim, *refs):
    parts, refs = refs[:count], refs[count:]
    coarse_up, gains, nodes, receivers, sources, ws, wo = refs[:7]
    new_coarse, senders, head, tail, held_here, sem = refs[7:]
    rows = coarse_up[...] + gains[1:2] * normed(added(parts))
    held_here[...] = rows
    move = pltpu.make_async_copy(held_here, new_coarse, sem)
    move.start()
    blocks = rows.shape[0]
    width = ws.shape[2]
    left = threefold(rows)
    for g in range(ws.shape[0]):
        columns = slice(g * width, (g + 1) * width)
        high, low = split(0.5 * dot(left, ws[g]))
        senders[0:blocks, columns] = high
        senders[blocks : 2 * blocks, columns] = low
    total = nodes.shape[0]
    wanted = upright(sources[...])
    for out, place in ((head, slice(0, rim)), (tail, slice(total - rim, total))):
        out[...] = down_rows(
            nodes[place], receivers[place], wanted[place], senders[...], wo[...], gains[2:3]
        )
    move.wait()


def down_middle_kernel(rim, nodes, receivers, sources, senders, wo, gains, middle):
    place = slice(rim, nodes.shape[0] - rim)
    middle[...] = down_rows(
        nodes[place], receivers[place], upright(sources[...])[place], senders[...], wo[...], gains[2:3]
    )


def bottom_rows(nodes, receivers, picks, senders, wo, gain, ahead=None):
    half = senders.shape[1] // 2
    hidden = []
    for place in (slice(0, half), slice(half, 2 * half)):
        picked = dot(picks, senders[:, place])
        if ahead is not None:
            picked = picked + ahead[:, place]
        hidden.append(silu_sum(picked, receivers[:, place], picks.shape[0] // nodes.shape[0]))
    return nodes + gain * normed(dot3(jnp.concatenate(hidden, axis=1), wo))


def put_strips(values, rim, out, columns):
    high, low = split(values)
    for i in range(values.shape[0] // rim):
        strip = slice(i * rim, (i + 1) * rim)
        out[2 * i * rim : (2 * i + 1) * rim, columns] = high[strip]
        out[(2 * i + 1) * rim : (2 * i + 2) * rim, columns] = low[strip]


def bottom_middle_kernel(rim, head, middle, tail, picks, ws, wr, wo, bias, gains, receivers, out, ahead, senders):
    nodes = jnp.concatenate([head[...], middle[...], tail[...]], axis=0)
    left = threefold(nodes)
    width = ws.shape[2]
    for g in range(ws.shape[0]):
        columns = slice(g * width, (g + 1) * width)
        put_strips(0.5 * dot(left, ws[g]), rim, senders, columns)
        receivers[:, columns] = 0.5 * (dot(left, wr[g]) + bias[g][0:1])
    total = nodes.shape[0]
    size = picks.shape[0] * rim // total
    for i in range(1, total // rim - 1):
        place = slice(i * rim, (i + 1) * rim)
        inner = slice((i - 1) * rim, i * rim)
        out[inner, :] = bottom_rows(
            middle[inner], receivers[place], picks[i * size : (i + 1) * size],
            senders[2 * (i - 1) * rim : 2 * (i + 2) * rim, :], wo[...], gains[3:4],
        )
    near, last = senders.shape[0], picks.shape[0] - size
    ahead[0:size, :] = dot(picks[0:size, 2 * rim : 6 * rim], senders[0 : 4 * rim, :])
    ahead[size : 2 * size, :] = dot(
        picks[last : last + size, 0 : 4 * rim], senders[near - 4 * rim : near, :]
    )


def bottom_edge_kernel(rim, before, after, head, tail, inner, ahead, picks, receivers, ws, wo, gains, out, outer, strips, sems):
    total = receivers.shape[0]
    size = picks.shape[0] * rim // total
    moves = [pltpu.make_async_copy(inner, out.at[pl.ds(rim, total - 2 * rim)], sems.at[0])]
    moves[0].start()
    left = threefold(jnp.concatenate([before[...], after[...]], axis=0))
    width = ws.shape[2]
    for g in range(ws.shape[0]):
        put_strips(0.5 * dot(left, ws[g]), rim, outer, slice(g * width, (g + 1) * width))
    for side, nodes in enumerate((head, tail)):
        first, column = (0, 0) if side == 0 else (total - rim, 4 * rim)
        place = slice(first, first + rim)
        chosen = picks[first // rim * size : (first // rim + 1) * size, column : column + 2 * rim]
        strips[side * rim : (side + 1) * rim, :] = bottom_rows(
            nodes[...], receivers[place], chosen, outer[2 * side * rim : 2 * (side + 1) * rim, :],
            wo[...], gains[3:4], ahead[side * size : (side + 1) * size, :],
        )
        strip = strips.at[pl.ds(side * rim, rim)]
        moves.append(pltpu.make_async_copy(strip, out.at[pl.ds(first, rim)], sems.at[1 + side]))
        moves[-1].start()
    for move in moves:
        move.wait()


whole = pl.BlockSpec(memory_space=pltpu.VMEM)
away = pl.BlockSpec(memory_space=pl.ANY)


def call(kernel, outs, operands, flops, scratch=(), far=(), far_outs=(), unread=0, limit=limit_bytes):
    moved = sum(x.size * x.dtype.itemsize for x in (*outs, *operands))
    read = len(operands) - unread
    specs = [away if i in far else whole for i in range(read)] + [away] * unread
    return pl.pallas_call(
        (lambda *refs: kernel(*refs[:read], *refs[read + unread :])) if unread else kernel,
        out_shape=tuple(outs),
        in_specs=specs,
        out_specs=tuple(away if i in far_outs else whole for i in range(len(outs))),
        scratch_shapes=list(scratch),
        compiler_params=pltpu.CompilerParams(vmem_limit_bytes=limit),
        cost_estimate=pl.CostEstimate(flops=int(flops), bytes_accessed=moved, transcendentals=0),
    )(*operands)


def like(shape, kind=f32):
    return jax.ShapeDtypeStruct(tuple(shape), kind)


def shifted(values, axis, step):
    count = lax.axis_size(axis)
    return lax.ppermute(values, axis, [(i, (i + step) % count) for i in range(count)])


def sub_parts(part):
    if lax.axis_size("sub") == 2:
        return [part, shifted(part, "sub", 1)]
    return [lax.psum(part, "sub")]


def coarse_pieces(senders, others):
    patches, lvls = lax.axis_size("patch"), lax.axis_size("lvl")
    if patches > most_direct:
        return [lax.all_gather(senders, ("patch", "lvl"), axis=0, tiled=True)], others
    near = [[senders] + [shifted(senders, "lvl", t) for t in range(1, lvls)]]
    pieces = [shifted(senders, "patch", s) for s in range(1, patches)]
    pieces, others = lax.optimization_barrier((pieces, others))
    near += [[piece] + [shifted(piece, "lvl", t) for t in range(1, lvls)] for piece in pieces]
    return [row[t] for t in range(lvls) for row in near], others


def held(values, event):
    return lax.optimization_barrier((values, event))[0]


def over_sub(pack):
    return [shifted(pack, "sub", s) for s in range(1, lax.axis_size("sub"))]


def partners(axis):
    if axis == "parts":
        return lax.axis_index(axis), lax.axis_size(axis)
    count = 2 if lax.axis_size(axis) % 2 == 0 else 1
    return lax.rem(lax.axis_index(axis), count), count


def over_partners(share_list, axis):
    size, count = lax.axis_size(axis), partners(axis)[1]
    return [
        [
            lax.ppermute(share, axis, [(i, i - i % count + (i + p) % count) for i in range(size)])
            for p in range(1, count)
        ]
        for share in share_list
    ]


def over_lvl(shares):
    return [
        [share] + [shifted(share, "lvl", t) for t in range(1, lax.axis_size("lvl"))]
        for share in shares
    ]


def all_shares(shares, others):
    near = over_lvl(shares)
    far = [over_lvl(row) for row in others]
    return [x for first, row in zip(near, far) for x in (first + [y for group in row for y in group])]


def body(
    node_states,
    coarse_states,
    children,
    down_sources,
    bottom_links,
    coarse_links,
    upward_sender,
    upward_receiver,
    upward_bias,
    upward_output,
    upward_gain,
    coarse_sender,
    coarse_receiver,
    coarse_bias,
    coarse_output,
    coarse_gain,
    downward_sender,
    downward_receiver,
    downward_bias,
    downward_output,
    downward_gain,
    bottom_sender,
    bottom_receiver,
    bottom_bias,
    bottom_output,
    bottom_gain,
):
    rows, latent = node_states.shape
    blocks = coarse_states.shape[0]
    width = upward_sender.shape[1]
    subs = lax.axis_size("sub")
    hidden = width * subs
    rim = rows // 4
    into = like((subs, 3 * latent, width), bf16)
    out_of = like((3 * hidden, latent), bf16)
    bias_rows = like((subs, 8, width))

    columns = latent // width
    lvls = lax.axis_size("lvl")

    def pack(axis):
        count = shares(axis)[1]
        return like((2 * latent // count + width // count * columns + 8, width))

    (part,) = call(
        upward_kernel,
        [like((blocks, latent))],
        [
            node_states, coarse_states, children.T, upward_sender, upward_receiver,
            upward_bias[None], upward_output,
        ],
        6 * rows * latent * width,
        limit=up_limit,
    )
    parts = sub_parts(part)
    down_own = (downward_sender, downward_receiver, downward_output, downward_bias[None])
    bottom_own = (bottom_sender, bottom_receiver, bottom_output, bottom_bias[None])
    (down_pack,), (bottom_pack,) = (
        call(
            functools.partial(share_kernel, axis),
            [pack(axis)],
            own,
            latent,
            [pltpu.SemaphoreType.DMA((3 + columns,))],
            far=range(4),
            limit=share_limit,
        )
        for axis, own in (("parts", down_own), ("patch", bottom_own))
    )
    gains, biases = call(
        stack_kernel,
        [like((4, latent)), like((3, width))],
        [
            upward_gain[None], coarse_gain[None], downward_gain[None], bottom_gain[None],
            coarse_bias[None], downward_bias[None], bottom_bias[None], part,
        ],
        latent * hidden,
        unread=1,
    )
    down_near = over_sub(down_pack)
    down_near = held(down_near, parts[-1])
    bottom_near = over_sub(bottom_pack)
    down_far = over_partners(down_near, "parts")
    coarse_up, senders, receivers = call(
        functools.partial(coarse_project_kernel, len(parts)),
        [like((blocks, latent)), like((blocks, width)), like((blocks, width))],
        [*parts, coarse_states, gains, biases, coarse_sender, coarse_receiver],
        12 * blocks * latent * width,
    )
    patches = lax.axis_size("patch")
    names = blocks * patches * lvls
    picks, bottom_picks = call(
        functools.partial(picks_kernel, rim, patches, blocks),
        [like((coarse_links.size, 2 * names), bf16), like((bottom_links.size, 6 * rim), bf16)],
        [coarse_links.T, bottom_links.T, senders],
        coarse_links.size * names,
        unread=1,
    )
    pieces, (picks, bottom_picks, down_near, down_far, bottom_near) = coarse_pieces(
        senders, (picks, bottom_picks, down_near, down_far, bottom_near)
    )
    down_packs = all_shares(down_near, down_far)
    bottom_far = over_partners(bottom_near, "patch")
    (part,) = call(
        functools.partial(coarse_kernel, len(pieces)),
        [like((blocks, latent))],
        [*pieces, picks, receivers, coarse_output],
        4 * coarse_links.size * names * width,
    )
    parts = sub_parts(part)
    receivers, ws, wo = call(
        functools.partial(down_weights_kernel, len(down_packs)),
        [like((rows, hidden)), into, out_of],
        [node_states, downward_sender, downward_receiver, biases, downward_output, *down_packs, part],
        6 * rows * latent * hidden,
        [pltpu.VMEM((subs, 3 * latent, width), bf16), pltpu.VMEM((subs, 8, width), f32)],
        unread=1,
    )
    new_coarse, senders, head, tail = call(
        functools.partial(down_edge_kernel, len(parts), rim),
        [like((blocks, latent)), like((2 * blocks, hidden), bf16), like((rim, latent)), like((rim, latent))],
        [*parts, coarse_up, gains, node_states, receivers, down_sources.T, ws, wo],
        6 * 2 * rim * latent * hidden,
        [pltpu.VMEM((blocks, latent), f32), pltpu.SemaphoreType.DMA],
        far_outs=(0,),
    )
    ring = ("patch", "lvl")
    before, after = shifted(tail, ring, 1), shifted(head, ring, -1)
    (middle,) = call(
        functools.partial(down_middle_kernel, rim),
        [like((rows - 2 * rim, latent))],
        [node_states, receivers, down_sources.T, senders, wo, gains],
        6 * (rows - 2 * rim) * latent * hidden,
    )

    bottom_near, bottom_far = held((bottom_near, bottom_far), head)
    bottom_packs = all_shares(bottom_near, bottom_far)
    ws, wr, wo, bias = call(
        functools.partial(bottom_weights_kernel, len(bottom_packs)),
        [into, into, out_of, bias_rows],
        [bottom_sender, bottom_receiver, biases, bottom_output, *bottom_packs],
        latent * hidden,
    )
    receivers, inner, ahead = call(
        functools.partial(bottom_middle_kernel, rim),
        [like((rows, hidden)), like((rows - 2 * rim, latent)), like((bottom_links.size // (rows // rim) * 2, hidden))],
        [head, middle, tail, bottom_picks, ws, wr, wo, bias, gains],
        (12 * rows + 12 * rows) * latent * hidden,
        [pltpu.VMEM((2 * rows, hidden), bf16)],
    )
    (new_nodes,) = call(
        functools.partial(bottom_edge_kernel, rim),
        [like((rows, latent))],
        [before, after, head, tail, inner, ahead, bottom_picks, receivers, ws, wo, gains],
        24 * rim * latent * hidden,
        [
            pltpu.VMEM((4 * rim, hidden), bf16),
            pltpu.VMEM((2 * rim, latent), f32),
            pltpu.SemaphoreType.DMA((3,)),
        ],
        far_outs=(0,),
    )
    return (new_nodes, new_coarse)


def solution(mesh):
    split_rows, level_rows = P(("parts", "patch", "lvl"), None), P(("patch", "lvl"), None)
    weights = (P(None, "sub"), P(None, "sub"), P("sub"), P("sub", None), P())
    in_specs = (split_rows, split_rows, *([level_rows] * 4), *(weights * 4))
    out_specs = (split_rows, split_rows)
    return jax.shard_map(body, mesh=mesh, in_specs=in_specs, out_specs=out_specs, check_vma=False)
```

```python
import functools

import jax
import jax.numpy as jnp
from jax import lax
from jax.experimental import pallas as pl
from jax.experimental.pallas import tpu as pltpu
from jax.sharding import PartitionSpec as P

epsilon = 1e-05
f32 = jnp.float32
bf16 = jnp.bfloat16
limit_bytes = 12 * 1024 * 1024
tight_limit = 64 * 1000 * 1000
most_direct = 4


def split(values):
    high = values.astype(bf16)
    return high, (values - high.astype(f32)).astype(bf16)


def dot(a, b):
    return jnp.dot(a, b, preferred_element_type=f32)


def threefold(values):
    high, low = split(values)
    return jnp.concatenate([high, high, low], axis=1)


def stacked(weights):
    high, low = split(weights)
    return jnp.concatenate([high, low, high], axis=0)


def dot3(a, b_stacked):
    return dot(threefold(a), b_stacked)


def normed(values):
    center = values - jnp.mean(values, axis=-1, keepdims=True)
    spread = jnp.mean(center * center, axis=-1, keepdims=True)
    return center * lax.rsqrt(spread + epsilon)


def upright(rows):
    count, size = rows.shape
    tall, wide = -count % 8, -size % 128
    if tall:
        rows = jnp.concatenate([rows, jnp.zeros((tall, size), rows.dtype)], axis=0)
    if wide:
        rows = jnp.concatenate([rows, jnp.zeros((count + tall, wide), rows.dtype)], axis=1)
    return jnp.transpose(rows)[:size, :count]


def one_hot(wanted, names):
    return jnp.concatenate(
        [
            jnp.where(wanted[:, k : k + 1] == names, 1.0, 0.0).astype(bf16)
            for k in range(wanted.shape[1])
        ],
        axis=0,
    )


def silu_sum(picked, halves, count):
    rows = halves.shape[0]
    total = None
    for k in range(count):
        u = picked[k * rows : (k + 1) * rows] + halves
        term = u + u * jnp.tanh(u)
        total = term if total is None else total + term
    return total


def added(refs):
    total = refs[0][...]
    for ref in refs[1:]:
        total = total + ref[...]
    return total


def started(copies, sems):
    moves = [pltpu.make_async_copy(a, b, sems.at[i]) for i, (a, b) in enumerate(copies)]
    for move in moves:
        move.start()
    return moves


def strips(source, target, count):
    rows = source.shape[0] // count
    return [
        (source.at[pl.ds(i * rows, rows)], target.at[pl.ds(i * rows, rows)]) for i in range(count)
    ]


def upward_kernel(nodes_hbm, coarse_hbm, ws_hbm, wr_hbm, wo_hbm, children, bias, part, nodes, coarse, ws, wr, wo, senders, sems):
    cuts = 4
    moves = started(
        strips(ws_hbm, ws, cuts)
        + strips(nodes_hbm, nodes, cuts)
        + [(coarse_hbm, coarse)]
        + strips(wr_hbm, wr, cuts)
        + strips(wo_hbm, wo, cuts),
        sems,
    )
    wanted = upright(children[...])
    names = lax.broadcasted_iota(jnp.int32, (wanted.shape[0], nodes.shape[0]), 1)
    picks = one_hot(wanted, names)
    picks = jnp.concatenate([picks, picks], axis=1)
    for move in moves[:cuts]:
        move.wait()
    ws_stacked = stacked(ws[...])
    rows, total = nodes.shape[0] // cuts, nodes.shape[0]
    for i in range(cuts):
        moves[cuts + i].wait()
        first, last = i * rows, (i + 1) * rows
        high, low = split(0.5 * dot3(nodes[first:last], ws_stacked))
        senders[first:last] = high
        senders[total + first : total + last] = low
    for move in moves[2 * cuts : 3 * cuts + 1]:
        move.wait()
    receivers = 0.5 * (dot3(coarse[...], stacked(wr[...])) + bias[...])
    hidden = silu_sum(dot(picks, senders[...]), receivers, wanted.shape[1])
    for move in moves[3 * cuts + 1 :]:
        move.wait()
    part[...] = dot3(hidden, stacked(wo[...]))


def stack_kernel(*refs):
    params, (gains, biases) = refs[:7], refs[7:]
    for i in range(4):
        gains[i : i + 1] = params[i][...]
    for i in range(3):
        biases[i : i + 1] = params[4 + i][...]


def share_kernel(axis, *refs):
    for move in started(share_copies(refs[:4], refs[4], axis), refs[5]):
        move.wait()


def shares(axis):
    lvls = lax.axis_size("lvl")
    place, count = partners(axis)
    return place * lvls + lax.axis_index("lvl"), count * lvls


def share_copies(sources, pack, axis):
    mine, count = shares(axis)
    width = pack.shape[1]
    copies, at = [], 0
    for source in sources:
        rows = source.shape[0] // count
        if source.shape[0] == 1:
            copies.append((source, pack.at[pl.ds(at, 1)]))
            at += 8
            continue
        strip = pl.ds(pl.multiple_of(mine * rows, rows), rows)
        for j in range(source.shape[1] // width):
            copies.append((source.at[strip, pl.ds(j * width, width)], pack.at[pl.ds(at, rows)]))
            at += rows
    return copies


def picks_kernel(rim, patches, blocks, coarse_links, bottom_links, coarse_picks, bottom_picks):
    wanted = upright(coarse_links[...])
    rows = wanted.shape[0]
    lvls = lax.axis_size("lvl")
    half = coarse_picks.shape[1] // 2
    column = lax.broadcasted_iota(jnp.int32, (rows, blocks), 1)
    for t in range(lvls):
        for s in range(patches):
            patch = lax.rem(lax.axis_index("patch") + patches - s, patches)
            lvl = lax.rem(lax.axis_index("lvl") + lvls - t, lvls)
            first = (patch * lvls + lvl) * blocks
            at = (t * patches + s) * blocks
            piece = one_hot(wanted, column + first)
            coarse_picks[:, at : at + blocks] = piece
            coarse_picks[:, half + at : half + at + blocks] = piece
    wanted = upright(bottom_links[...])
    size = rim * wanted.shape[1]
    names = lax.broadcasted_iota(jnp.int32, (rim, 3 * rim), 1)
    for i in range(wanted.shape[0] // rim):
        picks = one_hot(wanted[i * rim : (i + 1) * rim], names + i * rim)
        for j in range(6):
            piece = picks[:, j // 2 * rim : (j // 2 + 1) * rim]
            bottom_picks[i * size : (i + 1) * size, j * rim : (j + 1) * rim] = piece


def coarse_project_kernel(count, *refs):
    parts, refs = refs[:count], refs[count:]
    coarse, gains, biases, ws, wr, updated, senders, receivers = refs
    rows = coarse[...] + gains[0:1] * normed(added(parts))
    updated[...] = rows
    senders[...] = 0.5 * dot3(rows, stacked(ws[...]))
    receivers[...] = 0.5 * (dot3(rows, stacked(wr[...])) + biases[0:1])


def coarse_kernel(count, *refs):
    pieces, (all_picks, receivers, wo) = refs[:count], refs[count : count + 3]
    part = refs[-1]
    senders = jnp.concatenate([piece[...] for piece in pieces], axis=0)
    picked = dot(all_picks[...], jnp.concatenate(split(senders), axis=0))
    hidden = silu_sum(picked, receivers[...], all_picks.shape[0] // receivers.shape[0])
    part[...] = dot3(hidden, stacked(wo[...]))


def fetched_shares(packs, axis):
    subs, lvls = lax.axis_size("sub"), lax.axis_size("lvl")
    sub, lvl = lax.axis_index("sub"), lax.axis_index("lvl")
    place, count = partners(axis)
    left = iter(packs)
    for s in range(1, subs):
        for p in range(count):
            for t in range(lvls):
                mine = lax.rem(place + count - p, count) * lvls + lax.rem(lvl + lvls - t, lvls)
                yield next(left), lax.rem(sub + subs - s, subs), mine, p == 0 and t == 0


def put_stacked(values, out, first, columns):
    high, low = split(values)
    depth, rows = out.shape[0] // 3, values.shape[0]
    for i, half in enumerate((high, low, high)):
        out[pl.ds(pl.multiple_of(i * depth + first, 16), rows), columns] = half


def collect_in(own, packs, axis, at, out):
    everything = slice(0, own.shape[1])
    put_stacked(own[...], out.at[lax.axis_index("sub")], 0, everything)
    share = own.shape[0] // shares(axis)[1]
    for pack, block, mine, _ in fetched_shares(packs, axis):
        put_stacked(pack[at : at + share, :], out.at[block], mine * share, everything)


def collect_out(own, packs, axis, at, out):
    width, latent = own.shape
    put_stacked(own[...], out, lax.axis_index("sub") * width, slice(0, latent))
    thin = width // shares(axis)[1]
    for pack, block, mine, _ in fetched_shares(packs, axis):
        for j in range(latent // width):
            part = pack[at + j * thin : at + (j + 1) * thin, :]
            put_stacked(part, out, block * width + mine * thin, slice(j * width, (j + 1) * width))


def collect_bias(own, packs, axis, at, out):
    out[lax.axis_index("sub")] = jnp.broadcast_to(own, (8, own.shape[1]))
    for pack, block, _, whole_row in fetched_shares(packs, axis):
        if whole_row:
            out[block] = jnp.broadcast_to(pack[at : at + 1, :], (8, own.shape[1]))


def down_weights_kernel(count, nodes, ws, wr, biases, wo, *refs):
    packs, (receivers, ws_all, wo_all, wr_all, bias_all) = refs[:count], refs[count:]
    width = ws.shape[1]
    share = ws.shape[0] // shares("parts")[1]
    collect_in(ws, packs, "parts", 0, ws_all)
    collect_in(wr, packs, "parts", share, wr_all)
    collect_out(wo, packs, "parts", 2 * share, wo_all)
    collect_bias(biases[1:2], packs, "parts", 3 * share, bias_all)
    states = threefold(nodes[...])
    for g in range(wr_all.shape[0]):
        receivers[:, g * width : (g + 1) * width] = 0.5 * (dot(states, wr_all[g]) + bias_all[g][0:1])


def bottom_weights_kernel(count, ws, wr, biases, wo, *refs):
    packs, (ws_all, wr_all, wo_all, bias_all) = refs[:count], refs[count:]
    share = ws.shape[0] // shares("patch")[1]
    collect_in(ws, packs, "patch", 0, ws_all)
    collect_in(wr, packs, "patch", share, wr_all)
    collect_out(wo, packs, "patch", 2 * share, wo_all)
    collect_bias(biases[2:3], packs, "patch", 3 * share, bias_all)


def down_rows(nodes, receivers, sources, senders, wo, gain):
    blocks = senders.shape[0] // 2
    column = lax.broadcasted_iota(jnp.int32, (nodes.shape[0], 2 * blocks), 1)
    names = jnp.where(column < blocks, column, column - blocks)
    picked = dot(one_hot(sources, names), senders)
    hidden = silu_sum(picked, receivers, sources.shape[1])
    return nodes + gain * normed(dot3(hidden, wo))


def down_edge_kernel(count, rim, *refs):
    parts, refs = refs[:count], refs[count:]
    coarse_up, gains, nodes, receivers, sources, ws, wo = refs[:7]
    new_coarse, senders, head, tail, held_here, sem = refs[7:]
    rows = coarse_up[...] + gains[1:2] * normed(added(parts))
    held_here[...] = rows
    move = pltpu.make_async_copy(held_here, new_coarse, sem)
    move.start()
    blocks = rows.shape[0]
    width = ws.shape[2]
    left = threefold(rows)
    for g in range(ws.shape[0]):
        columns = slice(g * width, (g + 1) * width)
        high, low = split(0.5 * dot(left, ws[g]))
        senders[0:blocks, columns] = high
        senders[blocks : 2 * blocks, columns] = low
    total = nodes.shape[0]
    wanted = upright(sources[...])
    for out, place in ((head, slice(0, rim)), (tail, slice(total - rim, total))):
        out[...] = down_rows(
            nodes[place], receivers[place], wanted[place], senders[...], wo[...], gains[2:3]
        )
    move.wait()


def down_middle_kernel(rim, nodes, receivers, sources, senders, wo, gains, middle):
    place = slice(rim, nodes.shape[0] - rim)
    middle[...] = down_rows(
        nodes[place], receivers[place], upright(sources[...])[place], senders[...], wo[...], gains[2:3]
    )


def bottom_rows(nodes, receivers, picks, senders, wo, gain, ahead=None):
    half = senders.shape[1] // 2
    hidden = []
    for place in (slice(0, half), slice(half, 2 * half)):
        picked = dot(picks, senders[:, place])
        if ahead is not None:
            picked = picked + ahead[:, place]
        hidden.append(silu_sum(picked, receivers[:, place], picks.shape[0] // nodes.shape[0]))
    return nodes + gain * normed(dot3(jnp.concatenate(hidden, axis=1), wo))


def put_strips(values, rim, out, columns):
    high, low = split(values)
    for i in range(values.shape[0] // rim):
        strip = slice(i * rim, (i + 1) * rim)
        out[2 * i * rim : (2 * i + 1) * rim, columns] = high[strip]
        out[(2 * i + 1) * rim : (2 * i + 2) * rim, columns] = low[strip]


def bottom_middle_kernel(rim, head, middle, tail, picks, ws, wr, wo, bias, gains, receivers, out, ahead, senders):
    nodes = jnp.concatenate([head[...], middle[...], tail[...]], axis=0)
    left = threefold(nodes)
    width = ws.shape[2]
    for g in range(ws.shape[0]):
        columns = slice(g * width, (g + 1) * width)
        put_strips(0.5 * dot(left, ws[g]), rim, senders, columns)
        receivers[:, columns] = 0.5 * (dot(left, wr[g]) + bias[g][0:1])
    total = nodes.shape[0]
    size = picks.shape[0] * rim // total
    for i in range(1, total // rim - 1):
        place = slice(i * rim, (i + 1) * rim)
        inner = slice((i - 1) * rim, i * rim)
        out[inner, :] = bottom_rows(
            middle[inner], receivers[place], picks[i * size : (i + 1) * size],
            senders[2 * (i - 1) * rim : 2 * (i + 2) * rim, :], wo[...], gains[3:4],
        )
    near, last = senders.shape[0], picks.shape[0] - size
    ahead[0:size, :] = dot(picks[0:size, 2 * rim : 6 * rim], senders[0 : 4 * rim, :])
    ahead[size : 2 * size, :] = dot(
        picks[last : last + size, 0 : 4 * rim], senders[near - 4 * rim : near, :]
    )


def bottom_edge_kernel(rim, before, after, head, tail, inner, ahead, picks, receivers, ws, wo, gains, out, outer, strips, sems):
    total = receivers.shape[0]
    size = picks.shape[0] * rim // total
    moves = [pltpu.make_async_copy(inner, out.at[pl.ds(rim, total - 2 * rim)], sems.at[0])]
    moves[0].start()
    left = threefold(jnp.concatenate([before[...], after[...]], axis=0))
    width = ws.shape[2]
    for g in range(ws.shape[0]):
        put_strips(0.5 * dot(left, ws[g]), rim, outer, slice(g * width, (g + 1) * width))
    for side, nodes in enumerate((head, tail)):
        first, column = (0, 0) if side == 0 else (total - rim, 4 * rim)
        place = slice(first, first + rim)
        chosen = picks[first // rim * size : (first // rim + 1) * size, column : column + 2 * rim]
        strips[side * rim : (side + 1) * rim, :] = bottom_rows(
            nodes[...], receivers[place], chosen, outer[2 * side * rim : 2 * (side + 1) * rim, :],
            wo[...], gains[3:4], ahead[side * size : (side + 1) * size, :],
        )
        strip = strips.at[pl.ds(side * rim, rim)]
        moves.append(pltpu.make_async_copy(strip, out.at[pl.ds(first, rim)], sems.at[1 + side]))
        moves[-1].start()
    for move in moves:
        move.wait()


whole = pl.BlockSpec(memory_space=pltpu.VMEM)
away = pl.BlockSpec(memory_space=pl.ANY)


def call(kernel, outs, operands, flops, scratch=(), far=(), far_outs=(), unread=0, limit=limit_bytes):
    moved = sum(x.size * x.dtype.itemsize for x in (*outs, *operands))
    read = len(operands) - unread
    specs = [away if i in far else whole for i in range(read)] + [away] * unread
    return pl.pallas_call(
        (lambda *refs: kernel(*refs[:read], *refs[read + unread :])) if unread else kernel,
        out_shape=tuple(outs),
        in_specs=specs,
        out_specs=tuple(away if i in far_outs else whole for i in range(len(outs))),
        scratch_shapes=list(scratch),
        compiler_params=pltpu.CompilerParams(vmem_limit_bytes=limit),
        cost_estimate=pl.CostEstimate(flops=int(flops), bytes_accessed=moved, transcendentals=0),
    )(*operands)


def like(shape, kind=f32):
    return jax.ShapeDtypeStruct(tuple(shape), kind)


def shifted(values, axis, step):
    count = lax.axis_size(axis)
    return lax.ppermute(values, axis, [(i, (i + step) % count) for i in range(count)])


def sub_parts(part):
    if lax.axis_size("sub") == 2:
        return [part, shifted(part, "sub", 1)]
    return [lax.psum(part, "sub")]


def coarse_pieces(senders, others):
    patches, lvls = lax.axis_size("patch"), lax.axis_size("lvl")
    if patches > most_direct:
        return [lax.all_gather(senders, ("patch", "lvl"), axis=0, tiled=True)], others
    near = [[senders] + [shifted(senders, "lvl", t) for t in range(1, lvls)]]
    pieces = [shifted(senders, "patch", s) for s in range(1, patches)]
    pieces, others = lax.optimization_barrier((pieces, others))
    near += [[piece] + [shifted(piece, "lvl", t) for t in range(1, lvls)] for piece in pieces]
    return [row[t] for t in range(lvls) for row in near], others


def held(values, event):
    return lax.optimization_barrier((values, event))[0]


def over_sub(pack):
    return [shifted(pack, "sub", s) for s in range(1, lax.axis_size("sub"))]


def partners(axis):
    if axis == "parts":
        return lax.axis_index(axis), lax.axis_size(axis)
    count = 2 if lax.axis_size(axis) % 2 == 0 else 1
    return lax.rem(lax.axis_index(axis), count), count


def over_partners(share_list, axis):
    size, count = lax.axis_size(axis), partners(axis)[1]
    return [
        [
            lax.ppermute(share, axis, [(i, i - i % count + (i + p) % count) for i in range(size)])
            for p in range(1, count)
        ]
        for share in share_list
    ]


def over_lvl(shares):
    return [
        [share] + [shifted(share, "lvl", t) for t in range(1, lax.axis_size("lvl"))]
        for share in shares
    ]


def all_shares(shares, others):
    near = over_lvl(shares)
    far = [over_lvl(row) for row in others]
    return [x for first, row in zip(near, far) for x in (first + [y for group in row for y in group])]


def body(
    node_states,
    coarse_states,
    children,
    down_sources,
    bottom_links,
    coarse_links,
    upward_sender,
    upward_receiver,
    upward_bias,
    upward_output,
    upward_gain,
    coarse_sender,
    coarse_receiver,
    coarse_bias,
    coarse_output,
    coarse_gain,
    downward_sender,
    downward_receiver,
    downward_bias,
    downward_output,
    downward_gain,
    bottom_sender,
    bottom_receiver,
    bottom_bias,
    bottom_output,
    bottom_gain,
):
    rows, latent = node_states.shape
    blocks = coarse_states.shape[0]
    width = upward_sender.shape[1]
    subs = lax.axis_size("sub")
    hidden = width * subs
    rim = rows // 4
    into = like((subs, 3 * latent, width), bf16)
    out_of = like((3 * hidden, latent), bf16)
    bias_rows = like((subs, 8, width))

    columns = latent // width
    lvls = lax.axis_size("lvl")

    def pack(axis):
        count = shares(axis)[1]
        return like((2 * latent // count + width // count * columns + 8, width))

    (part,) = call(
        upward_kernel,
        [like((blocks, latent))],
        [
            node_states, coarse_states, upward_sender, upward_receiver, upward_output,
            children.T, upward_bias[None],
        ],
        6 * rows * latent * width,
        [
            pltpu.VMEM((rows, latent), f32),
            pltpu.VMEM((blocks, latent), f32),
            pltpu.VMEM((latent, width), f32),
            pltpu.VMEM((latent, width), f32),
            pltpu.VMEM((width, latent), f32),
            pltpu.VMEM((2 * rows, width), bf16),
            pltpu.SemaphoreType.DMA((17,)),
        ],
        far=range(5),
        limit=tight_limit,
    )
    parts = sub_parts(part)
    down_own = (downward_sender, downward_receiver, downward_output, downward_bias[None])
    bottom_own = (bottom_sender, bottom_receiver, bottom_output, bottom_bias[None])
    (down_pack,), (bottom_pack,) = (
        call(
            functools.partial(share_kernel, axis),
            [pack(axis)],
            own,
            latent,
            [pltpu.SemaphoreType.DMA((3 + columns,))],
            far=range(4),
            limit=tight_limit,
        )
        for axis, own in (("parts", down_own), ("patch", bottom_own))
    )
    gains, biases = call(
        stack_kernel,
        [like((4, latent)), like((3, width))],
        [
            upward_gain[None], coarse_gain[None], downward_gain[None], bottom_gain[None],
            coarse_bias[None], downward_bias[None], bottom_bias[None], part,
        ],
        latent * hidden,
        unread=1,
    )
    down_near, bottom_near = over_sub(down_pack), over_sub(bottom_pack)
    coarse_up, senders, receivers = call(
        functools.partial(coarse_project_kernel, len(parts)),
        [like((blocks, latent)), like((blocks, width)), like((blocks, width))],
        [*parts, coarse_states, gains, biases, coarse_sender, coarse_receiver],
        12 * blocks * latent * width,
    )
    patches = lax.axis_size("patch")
    names = blocks * patches * lvls
    picks, bottom_picks = call(
        functools.partial(picks_kernel, rim, patches, blocks),
        [like((coarse_links.size, 2 * names), bf16), like((bottom_links.size, 6 * rim), bf16)],
        [coarse_links.T, bottom_links.T, senders],
        10**11,
        unread=1,
    )
    pieces, (picks, bottom_picks, down_near) = coarse_pieces(
        senders, (picks, bottom_picks, down_near)
    )
    down_far = over_partners(down_near, "parts")
    (part,) = call(
        functools.partial(coarse_kernel, len(pieces)),
        [like((blocks, latent))],
        [*pieces, picks, receivers, coarse_output],
        4 * coarse_links.size * names * width,
    )
    parts = sub_parts(part)
    bottom_near = held(bottom_near, part)
    bottom_far = over_partners(bottom_near, "patch")
    down_packs = all_shares(*held((down_near, down_far), parts[-1]))
    receivers, ws, wo = call(
        functools.partial(down_weights_kernel, len(down_packs)),
        [like((rows, hidden)), into, out_of],
        [node_states, downward_sender, downward_receiver, biases, downward_output, *down_packs, part, *(x for row in bottom_far for x in row)],
        6 * rows * latent * hidden,
        [pltpu.VMEM((subs, 3 * latent, width), bf16), pltpu.VMEM((subs, 8, width), f32)],
        unread=1 + sum(map(len, bottom_far)),
    )
    new_coarse, senders, head, tail = call(
        functools.partial(down_edge_kernel, len(parts), rim),
        [like((blocks, latent)), like((2 * blocks, hidden), bf16), like((rim, latent)), like((rim, latent))],
        [*parts, coarse_up, gains, node_states, receivers, down_sources.T, ws, wo],
        6 * 2 * rim * latent * hidden,
        [pltpu.VMEM((blocks, latent), f32), pltpu.SemaphoreType.DMA],
        far_outs=(0,),
    )
    ring = ("patch", "lvl")
    before, after = shifted(tail, ring, 1), shifted(head, ring, -1)
    (middle,) = call(
        functools.partial(down_middle_kernel, rim),
        [like((rows - 2 * rim, latent))],
        [node_states, receivers, down_sources.T, senders, wo, gains],
        6 * (rows - 2 * rim) * latent * hidden,
    )

    bottom_near, bottom_far = held((bottom_near, bottom_far), head)
    bottom_packs = all_shares(bottom_near, bottom_far)
    ws, wr, wo, bias = call(
        functools.partial(bottom_weights_kernel, len(bottom_packs)),
        [into, into, out_of, bias_rows],
        [bottom_sender, bottom_receiver, biases, bottom_output, *bottom_packs],
        latent * hidden,
    )
    receivers, inner, ahead = call(
        functools.partial(bottom_middle_kernel, rim),
        [like((rows, hidden)), like((rows - 2 * rim, latent)), like((bottom_links.size // (rows // rim) * 2, hidden))],
        [head, middle, tail, bottom_picks, ws, wr, wo, bias, gains],
        (12 * rows + 12 * rows) * latent * hidden,
        [pltpu.VMEM((2 * rows, hidden), bf16)],
    )
    (new_nodes,) = call(
        functools.partial(bottom_edge_kernel, rim),
        [like((rows, latent))],
        [before, after, head, tail, inner, ahead, bottom_picks, receivers, ws, wo, gains],
        24 * rim * latent * hidden,
        [
            pltpu.VMEM((4 * rim, hidden), bf16),
            pltpu.VMEM((2 * rim, latent), f32),
            pltpu.SemaphoreType.DMA((3,)),
        ],
        far_outs=(0,),
    )
    return (new_nodes, new_coarse)


def solution(mesh):
    split_rows, level_rows = P(("parts", "patch", "lvl"), None), P(("patch", "lvl"), None)
    weights = (P(None, "sub"), P(None, "sub"), P("sub"), P("sub", None), P())
    in_specs = (split_rows, split_rows, *([level_rows] * 4), *(weights * 4))
    out_specs = (split_rows, split_rows)
    return jax.shard_map(body, mesh=mesh, in_specs=in_specs, out_specs=out_specs, check_vma=False)
```

```python
import functools

import jax
import jax.numpy as jnp
from jax import lax
from jax.experimental import pallas as pl
from jax.experimental.pallas import tpu as pltpu
from jax.sharding import PartitionSpec as P

epsilon = 1e-05
f32 = jnp.float32
bf16 = jnp.bfloat16
limit_bytes = 12 * 1024 * 1024
share_limit = 58 * 1000 * 1000
up_limit = 50 * 1000 * 1000
most_direct = 4


def split(values):
    high = values.astype(bf16)
    return high, (values - high.astype(f32)).astype(bf16)


def dot(a, b):
    return jnp.dot(a, b, preferred_element_type=f32)


def threefold(values):
    high, low = split(values)
    return jnp.concatenate([high, high, low], axis=1)


def stacked(weights):
    high, low = split(weights)
    return jnp.concatenate([high, low, high], axis=0)


def dot3(a, b_stacked):
    return dot(threefold(a), b_stacked)


def normed(values):
    center = values - jnp.mean(values, axis=-1, keepdims=True)
    spread = jnp.mean(center * center, axis=-1, keepdims=True)
    return center * lax.rsqrt(spread + epsilon)


def upright(rows):
    count, size = rows.shape
    tall, wide = -count % 8, -size % 128
    if tall:
        rows = jnp.concatenate([rows, jnp.zeros((tall, size), rows.dtype)], axis=0)
    if wide:
        rows = jnp.concatenate([rows, jnp.zeros((count + tall, wide), rows.dtype)], axis=1)
    return jnp.transpose(rows)[:size, :count]


def one_hot(wanted, names):
    return jnp.concatenate(
        [
            jnp.where(wanted[:, k : k + 1] == names, 1.0, 0.0).astype(bf16)
            for k in range(wanted.shape[1])
        ],
        axis=0,
    )


def silu_sum(picked, halves, count):
    rows = halves.shape[0]
    total = None
    for k in range(count):
        u = picked[k * rows : (k + 1) * rows] + halves
        term = u + u * jnp.tanh(u)
        total = term if total is None else total + term
    return total


def added(refs):
    total = refs[0][...]
    for ref in refs[1:]:
        total = total + ref[...]
    return total


def started(copies, sems):
    moves = [pltpu.make_async_copy(a, b, sems.at[i]) for i, (a, b) in enumerate(copies)]
    for move in moves:
        move.start()
    return moves


def upward_kernel(nodes, coarse, children, ws, wr, bias, wo, part):
    wanted = upright(children[...])
    names = lax.broadcasted_iota(jnp.int32, (wanted.shape[0], nodes.shape[0]), 1)
    picks = one_hot(wanted, names)
    senders = jnp.concatenate(split(0.5 * dot3(nodes[...], stacked(ws[...]))), axis=0)
    receivers = 0.5 * (dot3(coarse[...], stacked(wr[...])) + bias[...])
    picked = dot(jnp.concatenate([picks, picks], axis=1), senders)
    hidden = silu_sum(picked, receivers, wanted.shape[1])
    part[...] = dot3(hidden, stacked(wo[...]))


def stack_kernel(*refs):
    params, (gains, biases) = refs[:7], refs[7:]
    for i in range(4):
        gains[i : i + 1] = params[i][...]
    for i in range(3):
        biases[i : i + 1] = params[4 + i][...]


def share_kernel(plan, *refs):
    packs, sems = refs[-1 - len(plan) : -1], refs[-1]
    copies, first = [], 0
    for (count, axis), pack in zip(plan, packs):
        copies += share_copies(refs[first : first + count], pack, axis)
        first += count
    for move in started(copies, sems):
        move.wait()


def shares(axis):
    lvls = lax.axis_size("lvl")
    place, count = partners(axis)
    return place * lvls + lax.axis_index("lvl"), count * lvls


def share_copies(sources, pack, axis):
    mine, count = shares(axis)
    width = pack.shape[1]
    copies, at = [], 0
    for source in sources:
        rows = source.shape[0] // count
        if source.shape[0] == 1:
            copies.append((source, pack.at[pl.ds(at, 1)]))
            at += 8
            continue
        strip = pl.ds(pl.multiple_of(mine * rows, rows), rows)
        for j in range(source.shape[1] // width):
            copies.append((source.at[strip, pl.ds(j * width, width)], pack.at[pl.ds(at, rows)]))
            at += rows
    return copies


def picks_kernel(rim, patches, blocks, coarse_links, bottom_links, coarse_picks, bottom_picks):
    wanted = upright(coarse_links[...])
    rows = wanted.shape[0]
    lvls = lax.axis_size("lvl")
    half = coarse_picks.shape[1] // 2
    column = lax.broadcasted_iota(jnp.int32, (rows, blocks), 1)
    for t in range(lvls):
        for s in range(patches):
            patch = lax.rem(lax.axis_index("patch") + patches - s, patches)
            lvl = lax.rem(lax.axis_index("lvl") + lvls - t, lvls)
            first = (patch * lvls + lvl) * blocks
            at = (t * patches + s) * blocks
            piece = one_hot(wanted, column + first)
            coarse_picks[:, at : at + blocks] = piece
            coarse_picks[:, half + at : half + at + blocks] = piece
    wanted = upright(bottom_links[...])
    size = rim * wanted.shape[1]
    names = lax.broadcasted_iota(jnp.int32, (rim, 3 * rim), 1)
    for i in range(wanted.shape[0] // rim):
        picks = one_hot(wanted[i * rim : (i + 1) * rim], names + i * rim)
        for j in range(6):
            piece = picks[:, j // 2 * rim : (j // 2 + 1) * rim]
            bottom_picks[i * size : (i + 1) * size, j * rim : (j + 1) * rim] = piece


def coarse_project_kernel(count, *refs):
    parts, refs = refs[:count], refs[count:]
    coarse, gains, biases, ws, wr, updated, senders, receivers = refs
    rows = coarse[...] + gains[0:1] * normed(added(parts))
    updated[...] = rows
    senders[...] = 0.5 * dot3(rows, stacked(ws[...]))
    receivers[...] = 0.5 * (dot3(rows, stacked(wr[...])) + biases[0:1])


def coarse_kernel(count, *refs):
    pieces, (all_picks, receivers, wo) = refs[:count], refs[count : count + 3]
    part = refs[-1]
    senders = jnp.concatenate([piece[...] for piece in pieces], axis=0)
    picked = dot(all_picks[...], jnp.concatenate(split(senders), axis=0))
    hidden = silu_sum(picked, receivers[...], all_picks.shape[0] // receivers.shape[0])
    part[...] = dot3(hidden, stacked(wo[...]))


def fetched_shares(packs, axis):
    subs, lvls = lax.axis_size("sub"), lax.axis_size("lvl")
    sub, lvl = lax.axis_index("sub"), lax.axis_index("lvl")
    place, count = partners(axis)
    left = iter(packs)
    for s in range(1, subs):
        for p in range(count):
            for t in range(lvls):
                mine = lax.rem(place + count - p, count) * lvls + lax.rem(lvl + lvls - t, lvls)
                yield next(left), lax.rem(sub + subs - s, subs), mine, p == 0 and t == 0


def put_stacked(values, out, first, columns):
    high, low = split(values)
    depth, rows = out.shape[0] // 3, values.shape[0]
    for i, half in enumerate((high, low, high)):
        out[pl.ds(pl.multiple_of(i * depth + first, 16), rows), columns] = half


def collect_in(own, packs, axis, at, out):
    everything = slice(0, own.shape[1])
    put_stacked(own[...], out.at[lax.axis_index("sub")], 0, everything)
    share = own.shape[0] // shares(axis)[1]
    for pack, block, mine, _ in fetched_shares(packs, axis):
        put_stacked(pack[at : at + share, :], out.at[block], mine * share, everything)


def collect_out(own, packs, axis, at, out):
    width, latent = own.shape
    put_stacked(own[...], out, lax.axis_index("sub") * width, slice(0, latent))
    thin = width // shares(axis)[1]
    for pack, block, mine, _ in fetched_shares(packs, axis):
        for j in range(latent // width):
            part = pack[at + j * thin : at + (j + 1) * thin, :]
            put_stacked(part, out, block * width + mine * thin, slice(j * width, (j + 1) * width))


def collect_bias(own, packs, axis, at, out):
    out[lax.axis_index("sub")] = jnp.broadcast_to(own, (8, own.shape[1]))
    for pack, block, _, whole_row in fetched_shares(packs, axis):
        if whole_row:
            out[block] = jnp.broadcast_to(pack[at : at + 1, :], (8, own.shape[1]))


def down_weights_kernel(counts, nodes, ws, wr, biases, wo, *refs):
    first, rest = refs[: counts[0]], refs[counts[0] : sum(counts)]
    receivers, ws_all, wo_all, wr_all, bias_all = refs[sum(counts) :]
    width = ws.shape[1]
    share = ws.shape[0] // shares("parts")[1]
    collect_in(ws, first, "parts", 0, ws_all)
    collect_in(wr, first, "parts", share, wr_all)
    collect_bias(biases[1:2], first, "parts", 2 * share, bias_all)
    collect_out(wo, rest, None, 0, wo_all)
    states = threefold(nodes[...])
    for g in range(wr_all.shape[0]):
        receivers[:, g * width : (g + 1) * width] = 0.5 * (dot(states, wr_all[g]) + bias_all[g][0:1])


def bottom_weights_kernel(count, ws, wr, biases, wo, *refs):
    packs, (ws_all, wr_all, wo_all, bias_all) = refs[:count], refs[count:]
    share = ws.shape[0] // shares("patch")[1]
    collect_in(ws, packs, "patch", 0, ws_all)
    collect_in(wr, packs, "patch", share, wr_all)
    collect_out(wo, packs, "patch", 2 * share, wo_all)
    collect_bias(biases[2:3], packs, "patch", 3 * share, bias_all)


def down_rows(nodes, receivers, sources, senders, wo, gain):
    blocks = senders.shape[0] // 2
    column = lax.broadcasted_iota(jnp.int32, (nodes.shape[0], 2 * blocks), 1)
    names = jnp.where(column < blocks, column, column - blocks)
    picked = dot(one_hot(sources, names), senders)
    hidden = silu_sum(picked, receivers, sources.shape[1])
    return nodes + gain * normed(dot3(hidden, wo))


def down_edge_kernel(count, rim, *refs):
    parts, refs = refs[:count], refs[count:]
    coarse_up, gains, nodes, receivers, sources, ws, wo = refs[:7]
    new_coarse, senders, head, tail, held_here, sem = refs[7:]
    rows = coarse_up[...] + gains[1:2] * normed(added(parts))
    held_here[...] = rows
    move = pltpu.make_async_copy(held_here, new_coarse, sem)
    move.start()
    blocks = rows.shape[0]
    width = ws.shape[2]
    left = threefold(rows)
    for g in range(ws.shape[0]):
        columns = slice(g * width, (g + 1) * width)
        high, low = split(0.5 * dot(left, ws[g]))
        senders[0:blocks, columns] = high
        senders[blocks : 2 * blocks, columns] = low
    total = nodes.shape[0]
    wanted = upright(sources[...])
    for out, place in ((head, slice(0, rim)), (tail, slice(total - rim, total))):
        out[...] = down_rows(
            nodes[place], receivers[place], wanted[place], senders[...], wo[...], gains[2:3]
        )
    move.wait()


def down_middle_kernel(rim, nodes, receivers, sources, senders, wo, gains, middle):
    place = slice(rim, nodes.shape[0] - rim)
    middle[...] = down_rows(
        nodes[place], receivers[place], upright(sources[...])[place], senders[...], wo[...], gains[2:3]
    )


def bottom_rows(nodes, receivers, picks, senders, wo, gain, ahead=None):
    half = senders.shape[1] // 2
    hidden = []
    for place in (slice(0, half), slice(half, 2 * half)):
        picked = dot(picks, senders[:, place])
        if ahead is not None:
            picked = picked + ahead[:, place]
        hidden.append(silu_sum(picked, receivers[:, place], picks.shape[0] // nodes.shape[0]))
    return nodes + gain * normed(dot3(jnp.concatenate(hidden, axis=1), wo))


def put_strips(values, rim, out, columns):
    high, low = split(values)
    for i in range(values.shape[0] // rim):
        strip = slice(i * rim, (i + 1) * rim)
        out[2 * i * rim : (2 * i + 1) * rim, columns] = high[strip]
        out[(2 * i + 1) * rim : (2 * i + 2) * rim, columns] = low[strip]


def bottom_middle_kernel(rim, head, middle, tail, picks, ws, wr, wo, bias, gains, receivers, out, ahead, senders):
    nodes = jnp.concatenate([head[...], middle[...], tail[...]], axis=0)
    left = threefold(nodes)
    width = ws.shape[2]
    for g in range(ws.shape[0]):
        columns = slice(g * width, (g + 1) * width)
        put_strips(0.5 * dot(left, ws[g]), rim, senders, columns)
        receivers[:, columns] = 0.5 * (dot(left, wr[g]) + bias[g][0:1])
    total = nodes.shape[0]
    size = picks.shape[0] * rim // total
    for i in range(1, total // rim - 1):
        place = slice(i * rim, (i + 1) * rim)
        inner = slice((i - 1) * rim, i * rim)
        out[inner, :] = bottom_rows(
            middle[inner], receivers[place], picks[i * size : (i + 1) * size],
            senders[2 * (i - 1) * rim : 2 * (i + 2) * rim, :], wo[...], gains[3:4],
        )
    near, last = senders.shape[0], picks.shape[0] - size
    ahead[0:size, :] = dot(picks[0:size, 2 * rim : 6 * rim], senders[0 : 4 * rim, :])
    ahead[size : 2 * size, :] = dot(
        picks[last : last + size, 0 : 4 * rim], senders[near - 4 * rim : near, :]
    )


def bottom_edge_kernel(rim, before, after, head, tail, inner, ahead, picks, receivers, ws, wo, gains, out, outer, strips, sems):
    total = receivers.shape[0]
    size = picks.shape[0] * rim // total
    moves = [pltpu.make_async_copy(inner, out.at[pl.ds(rim, total - 2 * rim)], sems.at[0])]
    moves[0].start()
    left = threefold(jnp.concatenate([before[...], after[...]], axis=0))
    width = ws.shape[2]
    for g in range(ws.shape[0]):
        put_strips(0.5 * dot(left, ws[g]), rim, outer, slice(g * width, (g + 1) * width))
    for side, nodes in enumerate((head, tail)):
        first, column = (0, 0) if side == 0 else (total - rim, 4 * rim)
        place = slice(first, first + rim)
        chosen = picks[first // rim * size : (first // rim + 1) * size, column : column + 2 * rim]
        strips[side * rim : (side + 1) * rim, :] = bottom_rows(
            nodes[...], receivers[place], chosen, outer[2 * side * rim : 2 * (side + 1) * rim, :],
            wo[...], gains[3:4], ahead[side * size : (side + 1) * size, :],
        )
        strip = strips.at[pl.ds(side * rim, rim)]
        moves.append(pltpu.make_async_copy(strip, out.at[pl.ds(first, rim)], sems.at[1 + side]))
        moves[-1].start()
    for move in moves:
        move.wait()


whole = pl.BlockSpec(memory_space=pltpu.VMEM)
away = pl.BlockSpec(memory_space=pl.ANY)


def call(kernel, outs, operands, flops, scratch=(), far=(), far_outs=(), unread=0, limit=limit_bytes):
    moved = sum(x.size * x.dtype.itemsize for x in (*outs, *operands))
    read = len(operands) - unread
    specs = [away if i in far else whole for i in range(read)] + [away] * unread
    return pl.pallas_call(
        (lambda *refs: kernel(*refs[:read], *refs[read + unread :])) if unread else kernel,
        out_shape=tuple(outs),
        in_specs=specs,
        out_specs=tuple(away if i in far_outs else whole for i in range(len(outs))),
        scratch_shapes=list(scratch),
        compiler_params=pltpu.CompilerParams(vmem_limit_bytes=limit),
        cost_estimate=pl.CostEstimate(flops=int(flops), bytes_accessed=moved, transcendentals=0),
    )(*operands)


def like(shape, kind=f32):
    return jax.ShapeDtypeStruct(tuple(shape), kind)


def shifted(values, axis, step):
    count = lax.axis_size(axis)
    return lax.ppermute(values, axis, [(i, (i + step) % count) for i in range(count)])


def sub_parts(part):
    if lax.axis_size("sub") == 2:
        return [part, shifted(part, "sub", 1)]
    return [lax.psum(part, "sub")]


def coarse_pieces(senders, others):
    patches, lvls = lax.axis_size("patch"), lax.axis_size("lvl")
    if patches > most_direct:
        return [lax.all_gather(senders, ("patch", "lvl"), axis=0, tiled=True)], others
    near = [[senders] + [shifted(senders, "lvl", t) for t in range(1, lvls)]]
    pieces = [shifted(senders, "patch", s) for s in range(1, patches)]
    pieces, others = lax.optimization_barrier((pieces, others))
    near += [[piece] + [shifted(piece, "lvl", t) for t in range(1, lvls)] for piece in pieces]
    return [row[t] for t in range(lvls) for row in near], others


def held(values, event):
    return lax.optimization_barrier((values, event))[0]


def over_sub(pack):
    return [shifted(pack, "sub", s) for s in range(1, lax.axis_size("sub"))]


def partners(axis):
    if axis is None:
        return 0, 1
    if axis == "parts":
        return lax.axis_index(axis), lax.axis_size(axis)
    count = 2 if lax.axis_size(axis) % 2 == 0 else 1
    return lax.rem(lax.axis_index(axis), count), count


def over_partners(share_list, axis):
    size, count = lax.axis_size(axis), partners(axis)[1]
    return [
        [
            lax.ppermute(share, axis, [(i, i - i % count + (i + p) % count) for i in range(size)])
            for p in range(1, count)
        ]
        for share in share_list
    ]


def over_lvl(shares):
    return [
        [share] + [shifted(share, "lvl", t) for t in range(1, lax.axis_size("lvl"))]
        for share in shares
    ]


def all_shares(shares, others):
    near = over_lvl(shares)
    far = [over_lvl(row) for row in others]
    return [x for first, row in zip(near, far) for x in (first + [y for group in row for y in group])]


def body(
    node_states,
    coarse_states,
    children,
    down_sources,
    bottom_links,
    coarse_links,
    upward_sender,
    upward_receiver,
    upward_bias,
    upward_output,
    upward_gain,
    coarse_sender,
    coarse_receiver,
    coarse_bias,
    coarse_output,
    coarse_gain,
    downward_sender,
    downward_receiver,
    downward_bias,
    downward_output,
    downward_gain,
    bottom_sender,
    bottom_receiver,
    bottom_bias,
    bottom_output,
    bottom_gain,
):
    rows, latent = node_states.shape
    blocks = coarse_states.shape[0]
    width = upward_sender.shape[1]
    subs = lax.axis_size("sub")
    hidden = width * subs
    rim = rows // 4
    into = like((subs, 3 * latent, width), bf16)
    out_of = like((3 * hidden, latent), bf16)
    bias_rows = like((subs, 8, width))

    columns = latent // width
    lvls = lax.axis_size("lvl")

    def pack(axis, into, out_of, bias):
        count = shares(axis)[1]
        return like((into * latent // count + out_of * (width // count) * columns + 8 * bias, width))

    (part,) = call(
        upward_kernel,
        [like((blocks, latent))],
        [
            node_states, coarse_states, children.T, upward_sender, upward_receiver,
            upward_bias[None], upward_output,
        ],
        6 * rows * latent * width,
        limit=up_limit,
    )
    parts = sub_parts(part)
    (first_pack,) = call(
        functools.partial(share_kernel, ((3, "parts"),)),
        [pack("parts", 2, 0, 1)],
        [downward_sender, downward_receiver, downward_bias[None]],
        10**9,
        [pltpu.SemaphoreType.DMA((3,))],
        far=range(3),
        limit=share_limit,
    )
    down_pack, bottom_pack = call(
        functools.partial(share_kernel, ((1, None), (4, "patch"))),
        [pack(None, 0, 1, 0), pack("patch", 2, 1, 1)],
        [downward_output, bottom_sender, bottom_receiver, bottom_output, bottom_bias[None]],
        10**9,
        [pltpu.SemaphoreType.DMA((3 + 2 * columns,))],
        far=range(5),
        limit=share_limit,
    )
    gains, biases = call(
        stack_kernel,
        [like((4, latent)), like((3, width))],
        [
            upward_gain[None], coarse_gain[None], downward_gain[None], bottom_gain[None],
            coarse_bias[None], downward_bias[None], bottom_bias[None], part,
        ],
        latent * hidden,
        unread=1,
    )
    first_near = held(over_sub(first_pack), parts[-1])
    down_near, bottom_near = over_sub(down_pack), over_sub(bottom_pack)
    first_far = over_partners(first_near, "parts")
    coarse_up, senders, receivers = call(
        functools.partial(coarse_project_kernel, len(parts)),
        [like((blocks, latent)), like((blocks, width)), like((blocks, width))],
        [*parts, coarse_states, gains, biases, coarse_sender, coarse_receiver],
        12 * blocks * latent * width,
    )
    patches = lax.axis_size("patch")
    names = blocks * patches * lvls
    picks, bottom_picks = call(
        functools.partial(picks_kernel, rim, patches, blocks),
        [like((coarse_links.size, 2 * names), bf16), like((bottom_links.size, 6 * rim), bf16)],
        [coarse_links.T, bottom_links.T, senders],
        coarse_links.size * names,
        unread=1,
    )
    pieces, (picks, bottom_picks, first_near, first_far, down_near, bottom_near) = coarse_pieces(
        senders, (picks, bottom_picks, first_near, first_far, down_near, bottom_near)
    )
    first_packs = all_shares(first_near, first_far)
    down_packs = [pack for row in over_lvl(down_near) for pack in row]
    bottom_far = over_partners(bottom_near, "patch")
    (part,) = call(
        functools.partial(coarse_kernel, len(pieces)),
        [like((blocks, latent))],
        [*pieces, picks, receivers, coarse_output],
        4 * coarse_links.size * names * width,
    )
    parts = sub_parts(part)
    receivers, ws, wo = call(
        functools.partial(down_weights_kernel, (len(first_packs), len(down_packs))),
        [like((rows, hidden)), into, out_of],
        [node_states, downward_sender, downward_receiver, biases, downward_output, *first_packs, *down_packs, part],
        6 * rows * latent * hidden,
        [pltpu.VMEM((subs, 3 * latent, width), bf16), pltpu.VMEM((subs, 8, width), f32)],
        unread=1,
    )
    new_coarse, senders, head, tail = call(
        functools.partial(down_edge_kernel, len(parts), rim),
        [like((blocks, latent)), like((2 * blocks, hidden), bf16), like((rim, latent)), like((rim, latent))],
        [*parts, coarse_up, gains, node_states, receivers, down_sources.T, ws, wo],
        6 * 2 * rim * latent * hidden,
        [pltpu.VMEM((blocks, latent), f32), pltpu.SemaphoreType.DMA],
        far_outs=(0,),
    )
    ring = ("patch", "lvl")
    before, after = shifted(tail, ring, 1), shifted(head, ring, -1)
    (middle,) = call(
        functools.partial(down_middle_kernel, rim),
        [like((rows - 2 * rim, latent))],
        [node_states, receivers, down_sources.T, senders, wo, gains],
        6 * (rows - 2 * rim) * latent * hidden,
    )

    bottom_near, bottom_far = held((bottom_near, bottom_far), head)
    bottom_packs = all_shares(bottom_near, bottom_far)
    ws, wr, wo, bias = call(
        functools.partial(bottom_weights_kernel, len(bottom_packs)),
        [into, into, out_of, bias_rows],
        [bottom_sender, bottom_receiver, biases, bottom_output, *bottom_packs],
        latent * hidden,
    )
    receivers, inner, ahead = call(
        functools.partial(bottom_middle_kernel, rim),
        [like((rows, hidden)), like((rows - 2 * rim, latent)), like((bottom_links.size // (rows // rim) * 2, hidden))],
        [head, middle, tail, bottom_picks, ws, wr, wo, bias, gains],
        (12 * rows + 12 * rows) * latent * hidden,
        [pltpu.VMEM((2 * rows, hidden), bf16)],
    )
    (new_nodes,) = call(
        functools.partial(bottom_edge_kernel, rim),
        [like((rows, latent))],
        [before, after, head, tail, inner, ahead, bottom_picks, receivers, ws, wo, gains],
        24 * rim * latent * hidden,
        [
            pltpu.VMEM((4 * rim, hidden), bf16),
            pltpu.VMEM((2 * rim, latent), f32),
            pltpu.SemaphoreType.DMA((3,)),
        ],
        far_outs=(0,),
    )
    return (new_nodes, new_coarse)


def solution(mesh):
    split_rows, level_rows = P(("parts", "patch", "lvl"), None), P(("patch", "lvl"), None)
    weights = (P(None, "sub"), P(None, "sub"), P("sub"), P("sub", None), P())
    in_specs = (split_rows, split_rows, *([level_rows] * 4), *(weights * 4))
    out_specs = (split_rows, split_rows)
    return jax.shard_map(body, mesh=mesh, in_specs=in_specs, out_specs=out_specs, check_vma=False)
```

```python
import functools

import jax
import jax.numpy as jnp
from jax import lax
from jax.experimental import pallas as pl
from jax.experimental.pallas import tpu as pltpu
from jax.sharding import PartitionSpec as P

epsilon = 1e-05
f32 = jnp.float32
bf16 = jnp.bfloat16
limit_bytes = 12 * 1024 * 1024
share_limit = 58 * 1000 * 1000
up_limit = 50 * 1000 * 1000
most_direct = 4


def split(values):
    high = values.astype(bf16)
    return high, (values - high.astype(f32)).astype(bf16)


def dot(a, b):
    return jnp.dot(a, b, preferred_element_type=f32)


def threefold(values):
    high, low = split(values)
    return jnp.concatenate([high, high, low], axis=1)


def stacked(weights):
    high, low = split(weights)
    return jnp.concatenate([high, low, high], axis=0)


def dot3(a, b_stacked):
    return dot(threefold(a), b_stacked)


def normed(values):
    center = values - jnp.mean(values, axis=-1, keepdims=True)
    spread = jnp.mean(center * center, axis=-1, keepdims=True)
    return center * lax.rsqrt(spread + epsilon)


def upright(rows):
    count, size = rows.shape
    tall, wide = -count % 8, -size % 128
    if tall:
        rows = jnp.concatenate([rows, jnp.zeros((tall, size), rows.dtype)], axis=0)
    if wide:
        rows = jnp.concatenate([rows, jnp.zeros((count + tall, wide), rows.dtype)], axis=1)
    return jnp.transpose(rows)[:size, :count]


def one_hot(wanted, names):
    return jnp.concatenate(
        [
            jnp.where(wanted[:, k : k + 1] == names, 1.0, 0.0).astype(bf16)
            for k in range(wanted.shape[1])
        ],
        axis=0,
    )


def silu_sum(picked, halves, count):
    rows = halves.shape[0]
    total = None
    for k in range(count):
        u = picked[k * rows : (k + 1) * rows] + halves
        term = u + u * jnp.tanh(u)
        total = term if total is None else total + term
    return total


def added(refs):
    total = refs[0][...]
    for ref in refs[1:]:
        total = total + ref[...]
    return total


def started(copies, sems):
    moves = [pltpu.make_async_copy(a, b, sems.at[i]) for i, (a, b) in enumerate(copies)]
    for move in moves:
        move.start()
    return moves


def upward_kernel(nodes, coarse, children, ws, wr, bias, wo, part):
    wanted = upright(children[...])
    names = lax.broadcasted_iota(jnp.int32, (wanted.shape[0], nodes.shape[0]), 1)
    picks = one_hot(wanted, names)
    senders = jnp.concatenate(split(0.5 * dot3(nodes[...], stacked(ws[...]))), axis=0)
    receivers = 0.5 * (dot3(coarse[...], stacked(wr[...])) + bias[...])
    picked = dot(jnp.concatenate([picks, picks], axis=1), senders)
    hidden = silu_sum(picked, receivers, wanted.shape[1])
    part[...] = dot3(hidden, stacked(wo[...]))


def stack_kernel(*refs):
    params, (gains, biases) = refs[:7], refs[7:]
    for i in range(4):
        gains[i : i + 1] = params[i][...]
    for i in range(3):
        biases[i : i + 1] = params[4 + i][...]


def share_kernel(axis, *refs):
    for move in started(share_copies(refs[:4], refs[4], axis), refs[5]):
        move.wait()


def shares(axis):
    lvls = lax.axis_size("lvl")
    place, count = partners(axis)
    return place * lvls + lax.axis_index("lvl"), count * lvls


def share_copies(sources, pack, axis):
    mine, count = shares(axis)
    width = pack.shape[1]
    copies, at = [], 0
    for source in sources:
        rows = source.shape[0] // count
        if source.shape[0] == 1:
            copies.append((source, pack.at[pl.ds(at, 1)]))
            at += 8
            continue
        strip = pl.ds(pl.multiple_of(mine * rows, rows), rows)
        for j in range(source.shape[1] // width):
            copies.append((source.at[strip, pl.ds(j * width, width)], pack.at[pl.ds(at, rows)]))
            at += rows
    return copies


def picks_kernel(rim, patches, blocks, coarse_links, bottom_links, coarse_picks, bottom_picks):
    wanted = upright(coarse_links[...])
    rows = wanted.shape[0]
    lvls = lax.axis_size("lvl")
    half = coarse_picks.shape[1] // 2
    column = lax.broadcasted_iota(jnp.int32, (rows, blocks), 1)
    for t in range(lvls):
        for s in range(patches):
            patch = lax.rem(lax.axis_index("patch") + patches - s, patches)
            lvl = lax.rem(lax.axis_index("lvl") + lvls - t, lvls)
            first = (patch * lvls + lvl) * blocks
            at = (t * patches + s) * blocks
            piece = one_hot(wanted, column + first)
            coarse_picks[:, at : at + blocks] = piece
            coarse_picks[:, half + at : half + at + blocks] = piece
    wanted = upright(bottom_links[...])
    size = rim * wanted.shape[1]
    names = lax.broadcasted_iota(jnp.int32, (rim, 3 * rim), 1)
    for i in range(wanted.shape[0] // rim):
        picks = one_hot(wanted[i * rim : (i + 1) * rim], names + i * rim)
        for j in range(6):
            piece = picks[:, j // 2 * rim : (j // 2 + 1) * rim]
            bottom_picks[i * size : (i + 1) * size, j * rim : (j + 1) * rim] = piece


def join_kernel(*refs):
    rows = refs[0].shape[0]
    for i, piece in enumerate(refs[:-1]):
        refs[-1][i * rows : (i + 1) * rows] = piece[...]


def coarse_project_kernel(count, *refs):
    parts, refs = refs[:count], refs[count:]
    coarse, gains, biases, ws, wr, updated, senders, receivers = refs
    rows = coarse[...] + gains[0:1] * normed(added(parts))
    updated[...] = rows
    senders[...] = 0.5 * dot3(rows, stacked(ws[...]))
    receivers[...] = 0.5 * (dot3(rows, stacked(wr[...])) + biases[0:1])


def coarse_kernel(count, *refs):
    pieces, (all_picks, receivers, wo) = refs[:count], refs[count : count + 3]
    part = refs[-1]
    senders = jnp.concatenate([piece[...] for piece in pieces], axis=0)
    picked = dot(all_picks[...], jnp.concatenate(split(senders), axis=0))
    hidden = silu_sum(picked, receivers[...], all_picks.shape[0] // receivers.shape[0])
    part[...] = dot3(hidden, stacked(wo[...]))


def fetched_shares(packs, axis):
    subs, lvls = lax.axis_size("sub"), lax.axis_size("lvl")
    sub, lvl = lax.axis_index("sub"), lax.axis_index("lvl")
    place, count = partners(axis)
    left = iter(packs)
    for s in range(1, subs):
        for p in range(count):
            for t in range(lvls):
                mine = lax.rem(place + count - p, count) * lvls + lax.rem(lvl + lvls - t, lvls)
                yield next(left), lax.rem(sub + subs - s, subs), mine, p == 0 and t == 0


def put_stacked(values, out, first, columns):
    high, low = split(values)
    depth, rows = out.shape[0] // 3, values.shape[0]
    for i, half in enumerate((high, low, high)):
        out[pl.ds(pl.multiple_of(i * depth + first, 16), rows), columns] = half


def collect_in(own, packs, axis, at, out):
    everything = slice(0, own.shape[1])
    put_stacked(own[...], out.at[lax.axis_index("sub")], 0, everything)
    share = own.shape[0] // shares(axis)[1]
    for pack, block, mine, _ in fetched_shares(packs, axis):
        put_stacked(pack[at : at + share, :], out.at[block], mine * share, everything)


def collect_out(own, packs, axis, at, out):
    width, latent = own.shape
    put_stacked(own[...], out, lax.axis_index("sub") * width, slice(0, latent))
    thin = width // shares(axis)[1]
    for pack, block, mine, _ in fetched_shares(packs, axis):
        for j in range(latent // width):
            part = pack[at + j * thin : at + (j + 1) * thin, :]
            put_stacked(part, out, block * width + mine * thin, slice(j * width, (j + 1) * width))


def collect_bias(own, packs, axis, at, out):
    out[lax.axis_index("sub")] = jnp.broadcast_to(own, (8, own.shape[1]))
    for pack, block, _, whole_row in fetched_shares(packs, axis):
        if whole_row:
            out[block] = jnp.broadcast_to(pack[at : at + 1, :], (8, own.shape[1]))


def down_weights_kernel(count, nodes, ws, wr, biases, wo, *refs):
    packs, (receivers, ws_all, wo_all, wr_all, bias_all) = refs[:count], refs[count:]
    width = ws.shape[1]
    share = ws.shape[0] // shares("parts")[1]
    collect_in(ws, packs, "parts", 0, ws_all)
    collect_in(wr, packs, "parts", share, wr_all)
    collect_out(wo, packs, "parts", 2 * share, wo_all)
    collect_bias(biases[1:2], packs, "parts", 3 * share, bias_all)
    states = threefold(nodes[...])
    for g in range(wr_all.shape[0]):
        receivers[:, g * width : (g + 1) * width] = 0.5 * (dot(states, wr_all[g]) + bias_all[g][0:1])


def bottom_weights_kernel(count, ws, wr, biases, wo, *refs):
    packs, (ws_all, wr_all, wo_all, bias_all) = refs[:count], refs[count:]
    share = ws.shape[0] // shares("patch")[1]
    collect_in(ws, packs, "patch", 0, ws_all)
    collect_in(wr, packs, "patch", share, wr_all)
    collect_out(wo, packs, "patch", 2 * share, wo_all)
    collect_bias(biases[2:3], packs, "patch", 3 * share, bias_all)


def down_rows(nodes, receivers, sources, senders, wo, gain):
    blocks = senders.shape[0] // 2
    column = lax.broadcasted_iota(jnp.int32, (nodes.shape[0], 2 * blocks), 1)
    names = jnp.where(column < blocks, column, column - blocks)
    picked = dot(one_hot(sources, names), senders)
    hidden = silu_sum(picked, receivers, sources.shape[1])
    return nodes + gain * normed(dot3(hidden, wo))


def down_edge_kernel(count, rim, *refs):
    parts, refs = refs[:count], refs[count:]
    coarse_up, gains, nodes, receivers, sources, ws, wo = refs[:7]
    new_coarse, senders, head, tail, held_here, sem = refs[7:]
    rows = coarse_up[...] + gains[1:2] * normed(added(parts))
    held_here[...] = rows
    move = pltpu.make_async_copy(held_here, new_coarse, sem)
    move.start()
    blocks = rows.shape[0]
    width = ws.shape[2]
    left = threefold(rows)
    for g in range(ws.shape[0]):
        columns = slice(g * width, (g + 1) * width)
        high, low = split(0.5 * dot(left, ws[g]))
        senders[0:blocks, columns] = high
        senders[blocks : 2 * blocks, columns] = low
    total = nodes.shape[0]
    wanted = upright(sources[...])
    for out, place in ((head, slice(0, rim)), (tail, slice(total - rim, total))):
        out[...] = down_rows(
            nodes[place], receivers[place], wanted[place], senders[...], wo[...], gains[2:3]
        )
    move.wait()


def down_middle_kernel(rim, nodes, receivers, sources, senders, wo, gains, middle):
    place = slice(rim, nodes.shape[0] - rim)
    middle[...] = down_rows(
        nodes[place], receivers[place], upright(sources[...])[place], senders[...], wo[...], gains[2:3]
    )


def bottom_rows(nodes, receivers, picks, senders, wo, gain, ahead=None):
    half = senders.shape[1] // 2
    hidden = []
    for place in (slice(0, half), slice(half, 2 * half)):
        picked = dot(picks, senders[:, place])
        if ahead is not None:
            picked = picked + ahead[:, place]
        hidden.append(silu_sum(picked, receivers[:, place], picks.shape[0] // nodes.shape[0]))
    return nodes + gain * normed(dot3(jnp.concatenate(hidden, axis=1), wo))


def put_strips(values, rim, out, columns):
    high, low = split(values)
    for i in range(values.shape[0] // rim):
        strip = slice(i * rim, (i + 1) * rim)
        out[2 * i * rim : (2 * i + 1) * rim, columns] = high[strip]
        out[(2 * i + 1) * rim : (2 * i + 2) * rim, columns] = low[strip]


def bottom_middle_kernel(rim, head, middle, tail, picks, ws, wr, wo, bias, gains, receivers, out, ahead, senders):
    nodes = jnp.concatenate([head[...], middle[...], tail[...]], axis=0)
    left = threefold(nodes)
    width = ws.shape[2]
    for g in range(ws.shape[0]):
        columns = slice(g * width, (g + 1) * width)
        put_strips(0.5 * dot(left, ws[g]), rim, senders, columns)
        receivers[:, columns] = 0.5 * (dot(left, wr[g]) + bias[g][0:1])
    total = nodes.shape[0]
    size = picks.shape[0] * rim // total
    for i in range(1, total // rim - 1):
        place = slice(i * rim, (i + 1) * rim)
        inner = slice((i - 1) * rim, i * rim)
        out[inner, :] = bottom_rows(
            middle[inner], receivers[place], picks[i * size : (i + 1) * size],
            senders[2 * (i - 1) * rim : 2 * (i + 2) * rim, :], wo[...], gains[3:4],
        )
    near, last = senders.shape[0], picks.shape[0] - size
    ahead[0:size, :] = dot(picks[0:size, 2 * rim : 6 * rim], senders[0 : 4 * rim, :])
    ahead[size : 2 * size, :] = dot(
        picks[last : last + size, 0 : 4 * rim], senders[near - 4 * rim : near, :]
    )


def bottom_edge_kernel(rim, before, after, head, tail, inner, ahead, picks, receivers, ws, wo, gains, out, outer, strips, sems):
    total = receivers.shape[0]
    size = picks.shape[0] * rim // total
    moves = [pltpu.make_async_copy(inner, out.at[pl.ds(rim, total - 2 * rim)], sems.at[0])]
    moves[0].start()
    left = threefold(jnp.concatenate([before[...], after[...]], axis=0))
    width = ws.shape[2]
    for g in range(ws.shape[0]):
        put_strips(0.5 * dot(left, ws[g]), rim, outer, slice(g * width, (g + 1) * width))
    for side, nodes in enumerate((head, tail)):
        first, column = (0, 0) if side == 0 else (total - rim, 4 * rim)
        place = slice(first, first + rim)
        chosen = picks[first // rim * size : (first // rim + 1) * size, column : column + 2 * rim]
        strips[side * rim : (side + 1) * rim, :] = bottom_rows(
            nodes[...], receivers[place], chosen, outer[2 * side * rim : 2 * (side + 1) * rim, :],
            wo[...], gains[3:4], ahead[side * size : (side + 1) * size, :],
        )
        strip = strips.at[pl.ds(side * rim, rim)]
        moves.append(pltpu.make_async_copy(strip, out.at[pl.ds(first, rim)], sems.at[1 + side]))
        moves[-1].start()
    for move in moves:
        move.wait()


whole = pl.BlockSpec(memory_space=pltpu.VMEM)
away = pl.BlockSpec(memory_space=pl.ANY)


def call(kernel, outs, operands, flops, scratch=(), far=(), far_outs=(), unread=0, limit=limit_bytes):
    moved = sum(x.size * x.dtype.itemsize for x in (*outs, *operands))
    read = len(operands) - unread
    specs = [away if i in far else whole for i in range(read)] + [away] * unread
    return pl.pallas_call(
        (lambda *refs: kernel(*refs[:read], *refs[read + unread :])) if unread else kernel,
        out_shape=tuple(outs),
        in_specs=specs,
        out_specs=tuple(away if i in far_outs else whole for i in range(len(outs))),
        scratch_shapes=list(scratch),
        compiler_params=pltpu.CompilerParams(vmem_limit_bytes=limit),
        cost_estimate=pl.CostEstimate(flops=int(flops), bytes_accessed=moved, transcendentals=0),
    )(*operands)


def like(shape, kind=f32):
    return jax.ShapeDtypeStruct(tuple(shape), kind)


def shifted(values, axis, step):
    count = lax.axis_size(axis)
    return lax.ppermute(values, axis, [(i, (i + step) % count) for i in range(count)])


def sub_parts(part):
    if lax.axis_size("sub") == 2:
        return [part, shifted(part, "sub", 1)]
    return [lax.psum(part, "sub")]


def coarse_pieces(senders, others):
    patches, lvls = lax.axis_size("patch"), lax.axis_size("lvl")
    if patches > most_direct:
        return [lax.all_gather(senders, ("patch", "lvl"), axis=0, tiled=True)], others
    pieces = [shifted(senders, "patch", s) for s in range(1, patches)]
    pieces, others = lax.optimization_barrier((pieces, others))
    rows, width = senders.shape
    (near,) = call(
        join_kernel, [like((patches * rows, width))], [senders, *pieces], patches * rows * width
    )
    return [near] + [shifted(near, "lvl", t) for t in range(1, lvls)], others


def held(values, event):
    return lax.optimization_barrier((values, event))[0]


def over_sub(pack):
    return [shifted(pack, "sub", s) for s in range(1, lax.axis_size("sub"))]


def partners(axis):
    if axis == "parts":
        return lax.axis_index(axis), lax.axis_size(axis)
    count = 2 if lax.axis_size(axis) % 2 == 0 else 1
    return lax.rem(lax.axis_index(axis), count), count


def over_partners(share_list, axis):
    size, count = lax.axis_size(axis), partners(axis)[1]
    return [
        [
            lax.ppermute(share, axis, [(i, i - i % count + (i + p) % count) for i in range(size)])
            for p in range(1, count)
        ]
        for share in share_list
    ]


def over_lvl(shares):
    return [
        [share] + [shifted(share, "lvl", t) for t in range(1, lax.axis_size("lvl"))]
        for share in shares
    ]


def all_shares(shares, others):
    near = over_lvl(shares)
    far = [over_lvl(row) for row in others]
    return [x for first, row in zip(near, far) for x in (first + [y for group in row for y in group])]


def body(
    node_states,
    coarse_states,
    children,
    down_sources,
    bottom_links,
    coarse_links,
    upward_sender,
    upward_receiver,
    upward_bias,
    upward_output,
    upward_gain,
    coarse_sender,
    coarse_receiver,
    coarse_bias,
    coarse_output,
    coarse_gain,
    downward_sender,
    downward_receiver,
    downward_bias,
    downward_output,
    downward_gain,
    bottom_sender,
    bottom_receiver,
    bottom_bias,
    bottom_output,
    bottom_gain,
):
    rows, latent = node_states.shape
    blocks = coarse_states.shape[0]
    width = upward_sender.shape[1]
    subs = lax.axis_size("sub")
    hidden = width * subs
    rim = rows // 4
    into = like((subs, 3 * latent, width), bf16)
    out_of = like((3 * hidden, latent), bf16)
    bias_rows = like((subs, 8, width))

    columns = latent // width
    lvls = lax.axis_size("lvl")

    def pack(axis):
        count = shares(axis)[1]
        return like((2 * latent // count + width // count * columns + 8, width))

    (part,) = call(
        upward_kernel,
        [like((blocks, latent))],
        [
            node_states, coarse_states, children.T, upward_sender, upward_receiver,
            upward_bias[None], upward_output,
        ],
        6 * rows * latent * width,
        limit=up_limit,
    )
    parts = sub_parts(part)
    down_own = (downward_sender, downward_receiver, downward_output, downward_bias[None])
    bottom_own = (bottom_sender, bottom_receiver, bottom_output, bottom_bias[None])
    (down_pack,), (bottom_pack,) = (
        call(
            functools.partial(share_kernel, axis),
            [pack(axis)],
            own,
            latent,
            [pltpu.SemaphoreType.DMA((3 + columns,))],
            far=range(4),
            limit=share_limit,
        )
        for axis, own in (("parts", down_own), ("patch", bottom_own))
    )
    gains, biases = call(
        stack_kernel,
        [like((4, latent)), like((3, width))],
        [
            upward_gain[None], coarse_gain[None], downward_gain[None], bottom_gain[None],
            coarse_bias[None], downward_bias[None], bottom_bias[None], part,
        ],
        latent * hidden,
        unread=1,
    )
    down_near = over_sub(down_pack)
    down_near = held(down_near, parts[-1])
    bottom_near = over_sub(bottom_pack)
    down_far = over_partners(down_near, "parts")
    coarse_up, senders, receivers = call(
        functools.partial(coarse_project_kernel, len(parts)),
        [like((blocks, latent)), like((blocks, width)), like((blocks, width))],
        [*parts, coarse_states, gains, biases, coarse_sender, coarse_receiver],
        12 * blocks * latent * width,
    )
    patches = lax.axis_size("patch")
    names = blocks * patches * lvls
    picks, bottom_picks = call(
        functools.partial(picks_kernel, rim, patches, blocks),
        [like((coarse_links.size, 2 * names), bf16), like((bottom_links.size, 6 * rim), bf16)],
        [coarse_links.T, bottom_links.T, senders],
        coarse_links.size * names,
        unread=1,
    )
    pieces, (picks, bottom_picks, down_near, down_far, bottom_near) = coarse_pieces(
        senders, (picks, bottom_picks, down_near, down_far, bottom_near)
    )
    down_packs = all_shares(down_near, down_far)
    bottom_far = over_partners(bottom_near, "patch")
    (part,) = call(
        functools.partial(coarse_kernel, len(pieces)),
        [like((blocks, latent))],
        [*pieces, picks, receivers, coarse_output],
        4 * coarse_links.size * names * width,
    )
    parts = sub_parts(part)
    receivers, ws, wo = call(
        functools.partial(down_weights_kernel, len(down_packs)),
        [like((rows, hidden)), into, out_of],
        [node_states, downward_sender, downward_receiver, biases, downward_output, *down_packs, part],
        6 * rows * latent * hidden,
        [pltpu.VMEM((subs, 3 * latent, width), bf16), pltpu.VMEM((subs, 8, width), f32)],
        unread=1,
    )
    new_coarse, senders, head, tail = call(
        functools.partial(down_edge_kernel, len(parts), rim),
        [like((blocks, latent)), like((2 * blocks, hidden), bf16), like((rim, latent)), like((rim, latent))],
        [*parts, coarse_up, gains, node_states, receivers, down_sources.T, ws, wo],
        6 * 2 * rim * latent * hidden,
        [pltpu.VMEM((blocks, latent), f32), pltpu.SemaphoreType.DMA],
        far_outs=(0,),
    )
    ring = ("patch", "lvl")
    before, after = shifted(tail, ring, 1), shifted(head, ring, -1)
    (middle,) = call(
        functools.partial(down_middle_kernel, rim),
        [like((rows - 2 * rim, latent))],
        [node_states, receivers, down_sources.T, senders, wo, gains],
        6 * (rows - 2 * rim) * latent * hidden,
    )

    bottom_near, bottom_far = held((bottom_near, bottom_far), head)
    bottom_packs = all_shares(bottom_near, bottom_far)
    ws, wr, wo, bias = call(
        functools.partial(bottom_weights_kernel, len(bottom_packs)),
        [into, into, out_of, bias_rows],
        [bottom_sender, bottom_receiver, biases, bottom_output, *bottom_packs],
        latent * hidden,
    )
    receivers, inner, ahead = call(
        functools.partial(bottom_middle_kernel, rim),
        [like((rows, hidden)), like((rows - 2 * rim, latent)), like((bottom_links.size // (rows // rim) * 2, hidden))],
        [head, middle, tail, bottom_picks, ws, wr, wo, bias, gains],
        (12 * rows + 12 * rows) * latent * hidden,
        [pltpu.VMEM((2 * rows, hidden), bf16)],
    )
    (new_nodes,) = call(
        functools.partial(bottom_edge_kernel, rim),
        [like((rows, latent))],
        [before, after, head, tail, inner, ahead, bottom_picks, receivers, ws, wo, gains],
        24 * rim * latent * hidden,
        [
            pltpu.VMEM((4 * rim, hidden), bf16),
            pltpu.VMEM((2 * rim, latent), f32),
            pltpu.SemaphoreType.DMA((3,)),
        ],
        far_outs=(0,),
    )
    return (new_nodes, new_coarse)


def solution(mesh):
    split_rows, level_rows = P(("parts", "patch", "lvl"), None), P(("patch", "lvl"), None)
    weights = (P(None, "sub"), P(None, "sub"), P("sub"), P("sub", None), P())
    in_specs = (split_rows, split_rows, *([level_rows] * 4), *(weights * 4))
    out_specs = (split_rows, split_rows)
    return jax.shard_map(body, mesh=mesh, in_specs=in_specs, out_specs=out_specs, check_vma=False)
```

```python
import functools

import jax
import jax.numpy as jnp
from jax import lax
from jax.experimental import pallas as pl
from jax.experimental.pallas import tpu as pltpu
from jax.sharding import PartitionSpec as P

epsilon = 1e-05
f32 = jnp.float32
bf16 = jnp.bfloat16
limit_bytes = 12 * 1024 * 1024
share_limit = 58 * 1000 * 1000
up_limit = 50 * 1000 * 1000
most_direct = 4


def split(values):
    high = values.astype(bf16)
    return high, (values - high.astype(f32)).astype(bf16)


def dot(a, b):
    return jnp.dot(a, b, preferred_element_type=f32)


def threefold(values):
    high, low = split(values)
    return jnp.concatenate([high, high, low], axis=1)


def stacked(weights):
    high, low = split(weights)
    return jnp.concatenate([high, low, high], axis=0)


def dot3(a, b_stacked):
    return dot(threefold(a), b_stacked)


def normed(values):
    center = values - jnp.mean(values, axis=-1, keepdims=True)
    spread = jnp.mean(center * center, axis=-1, keepdims=True)
    return center * lax.rsqrt(spread + epsilon)


def upright(rows):
    count, size = rows.shape
    tall, wide = -count % 8, -size % 128
    if tall:
        rows = jnp.concatenate([rows, jnp.zeros((tall, size), rows.dtype)], axis=0)
    if wide:
        rows = jnp.concatenate([rows, jnp.zeros((count + tall, wide), rows.dtype)], axis=1)
    return jnp.transpose(rows)[:size, :count]


def one_hot(wanted, names):
    return jnp.concatenate(
        [
            jnp.where(wanted[:, k : k + 1] == names, 1.0, 0.0).astype(bf16)
            for k in range(wanted.shape[1])
        ],
        axis=0,
    )


def silu_sum(picked, halves, count):
    rows = halves.shape[0]
    total = None
    for k in range(count):
        u = picked[k * rows : (k + 1) * rows] + halves
        term = u + u * jnp.tanh(u)
        total = term if total is None else total + term
    return total


def added(refs):
    total = refs[0][...]
    for ref in refs[1:]:
        total = total + ref[...]
    return total


def started(copies, sems):
    moves = [pltpu.make_async_copy(a, b, sems.at[i]) for i, (a, b) in enumerate(copies)]
    for move in moves:
        move.start()
    return moves


def upward_kernel(nodes, coarse, children, ws, wr, bias, wo, part):
    wanted = upright(children[...])
    names = lax.broadcasted_iota(jnp.int32, (wanted.shape[0], nodes.shape[0]), 1)
    picks = one_hot(wanted, names)
    senders = jnp.concatenate(split(0.5 * dot3(nodes[...], stacked(ws[...]))), axis=0)
    receivers = 0.5 * (dot3(coarse[...], stacked(wr[...])) + bias[...])
    picked = dot(jnp.concatenate([picks, picks], axis=1), senders)
    hidden = silu_sum(picked, receivers, wanted.shape[1])
    part[...] = dot3(hidden, stacked(wo[...]))


def stack_kernel(*refs):
    params, (gains, biases) = refs[:7], refs[7:]
    for i in range(4):
        gains[i : i + 1] = params[i][...]
    for i in range(3):
        biases[i : i + 1] = params[4 + i][...]


def share_kernel(axis, *refs):
    for move in started(share_copies(refs[:4], refs[4], axis), refs[5]):
        move.wait()


def shares(axis):
    lvls = lax.axis_size("lvl")
    place, count = partners(axis)
    return place * lvls + lax.axis_index("lvl"), count * lvls


def share_copies(sources, pack, axis):
    mine, count = shares(axis)
    width = pack.shape[1]
    copies, at = [], 0
    for source in sources:
        rows = source.shape[0] // count
        if source.shape[0] == 1:
            copies.append((source, pack.at[pl.ds(at, 1)]))
            at += 8
            continue
        strip = pl.ds(pl.multiple_of(mine * rows, rows), rows)
        for j in range(source.shape[1] // width):
            copies.append((source.at[strip, pl.ds(j * width, width)], pack.at[pl.ds(at, rows)]))
            at += rows
    return copies


def picks_kernel(rim, patches, blocks, coarse_links, bottom_links, coarse_picks, bottom_picks):
    wanted = upright(coarse_links[...])
    rows = wanted.shape[0]
    lvls = lax.axis_size("lvl")
    half = coarse_picks.shape[1] // 2
    column = lax.broadcasted_iota(jnp.int32, (rows, blocks), 1)
    for t in range(lvls):
        for s in range(patches):
            patch = lax.rem(lax.axis_index("patch") + patches - s, patches)
            lvl = lax.rem(lax.axis_index("lvl") + lvls - t, lvls)
            first = (patch * lvls + lvl) * blocks
            at = (t * patches + s) * blocks
            piece = one_hot(wanted, column + first)
            coarse_picks[:, at : at + blocks] = piece
            coarse_picks[:, half + at : half + at + blocks] = piece
    wanted = upright(bottom_links[...])
    size = rim * wanted.shape[1]
    names = lax.broadcasted_iota(jnp.int32, (rim, 3 * rim), 1)
    for i in range(wanted.shape[0] // rim):
        picks = one_hot(wanted[i * rim : (i + 1) * rim], names + i * rim)
        for j in range(6):
            piece = picks[:, j // 2 * rim : (j // 2 + 1) * rim]
            bottom_picks[i * size : (i + 1) * size, j * rim : (j + 1) * rim] = piece


def join_kernel(*refs):
    rows = refs[0].shape[0]
    for i, piece in enumerate(refs[:-1]):
        refs[-1][i * rows : (i + 1) * rows] = piece[...]


def coarse_project_kernel(count, *refs):
    parts, refs = refs[:count], refs[count:]
    coarse, gains, biases, ws, wr, updated, senders, receivers = refs
    rows = coarse[...] + gains[0:1] * normed(added(parts))
    updated[...] = rows
    senders[...] = 0.5 * dot3(rows, stacked(ws[...]))
    receivers[...] = 0.5 * (dot3(rows, stacked(wr[...])) + biases[0:1])


def coarse_kernel(count, *refs):
    pieces, (all_picks, receivers, wo) = refs[:count], refs[count : count + 3]
    part = refs[-1]
    senders = jnp.concatenate([piece[...] for piece in pieces], axis=0)
    picked = dot(all_picks[...], jnp.concatenate(split(senders), axis=0))
    hidden = silu_sum(picked, receivers[...], all_picks.shape[0] // receivers.shape[0])
    part[...] = dot3(hidden, stacked(wo[...]))


def fetched_shares(packs, axis):
    subs, lvls = lax.axis_size("sub"), lax.axis_size("lvl")
    sub, lvl = lax.axis_index("sub"), lax.axis_index("lvl")
    place, count = partners(axis)
    left = iter(packs)
    for s in range(1, subs):
        for p in range(count):
            for t in range(lvls):
                mine = lax.rem(place + count - p, count) * lvls + lax.rem(lvl + lvls - t, lvls)
                yield next(left), lax.rem(sub + subs - s, subs), mine, p == 0 and t == 0


def put_stacked(values, out, first, columns):
    high, low = split(values)
    depth, rows = out.shape[0] // 3, values.shape[0]
    for i, half in enumerate((high, low, high)):
        out[pl.ds(pl.multiple_of(i * depth + first, 16), rows), columns] = half


def collect_in(own, packs, axis, at, out):
    everything = slice(0, own.shape[1])
    put_stacked(own[...], out.at[lax.axis_index("sub")], 0, everything)
    share = own.shape[0] // shares(axis)[1]
    for pack, block, mine, _ in fetched_shares(packs, axis):
        put_stacked(pack[at : at + share, :], out.at[block], mine * share, everything)


def collect_out(own, packs, axis, at, out):
    width, latent = own.shape
    put_stacked(own[...], out, lax.axis_index("sub") * width, slice(0, latent))
    thin = width // shares(axis)[1]
    for pack, block, mine, _ in fetched_shares(packs, axis):
        for j in range(latent // width):
            part = pack[at + j * thin : at + (j + 1) * thin, :]
            put_stacked(part, out, block * width + mine * thin, slice(j * width, (j + 1) * width))


def collect_bias(own, packs, axis, at, out):
    out[lax.axis_index("sub")] = jnp.broadcast_to(own, (8, own.shape[1]))
    for pack, block, _, whole_row in fetched_shares(packs, axis):
        if whole_row:
            out[block] = jnp.broadcast_to(pack[at : at + 1, :], (8, own.shape[1]))


def down_weights_kernel(count, nodes, ws, wr, biases, wo, *refs):
    packs, (receivers, ws_all, wo_all, wr_all, bias_all) = refs[:count], refs[count:]
    width = ws.shape[1]
    share = ws.shape[0] // shares("parts")[1]
    collect_in(ws, packs, "parts", 0, ws_all)
    collect_in(wr, packs, "parts", share, wr_all)
    collect_out(wo, packs, "parts", 2 * share, wo_all)
    collect_bias(biases[1:2], packs, "parts", 3 * share, bias_all)
    states = threefold(nodes[...])
    for g in range(wr_all.shape[0]):
        receivers[:, g * width : (g + 1) * width] = 0.5 * (dot(states, wr_all[g]) + bias_all[g][0:1])


def bottom_weights_kernel(count, ws, wr, biases, wo, *refs):
    packs, (ws_all, wr_all, wo_all, bias_all) = refs[:count], refs[count:]
    share = ws.shape[0] // shares("patch")[1]
    collect_in(ws, packs, "patch", 0, ws_all)
    collect_in(wr, packs, "patch", share, wr_all)
    collect_out(wo, packs, "patch", 2 * share, wo_all)
    collect_bias(biases[2:3], packs, "patch", 3 * share, bias_all)


def down_rows(nodes, receivers, sources, senders, wo, gain):
    blocks = senders.shape[0] // 2
    column = lax.broadcasted_iota(jnp.int32, (nodes.shape[0], 2 * blocks), 1)
    names = jnp.where(column < blocks, column, column - blocks)
    picked = dot(one_hot(sources, names), senders)
    hidden = silu_sum(picked, receivers, sources.shape[1])
    return nodes + gain * normed(dot3(hidden, wo))


def down_edge_kernel(count, rim, *refs):
    parts, refs = refs[:count], refs[count:]
    coarse_up, gains, nodes, receivers, sources, ws, wo = refs[:7]
    new_coarse, senders, head, tail, held_here, sem = refs[7:]
    rows = coarse_up[...] + gains[1:2] * normed(added(parts))
    held_here[...] = rows
    move = pltpu.make_async_copy(held_here, new_coarse, sem)
    move.start()
    blocks = rows.shape[0]
    width = ws.shape[2]
    left = threefold(rows)
    for g in range(ws.shape[0]):
        columns = slice(g * width, (g + 1) * width)
        high, low = split(0.5 * dot(left, ws[g]))
        senders[0:blocks, columns] = high
        senders[blocks : 2 * blocks, columns] = low
    total = nodes.shape[0]
    wanted = upright(sources[...])
    for out, place in ((head, slice(0, rim)), (tail, slice(total - rim, total))):
        out[...] = down_rows(
            nodes[place], receivers[place], wanted[place], senders[...], wo[...], gains[2:3]
        )
    move.wait()


def down_middle_kernel(rim, nodes, receivers, sources, senders, wo, gains, middle):
    place = slice(rim, nodes.shape[0] - rim)
    middle[...] = down_rows(
        nodes[place], receivers[place], upright(sources[...])[place], senders[...], wo[...], gains[2:3]
    )


def bottom_rows(nodes, receivers, picks, senders, wo, gain, ahead=None):
    half = senders.shape[1] // 2
    hidden = []
    for place in (slice(0, half), slice(half, 2 * half)):
        picked = dot(picks, senders[:, place])
        if ahead is not None:
            picked = picked + ahead[:, place]
        hidden.append(silu_sum(picked, receivers[:, place], picks.shape[0] // nodes.shape[0]))
    return nodes + gain * normed(dot3(jnp.concatenate(hidden, axis=1), wo))


def put_strips(values, rim, out, columns):
    high, low = split(values)
    for i in range(values.shape[0] // rim):
        strip = slice(i * rim, (i + 1) * rim)
        out[2 * i * rim : (2 * i + 1) * rim, columns] = high[strip]
        out[(2 * i + 1) * rim : (2 * i + 2) * rim, columns] = low[strip]


def bottom_middle_kernel(rim, head, middle, tail, picks, ws, wr, wo, bias, gains, receivers, out, ahead, senders):
    nodes = jnp.concatenate([head[...], middle[...], tail[...]], axis=0)
    left = threefold(nodes)
    width = ws.shape[2]
    for g in range(ws.shape[0]):
        columns = slice(g * width, (g + 1) * width)
        put_strips(0.5 * dot(left, ws[g]), rim, senders, columns)
        receivers[:, columns] = 0.5 * (dot(left, wr[g]) + bias[g][0:1])
    total = nodes.shape[0]
    size = picks.shape[0] * rim // total
    for i in range(1, total // rim - 1):
        place = slice(i * rim, (i + 1) * rim)
        inner = slice((i - 1) * rim, i * rim)
        out[inner, :] = bottom_rows(
            middle[inner], receivers[place], picks[i * size : (i + 1) * size],
            senders[2 * (i - 1) * rim : 2 * (i + 2) * rim, :], wo[...], gains[3:4],
        )
    near, last = senders.shape[0], picks.shape[0] - size
    ahead[0:size, :] = dot(picks[0:size, 2 * rim : 6 * rim], senders[0 : 4 * rim, :])
    ahead[size : 2 * size, :] = dot(
        picks[last : last + size, 0 : 4 * rim], senders[near - 4 * rim : near, :]
    )


def bottom_edge_kernel(rim, before, after, head, tail, inner, ahead, picks, receivers, ws, wo, gains, out, outer, strips, sems):
    total = receivers.shape[0]
    size = picks.shape[0] * rim // total
    moves = [pltpu.make_async_copy(inner, out.at[pl.ds(rim, total - 2 * rim)], sems.at[0])]
    moves[0].start()
    left = threefold(jnp.concatenate([before[...], after[...]], axis=0))
    width = ws.shape[2]
    for g in range(ws.shape[0]):
        put_strips(0.5 * dot(left, ws[g]), rim, outer, slice(g * width, (g + 1) * width))
    for side, nodes in enumerate((head, tail)):
        first, column = (0, 0) if side == 0 else (total - rim, 4 * rim)
        place = slice(first, first + rim)
        chosen = picks[first // rim * size : (first // rim + 1) * size, column : column + 2 * rim]
        strips[side * rim : (side + 1) * rim, :] = bottom_rows(
            nodes[...], receivers[place], chosen, outer[2 * side * rim : 2 * (side + 1) * rim, :],
            wo[...], gains[3:4], ahead[side * size : (side + 1) * size, :],
        )
        strip = strips.at[pl.ds(side * rim, rim)]
        moves.append(pltpu.make_async_copy(strip, out.at[pl.ds(first, rim)], sems.at[1 + side]))
        moves[-1].start()
    for move in moves:
        move.wait()


whole = pl.BlockSpec(memory_space=pltpu.VMEM)
away = pl.BlockSpec(memory_space=pl.ANY)


def call(kernel, outs, operands, flops, scratch=(), far=(), far_outs=(), unread=0, limit=limit_bytes):
    moved = sum(x.size * x.dtype.itemsize for x in (*outs, *operands))
    read = len(operands) - unread
    specs = [away if i in far else whole for i in range(read)] + [away] * unread
    return pl.pallas_call(
        (lambda *refs: kernel(*refs[:read], *refs[read + unread :])) if unread else kernel,
        out_shape=tuple(outs),
        in_specs=specs,
        out_specs=tuple(away if i in far_outs else whole for i in range(len(outs))),
        scratch_shapes=list(scratch),
        compiler_params=pltpu.CompilerParams(vmem_limit_bytes=limit),
        cost_estimate=pl.CostEstimate(flops=int(flops), bytes_accessed=moved, transcendentals=0),
    )(*operands)


def like(shape, kind=f32):
    return jax.ShapeDtypeStruct(tuple(shape), kind)


def shifted(values, axis, step):
    count = lax.axis_size(axis)
    return lax.ppermute(values, axis, [(i, (i + step) % count) for i in range(count)])


def sub_parts(part):
    if lax.axis_size("sub") == 2:
        return [part, shifted(part, "sub", 1)]
    return [lax.psum(part, "sub")]


def coarse_pieces(senders, others):
    patches, lvls = lax.axis_size("patch"), lax.axis_size("lvl")
    if patches > most_direct:
        return [lax.all_gather(senders, ("patch", "lvl"), axis=0, tiled=True)], others
    pieces = [shifted(senders, "patch", s) for s in range(1, patches)]
    pieces, others = lax.optimization_barrier((pieces, others))
    rows, width = senders.shape
    (near,) = call(
        join_kernel, [like((patches * rows, width))], [senders, *pieces], patches * rows * width
    )
    return [near] + [shifted(near, "lvl", t) for t in range(1, lvls)], others


def held(values, event):
    return lax.optimization_barrier((values, event))[0]


def over_sub(pack):
    return [shifted(pack, "sub", s) for s in range(1, lax.axis_size("sub"))]


def partners(axis):
    if axis == "parts":
        return lax.axis_index(axis), lax.axis_size(axis)
    count = 2 if lax.axis_size(axis) % 2 == 0 else 1
    return lax.rem(lax.axis_index(axis), count), count


def over_partners(share_list, axis):
    size, count = lax.axis_size(axis), partners(axis)[1]
    return [
        [
            lax.ppermute(share, axis, [(i, i - i % count + (i + p) % count) for i in range(size)])
            for p in range(1, count)
        ]
        for share in share_list
    ]


def over_lvl(shares):
    return [
        [share] + [shifted(share, "lvl", t) for t in range(1, lax.axis_size("lvl"))]
        for share in shares
    ]


def all_shares(shares, others):
    near = over_lvl(shares)
    far = [over_lvl(row) for row in others]
    return [x for first, row in zip(near, far) for x in (first + [y for group in row for y in group])]


def body(
    node_states,
    coarse_states,
    children,
    down_sources,
    bottom_links,
    coarse_links,
    upward_sender,
    upward_receiver,
    upward_bias,
    upward_output,
    upward_gain,
    coarse_sender,
    coarse_receiver,
    coarse_bias,
    coarse_output,
    coarse_gain,
    downward_sender,
    downward_receiver,
    downward_bias,
    downward_output,
    downward_gain,
    bottom_sender,
    bottom_receiver,
    bottom_bias,
    bottom_output,
    bottom_gain,
):
    rows, latent = node_states.shape
    blocks = coarse_states.shape[0]
    width = upward_sender.shape[1]
    subs = lax.axis_size("sub")
    hidden = width * subs
    rim = rows // 4
    into = like((subs, 3 * latent, width), bf16)
    out_of = like((3 * hidden, latent), bf16)
    bias_rows = like((subs, 8, width))

    columns = latent // width
    lvls = lax.axis_size("lvl")

    def pack(axis):
        count = shares(axis)[1]
        return like((2 * latent // count + width // count * columns + 8, width))

    (part,) = call(
        upward_kernel,
        [like((blocks, latent))],
        [
            node_states, coarse_states, children.T, upward_sender, upward_receiver,
            upward_bias[None], upward_output,
        ],
        6 * rows * latent * width,
        limit=up_limit,
    )
    parts = sub_parts(part)
    down_own = (downward_sender, downward_receiver, downward_output, downward_bias[None])
    bottom_own = (bottom_sender, bottom_receiver, bottom_output, bottom_bias[None])
    (down_pack,), (bottom_pack,) = (
        call(
            functools.partial(share_kernel, axis),
            [pack(axis)],
            own,
            8 * latent**3,
            [pltpu.SemaphoreType.DMA((3 + columns,))],
            far=range(4),
            limit=share_limit,
        )
        for axis, own in (("parts", down_own), ("patch", bottom_own))
    )
    gains, biases = call(
        stack_kernel,
        [like((4, latent)), like((3, width))],
        [
            upward_gain[None], coarse_gain[None], downward_gain[None], bottom_gain[None],
            coarse_bias[None], downward_bias[None], bottom_bias[None], part,
        ],
        latent * hidden,
        unread=1,
    )
    down_near = over_sub(down_pack)
    down_near = held(down_near, parts[-1])
    bottom_near = over_sub(bottom_pack)
    down_far = over_partners(down_near, "parts")
    coarse_up, senders, receivers = call(
        functools.partial(coarse_project_kernel, len(parts)),
        [like((blocks, latent)), like((blocks, width)), like((blocks, width))],
        [*parts, coarse_states, gains, biases, coarse_sender, coarse_receiver],
        12 * blocks * latent * width,
    )
    patches = lax.axis_size("patch")
    names = blocks * patches * lvls
    picks, bottom_picks = call(
        functools.partial(picks_kernel, rim, patches, blocks),
        [like((coarse_links.size, 2 * names), bf16), like((bottom_links.size, 6 * rim), bf16)],
        [coarse_links.T, bottom_links.T, senders],
        coarse_links.size * names,
        unread=1,
    )
    pieces, (picks, bottom_picks, down_near, down_far, bottom_near) = coarse_pieces(
        senders, (picks, bottom_picks, down_near, down_far, bottom_near)
    )
    down_packs = all_shares(down_near, down_far)
    bottom_far = over_partners(bottom_near, "patch")
    (part,) = call(
        functools.partial(coarse_kernel, len(pieces)),
        [like((blocks, latent))],
        [*pieces, picks, receivers, coarse_output],
        4 * coarse_links.size * names * width,
    )
    parts = sub_parts(part)
    receivers, ws, wo = call(
        functools.partial(down_weights_kernel, len(down_packs)),
        [like((rows, hidden)), into, out_of],
        [node_states, downward_sender, downward_receiver, biases, downward_output, *down_packs, part],
        6 * rows * latent * hidden,
        [pltpu.VMEM((subs, 3 * latent, width), bf16), pltpu.VMEM((subs, 8, width), f32)],
        unread=1,
    )
    new_coarse, senders, head, tail = call(
        functools.partial(down_edge_kernel, len(parts), rim),
        [like((blocks, latent)), like((2 * blocks, hidden), bf16), like((rim, latent)), like((rim, latent))],
        [*parts, coarse_up, gains, node_states, receivers, down_sources.T, ws, wo],
        6 * 2 * rim * latent * hidden,
        [pltpu.VMEM((blocks, latent), f32), pltpu.SemaphoreType.DMA],
        far_outs=(0,),
    )
    ring = ("patch", "lvl")
    before, after = shifted(tail, ring, 1), shifted(head, ring, -1)
    (middle,) = call(
        functools.partial(down_middle_kernel, rim),
        [like((rows - 2 * rim, latent))],
        [node_states, receivers, down_sources.T, senders, wo, gains],
        6 * (rows - 2 * rim) * latent * hidden,
    )

    bottom_near, bottom_far = held((bottom_near, bottom_far), head)
    bottom_packs = all_shares(bottom_near, bottom_far)
    ws, wr, wo, bias = call(
        functools.partial(bottom_weights_kernel, len(bottom_packs)),
        [into, into, out_of, bias_rows],
        [bottom_sender, bottom_receiver, biases, bottom_output, *bottom_packs],
        latent * hidden,
    )
    receivers, inner, ahead = call(
        functools.partial(bottom_middle_kernel, rim),
        [like((rows, hidden)), like((rows - 2 * rim, latent)), like((bottom_links.size // (rows // rim) * 2, hidden))],
        [head, middle, tail, bottom_picks, ws, wr, wo, bias, gains],
        (12 * rows + 12 * rows) * latent * hidden,
        [pltpu.VMEM((2 * rows, hidden), bf16)],
    )
    (new_nodes,) = call(
        functools.partial(bottom_edge_kernel, rim),
        [like((rows, latent))],
        [before, after, head, tail, inner, ahead, bottom_picks, receivers, ws, wo, gains],
        24 * rim * latent * hidden,
        [
            pltpu.VMEM((4 * rim, hidden), bf16),
            pltpu.VMEM((2 * rim, latent), f32),
            pltpu.SemaphoreType.DMA((3,)),
        ],
        far_outs=(0,),
    )
    return (new_nodes, new_coarse)


def solution(mesh):
    split_rows, level_rows = P(("parts", "patch", "lvl"), None), P(("patch", "lvl"), None)
    weights = (P(None, "sub"), P(None, "sub"), P("sub"), P("sub", None), P())
    in_specs = (split_rows, split_rows, *([level_rows] * 4), *(weights * 4))
    out_specs = (split_rows, split_rows)
    return jax.shard_map(body, mesh=mesh, in_specs=in_specs, out_specs=out_specs, check_vma=False)
```
